512 devices in a mesh: dp: 32 (over y, x), tm: 16 (over z, core).
Axes of the slice: x: 4, y: 8, z: 8, core: 2. Of those that a mesh axis runs over, the one named last changes fastest.
Arguments:
- pixels: bfloat16 [32, 16, 32, 192], P('dp', 'tm'), may hold values from -1 to 1
- counts: int32 [16, 32, 32], P('tm'), may hold values from 0 to 2, as said below
- clip_lengths: int32 [32, 4], P('dp'), may hold values from 1 to 17, 64 in all within a row
- in_weight: bfloat16 [3, 3, 3, 3, 128], replicated, may hold values from -0.625 to 0.625
- in_bias: float32 [128], replicated, may hold values from -3 to 3
- norm1_gain: float32 [128], replicated, may hold values from 0.5 to 1.5
- norm1_bias: float32 [128], replicated, may hold values from -3 to 3
- conv1_weight: bfloat16 [3, 3, 3, 128, 128], replicated, may hold values from -0.109375 to 0.109375
- norm2_gain: float32 [128], replicated, may hold values from 0.5 to 1.5
- norm2_bias: float32 [128], replicated, may hold values from -3 to 3
- conv2_weight: bfloat16 [3, 3, 3, 128, 128], replicated, may hold values from -0.109375 to 0.109375
- down_weight: bfloat16 [3, 3, 128, 128], replicated, may hold values from -0.1875 to 0.1875
Outputs:
- latents: bfloat16 [32, 16, 32, 2048], P('dp', 'tm')
The draws below stay inside these ranges and needn't reach their ends.
Inputs may be any that keep to these rules, and one draw needn't show every extreme that they name: For each time block, every row and every column of counts sums to 32, and every row holds exactly one entry equal to 2. `clip_lengths`: each row sums to 64, and its longest clip has exactly 17 frames.
All inputs are finite; a program needn't handle non-finite values.
Results may differ from the reference program's by a relative error of at most 0.011.
Values may be sent and summed in bfloat16 or wider, within the bound.
No kernel may reach another device: no remote copies, remote signals or barrier semaphores. Data moves between devices by JAX's collectives and lax.ppermute only.
A program may use at most 128 MiB of HBM per device.

```python
import math
import jax
import jax.numpy as jnp
import numpy as np
from jax import lax

CH = 128
GROUPS = 32
FT = 4
HS = 32
PW = 16
RB = 4
KC = 4
U = 32
MOSTF = 17
N_DP = 32
N_TM = 16


def draw_counts(key, part):
    key = jax.random.fold_in(key, 7)
    keys = jax.random.split(key, N_TM)
    places = jnp.arange(N_DP, dtype=jnp.int32)

    def one_block(sub):
        first, second = jax.random.split(sub)
        order = jax.random.permutation(first, N_DP).astype(jnp.int32)
        turn = jax.random.randint(second, (), 1, N_DP).astype(jnp.int32)
        other = jnp.take(order, (places + turn) % N_DP)
        more = (order[:, None] == places[None, :]).astype(jnp.int32)
        fewer = (other[:, None] == places[None, :]).astype(jnp.int32)
        return U // N_DP + more - fewer
    return jax.vmap(one_block)(keys).astype(jnp.int32)


def shard_levels(stream_key, dims, cuts, smallest, top_value):
    level = 1.0
    for axis_at, blocks in cuts:
        draws = jax.random.uniform(jax.random.fold_in(jax.random.fold_in(stream_key, 6), axis_at), (blocks,), jnp.float32, smallest / len(cuts), top_value / len(cuts))
        level = level * jnp.repeat(jnp.exp(draws), dims[axis_at] // blocks).reshape((-1,) + (1,) * (len(dims) - 1 - axis_at))
    return level


def profile(amount, total, most, slope):
    loads = [(1 << 20) // math.isqrt(grade ** slope) + 1 for grade in range(2, amount + 1)]
    surplus, given = total - most - (amount - 1), [1] * (amount - 1)
    while surplus > 0:
        free = [i for i in range(amount - 1) if given[i] < most]
        mass, remaining = sum([loads[i] for i in free]), surplus
        for i in free:
            more = min(most - given[i], max(1, remaining * loads[i] // mass), surplus)
            given[i] = given[i] + more
            surplus = surplus - more
    return np.array([most] + given)


def uneven_parts(stream_key, amount, total, limit, slope):
    if amount == 2:
        one = jax.random.randint(stream_key, (), max(1, total - limit), min(limit, total - 1) + 1)
        return jnp.stack([one, total - one])
    tallies = jnp.asarray(profile(amount, total, limit, slope), jnp.int32)
    twos = (amount - 1) // 2
    donor, receiver = tallies[1:1 + 2 * twos:2], tallies[2:2 + 2 * twos:2]
    slack = jnp.minimum(donor - 1, limit - receiver)
    shifted = jax.random.randint(jax.random.fold_in(stream_key, 1), (twos,), 0, 1 << 20) % (slack + 1)
    tallies = tallies.at[1:1 + 2 * twos:2].set(donor - shifted).at[2:2 + 2 * twos:2].set(receiver + shifted)
    return tallies[jax.random.permutation(jax.random.fold_in(stream_key, 2), amount)]


def bell_draw(stream_key, shape, deviation, limit, held_as=jnp.bfloat16):
    return jnp.clip(deviation * jax.random.normal(stream_key, shape, jnp.float32), -limit, limit).astype(held_as)


def setup_inputs(seed: int = 0) -> dict:
    splits = jax.random.split(jax.random.key(seed), 13)
    return {
        "pixels": jnp.clip(jax.random.uniform(splits[0], (N_DP, N_TM, U, RB * PW * 3), jnp.float32, -1.0, 1.0) * shard_levels(splits[0], (N_DP, N_TM, U, RB * PW * 3), ((0, 32), (1, 16)), -0.4, 0.0), -1.0, 1.0).astype(jnp.bfloat16),
        "counts": draw_counts(jax.random.fold_in(splits[12], 71), 0),
        "clip_lengths": jax.vmap(lambda own: uneven_parts(own, KC, FT * N_TM, MOSTF, 2))(jax.random.split(splits[2], N_DP)).reshape((N_DP, KC)).astype(jnp.int32),
        "in_weight": bell_draw(splits[3], (3, 3, 3, 3, CH), 81 ** -0.5, 0.625),
        "in_bias": bell_draw(splits[4], (CH,), 0.5, 3.0, jnp.float32),
        "norm1_gain": jnp.clip(1.0 + 0.1 * jax.random.normal(splits[5], (CH,), jnp.float32), 0.5, 1.5),
        "norm1_bias": bell_draw(splits[6], (CH,), 0.5, 3.0, jnp.float32),
        "conv1_weight": bell_draw(splits[7], (3, 3, 3, CH, CH), (27 * CH) ** -0.5, 0.109375),
        "norm2_gain": jnp.clip(1.0 + 0.1 * jax.random.normal(splits[8], (CH,), jnp.float32), 0.5, 1.5),
        "norm2_bias": bell_draw(splits[9], (CH,), 0.5, 3.0, jnp.float32),
        "conv2_weight": bell_draw(splits[10], (3, 3, 3, CH, CH), (27 * CH) ** -0.5, 0.109375),
        "down_weight": bell_draw(splits[11], (3, 3, CH, CH), (9 * CH) ** -0.5, 0.1875),
    }


EPS = 1e-06
HIGH = lax.Precision.HIGHEST

def causal_conv(frames, begin, weight):
    count, height, width, chans = frames.shape
    index = jnp.arange(count, dtype=jnp.int32)
    padded = jnp.pad(frames, ((0, 0), (1, 1), (1, 1), (0, 0)))
    total = jnp.zeros((count * height * width, weight.shape[-1]), jnp.float32)
    for lag in range(3):
        picks = jnp.maximum(index - lag, begin).astype(jnp.int32)
        chosen = jnp.take(padded, picks, axis=0)
        for row in range(3):
            band = chosen[:, row:row + height]
            patch = jnp.concatenate([band[:, :, col:col + width] for col in range(3)], axis=-1)
            total = total + jnp.dot(patch.reshape(-1, 3 * chans), weight[2 - lag, row].reshape(3 * chans, -1), preferred_element_type=jnp.float32)
    return total.reshape(count, height, width, -1)

def norm_silu(values, onehot, lengths, gain, bias):
    count, height, width, chans = values.shape
    share = chans // GROUPS
    size = lengths.astype(jnp.float32) * (height * width * share)
    wide = values.astype(jnp.float32)
    sums = lax.optimization_barrier(jnp.sum(wide, axis=(1, 2))).reshape(count, GROUPS, share).sum(-1)
    mean = jnp.dot(onehot.T, sums, precision=HIGH) / size[:, None]
    mean_frame = jnp.repeat(jnp.dot(onehot, mean, precision=HIGH), share, axis=1)
    centered = wide - mean_frame[:, None, None, :]
    dev = lax.optimization_barrier(jnp.sum(centered * centered, axis=(1, 2))).reshape(count, GROUPS, share).sum(-1)
    var = jnp.dot(onehot.T, dev, precision=HIGH) / size[:, None]
    scale = jnp.repeat(jnp.dot(onehot, lax.rsqrt(var + EPS), precision=HIGH), share, axis=1)
    return jax.nn.silu(centered * scale[:, None, None, :] * gain + bias).astype(jnp.bfloat16)

def shrink(values, weight):
    count, height, width, chans = values.shape
    padded = jnp.pad(values, ((0, 0), (0, 1), (0, 1), (0, 0)))
    total = jnp.zeros((count * (height // 2) * (width // 2), weight.shape[-1]), jnp.float32)
    for row in range(3):
        band = padded[:, row:row + height:2]
        patch = jnp.concatenate([band[:, :, col:col + width:2] for col in range(3)], axis=-1)
        total = total + jnp.dot(patch.reshape(-1, 3 * chans), weight[row].reshape(3 * chans, -1), preferred_element_type=jnp.float32)
    return total.reshape(count, height // 2, width // 2, -1)

def reference(pixels, counts, clip_lengths, in_weight, in_bias, norm1_gain, norm1_bias, conv1_weight, norm2_gain, norm2_bias, conv2_weight, down_weight):
    places = jnp.arange(U, dtype=jnp.int32)
    enc_ids = jnp.arange(N_DP, dtype=jnp.int32)
    columns = []
    for block in range(N_TM):
        table = counts[block].astype(jnp.int32)
        send_start = (jnp.cumsum(table, axis=1) - table).astype(jnp.int32)
        recv_end = jnp.cumsum(table, axis=0).astype(jnp.int32)
        recv_start = (recv_end - table).astype(jnp.int32)
        source = lax.optimization_barrier(jnp.sum((recv_end.T[:, None, :] <= places[None, :, None]).astype(jnp.int32), axis=2)).astype(jnp.int32)
        spot = send_start[source, enc_ids[:, None]] + places[None, :] - recv_start[source, enc_ids[:, None]]
        columns.append(pixels[source, block, spot])
    routed = jnp.stack(columns, axis=1)
    frames_all = routed.reshape(N_DP, N_TM * FT, HS, PW, 3)

    def encode(item):
        frames, lengths = item
        lengths = lengths.astype(jnp.int32)
        ends = jnp.cumsum(lengths).astype(jnp.int32)
        starts = (ends - lengths).astype(jnp.int32)
        index = jnp.arange(frames.shape[0], dtype=jnp.int32)
        ident = lax.optimization_barrier(jnp.sum((ends[None, :] <= index[:, None]).astype(jnp.int32), axis=1)).astype(jnp.int32)
        begin = jnp.take(starts, ident).astype(jnp.int32)
        onehot = (ident[:, None] == jnp.arange(lengths.shape[0], dtype=jnp.int32)[None, :]).astype(jnp.float32)
        base = (causal_conv(frames, begin, in_weight) + in_bias).astype(jnp.bfloat16)
        act1 = norm_silu(base, onehot, lengths, norm1_gain, norm1_bias)
        middle = causal_conv(act1, begin, conv1_weight).astype(jnp.bfloat16)
        act2 = norm_silu(middle, onehot, lengths, norm2_gain, norm2_bias)
        resid = (base.astype(jnp.float32) + causal_conv(act2, begin, conv2_weight)).astype(jnp.bfloat16)
        return shrink(resid, down_weight).astype(jnp.bfloat16)
    encoded = lax.map(encode, (frames_all, clip_lengths))
    enc_units = encoded.reshape(N_DP, N_TM, U, -1)
    outputs = []
    for block in range(N_TM):
        table = counts[block].astype(jnp.int32)
        send_end = jnp.cumsum(table, axis=1).astype(jnp.int32)
        send_start = (send_end - table).astype(jnp.int32)
        recv_start = (jnp.cumsum(table, axis=0) - table).astype(jnp.int32)
        owner = lax.optimization_barrier(jnp.sum((send_end[:, None, :] <= places[None, :, None]).astype(jnp.int32), axis=2)).astype(jnp.int32)
        loaders = enc_ids[:, None]
        spot = recv_start[loaders, owner] + places[None, :] - send_start[loaders, owner]
        outputs.append(enc_units[owner, block, spot])
    return jnp.stack(outputs, axis=1)
```

```python
import jax
import jax.numpy as jnp
from jax import lax
from jax.experimental import pallas as pl
from jax.experimental.pallas import tpu as pltpu
from jax.sharding import PartitionSpec as P


F32 = jnp.float32
BF16 = jnp.bfloat16
EPS = 1e-06
NDP = 32
NTM = 16
FT = 4
CLIPS = 4
CH = 128
AREA = 512
FRAME_N = AREA * 4
VMEM_LIMIT = 24 * 1024 * 1024


def iota(shape, dim):
    return lax.broadcasted_iota(jnp.int32, shape, dim)


def onehot(cond):
    return jnp.where(cond, 1.0, 0.0).astype(BF16)


def mm(a, b):
    return jnp.dot(a, b, preferred_element_type=F32)


def pick_lane(values, lane):
    return jnp.sum(jnp.where(iota(values.shape, 1) == lane, values, 0.0), axis=1, keepdims=True)


def pack_kernel(counts_ref, pixels_ref, out_ref):
    station = lax.axis_index("dp")
    table = counts_ref[0].astype(F32)
    sub, lane = iota((NDP, NDP), 0), iota((NDP, NDP), 1)
    row = jnp.sum(jnp.where(sub == station, table, 0.0), axis=0, keepdims=True)
    recv = jnp.sum(jnp.where(sub < station, table, 0.0), axis=0, keepdims=True)
    row8 = jnp.broadcast_to(row, (8, NDP))
    start = mm(row8.astype(BF16), onehot(sub < lane))[0:1]
    spread = (iota((256, NDP), 0) // 8 == iota((256, NDP), 1)).astype(F32)
    count_i = jnp.sum(spread * row, axis=1, keepdims=True)
    start_i = jnp.sum(spread * start, axis=1, keepdims=True)
    recv_i = jnp.sum(spread * recv, axis=1, keepdims=True)
    i, m = iota((256, 128), 0), iota((256, 128), 1)
    slot = ((i // 4) % 2).astype(F32)
    valid = slot < count_i
    unit = (m % 32).astype(F32)
    place = onehot((unit == start_i + slot) & (m // 32 == i % 4) & valid)
    src, dst = iota((192, 128), 0), iota((192, 128), 1)
    t = dst % 32
    wanted = 24 * (dst // 32) - 3 + t
    inside = (t < 30) & (dst < 64) & (wanted >= 0) & (wanted < 48)
    pixels = pixels_ref[0, 0]
    rows = [mm(pixels, onehot((src == 48 * q + wanted) & inside)).astype(BF16) for q in range(4)]
    packed = mm(place, jnp.concatenate(rows, axis=0))
    packed = jnp.where(m == 64, jnp.where(valid, recv_i + slot, 255.0), packed)
    out_ref[...] = packed.astype(BF16)


def spread_kernel(weight_ref, out_ref, taps_ref):
    taps_ref[...] = jnp.zeros_like(taps_ref)
    for a in range(3):
        for b in range(3):
            for c in range(3):
                taps_ref[(a * 3 + b) * 3 + c, 0:3, :] = weight_ref[a, b, c].astype(F32)
    taps = taps_ref[...].reshape(27 * 8, CH).astype(BF16)
    r, j = iota((384, 216), 0), iota((384, 216), 1)
    dyi = (r // 32) % 4
    row_key = jnp.where(dyi < 3, ((2 - r // 128) * 3 + dyi) * 64 + r % 32, -1000)
    tap, color = j // 8, j % 8
    col_key = jnp.where(color < 3, (tap // 3) * 64 + (tap % 3) * 3 + color, -5000)
    diff = row_key - col_key
    for l in range(8):
        out_ref[:, l * CH : (l + 1) * CH] = mm(onehot(diff == 3 * l), taps).astype(BF16)


def clip_ends(lengths_ref):
    ends, total = [], 0
    for c in range(CLIPS):
        total = total + lengths_ref[0, c]
        ends.append(total)
    return ends


def clip_of(ends, frame):
    ident = jnp.int32(0)
    begin = jnp.int32(0)
    for c in range(CLIPS - 1):
        past = frame >= ends[c]
        ident = jnp.where(past, jnp.int32(c + 1), ident)
        begin = jnp.where(past, ends[c], begin)
    return ident, begin


def group_sum(x):
    lane = iota(x.shape, 1)
    x = x + pltpu.roll(x, 127, 1)
    x = x + pltpu.roll(x, 126, 1)
    x = jnp.where(lane % 4 == 0, x, 0.0)
    x = x + pltpu.roll(x, 1, 1)
    return x + pltpu.roll(x, 2, 1)


def shift_k(tile, step):
    moved = pltpu.roll(tile, step % 8, 0)
    return jnp.where(iota(tile.shape, 0) == (0 if step == 1 else 7), 0.0, moved)


def unpack_rows(arrived):
    wide = arrived.astype(F32)
    pos = wide[:, 64:65].astype(jnp.int32)
    i, m = iota((256, 128), 0), iota((256, 128), 1)
    target = (pos // 8) * 32 + (i % 4) * 8 + pos % 8
    select = jnp.where((m == target) & (pos < 32), 1.0, 0.0)
    rows = mm(select.T.astype(BF16), arrived)
    return jnp.where(iota((128, 128), 1) < 64, rows, 0.0)


def base_kernel(lengths_ref, own_ref, prev_ref, matrix_ref, bias_ref, base_ref, stat_ref, x_ref, lhs_ref):
    column = lax.axis_index("tm")
    low = iota((8, 128), 1) < 32
    for block, ref in enumerate((prev_ref, own_ref)):
        rows = unpack_rows(ref[...])
        for f in range(4):
            tiles = [rows[f * 32 + q * 8 : f * 32 + q * 8 + 8] for q in range(4)]
            out = []
            for q in range(4):
                above = tiles[q - 1] if q > 0 else shift_k(tiles[3], 1)
                below = tiles[q + 1] if q < 3 else shift_k(tiles[0], -1)
                for h in range(2):
                    a, b, c = above, tiles[q], below
                    if h:
                        a, b, c = (pltpu.roll(v, 96, 1) for v in (a, b, c))
                    a, b, c = (jnp.where(low, v, 0.0) for v in (a, b, c))
                    out.append(a + pltpu.roll(b, 32, 1) + pltpu.roll(c, 64, 1))
            x_ref[block * 4 + f] = jnp.concatenate(out, axis=0).astype(BF16)
    ends = clip_ends(lengths_ref)
    for o in range(6):
        frame = column * FT - 2 + o
        unused, begin = clip_of(ends, frame)
        for lag in range(3):
            p = jnp.clip(jnp.maximum(frame - lag, begin) - (column * FT - 4), 0, 7)
            lhs_ref[o * 64 : (o + 1) * 64, lag * 128 : (lag + 1) * 128] = x_ref[p]
    bias = bias_ref[...]
    sums = [jnp.zeros((1, CH), F32)] * 4
    for pair in range(4):
        both = mm(lhs_ref[...], matrix_ref[:, pair * 256 : (pair + 1) * 256])
        for half in range(2):
            value = (both[:, half * CH : (half + 1) * CH] + bias).astype(BF16)
            for o in range(6):
                part = value[o * 64 : (o + 1) * 64]
                base_ref[o, pair * 2 + half] = part.reshape(4, 16, CH)
                if o >= 2:
                    sums[o - 2] = sums[o - 2] + jnp.sum(part.astype(F32), axis=0, keepdims=True)
    total = group_sum(jnp.concatenate(sums, axis=0))
    devs = []
    for o in range(4):
        wide = base_ref[o + 2].astype(F32).reshape(AREA, CH) - total[o : o + 1] * (1.0 / FRAME_N)
        devs.append(jnp.sum(wide * wide, axis=0, keepdims=True))
    stats = jnp.concatenate([total, group_sum(jnp.concatenate(devs, axis=0))], axis=0)
    for j in range(NTM):
        stat_ref[j] = stats


def clip_scales(stats, lengths_ref, ends, gain, norm_ref):
    frame = iota((NTM, 8, CH), 0) * FT + iota((NTM, 8, CH), 1) % 4
    is_sum = iota((NTM, 8, CH), 1) < 4
    for c in range(CLIPS):
        inside = frame < ends[c]
        if c:
            inside = inside & (frame >= ends[c - 1])
        size = (lengths_ref[0, c] * FRAME_N).astype(F32)
        kept = jnp.sum(jnp.where(inside & is_sum, stats, 0.0), axis=0)
        mean = jnp.sum(kept, axis=0, keepdims=True) / size
        off = stats * (1.0 / FRAME_N) - mean
        dev = jnp.where(is_sum, FRAME_N * (off * off), stats)
        kept = jnp.sum(jnp.where(inside, dev, 0.0), axis=0)
        var = jnp.sum(kept, axis=0, keepdims=True) / size
        norm_ref[c, 0:1, :] = mean
        norm_ref[c, 1:2, :] = lax.rsqrt(var + EPS) * gain


def store_padded(act_ref, o, place, tiles):
    column = []
    for h in range(2):
        own = [tiles[q][h] for q in range(4)]
        column.append([shift_k(own[3], 1)] + own + [shift_k(own[0], -1)])
    flat = [column[h][q] for q in range(6) for h in range(2)]
    act_ref[o, place] = jnp.concatenate(flat, axis=0).astype(BF16).reshape(6, 16, CH)


def norm_frame(value_of, act_ref, o, mean, scale, bias):
    zero = jnp.zeros((8, CH), F32)
    for l in range(8):
        v = (value_of(l).astype(F32).reshape(64, CH) - mean) * scale + bias
        v = v / (1.0 + jnp.exp(-v))
        tiles = [[v[q * 16 + h * 8 : q * 16 + h * 8 + 8] for h in range(2)] for q in range(4)]
        store_padded(act_ref, o, l + 1, tiles)
        if l == 0:
            store_padded(act_ref, o, 9, [[tiles[q][1], zero] for q in range(4)])
        if l == 7:
            store_padded(act_ref, o, 0, [[zero, tiles[q][0]] for q in range(4)])


def conv_frame(act_ref, weight_ref, picks):
    total = None
    for lag in range(3):
        taps = []
        for row in range(3):
            for col in range(3):
                taps.append(act_ref[picks[lag], col : col + 8, row : row + 4].reshape(AREA, CH))
        matrix = weight_ref[2 - lag].reshape(9 * CH, CH)
        part = mm(jnp.concatenate(taps, axis=1), matrix)
        total = part if total is None else total + part
    return total


def frame_picks(ends, column, o):
    frame = column * FT - 2 + o
    unused, begin = clip_of(ends, frame)
    return [jnp.clip(jnp.maximum(frame - lag, begin) - (column * FT - 2), 0, 5) for lag in range(3)]


def conv1_kernel(
    lengths_ref, base_ref, stats_ref, gain_ref, bias_ref, weight_ref,
    middle_ref, tail_ref, stat_ref, act_ref, norm_ref, own_ref,
):
    column = lax.axis_index("tm")
    ends = clip_ends(lengths_ref)
    clip_scales(stats_ref[...], lengths_ref, ends, gain_ref[...], norm_ref)
    bias = bias_ref[...]

    def norm_step(o, carry):
        ident, unused = clip_of(ends, column * FT - 2 + o)
        norm_frame(lambda l: base_ref[o, l], act_ref, o, norm_ref[ident, 0:1, :], norm_ref[ident, 1:2, :], bias)
        return carry

    lax.fori_loop(0, 6, norm_step, 0)

    def conv_step(f, carry):
        total = conv_frame(act_ref, weight_ref, frame_picks(ends, column, f + 2)).astype(BF16)
        middle_ref[f] = total.reshape(8, 4, 16, CH)
        wide = total.astype(F32)
        sums = group_sum(jnp.broadcast_to(jnp.sum(wide, axis=0, keepdims=True), (8, CH)))
        wide = wide - sums[0:1] * (1.0 / FRAME_N)
        devs = group_sum(jnp.broadcast_to(jnp.sum(wide * wide, axis=0, keepdims=True), (8, CH)))
        own_ref[f] = sums
        own_ref[f + 4] = devs
        return carry

    lax.fori_loop(0, 4, conv_step, 0)
    tail_ref[...] = middle_ref[2:4]
    stats = jnp.concatenate([own_ref[n, 0:1, :] for n in range(8)], axis=0)
    for j in range(NTM):
        stat_ref[j] = stats


def conv2_kernel(
    lengths_ref, counts_ref, base_ref, middle_ref, lead_ref, stats_ref, gain_ref, bias_ref, weight_ref, down_ref,
    out_ref, act_ref, norm_ref, resid_ref, latent_ref,
):
    column = lax.axis_index("tm")
    station = lax.axis_index("dp")
    ends = clip_ends(lengths_ref)
    clip_scales(stats_ref[...], lengths_ref, ends, gain_ref[...], norm_ref)
    bias = bias_ref[...]

    def norm_step(source):
        def step(o, carry):
            ident, unused = clip_of(ends, column * FT - 2 + o)
            value_of = (lambda l: lead_ref[o, l]) if source == 0 else (lambda l: middle_ref[o - 2, l])
            norm_frame(value_of, act_ref, o, norm_ref[ident, 0:1, :], norm_ref[ident, 1:2, :], bias)
            return carry

        return step

    lax.fori_loop(0, 2, norm_step(0), 0)
    lax.fori_loop(2, 6, norm_step(1), 0)
    down = down_ref[...].reshape(9 * CH, CH)

    def conv_step(f, carry):
        total = conv_frame(act_ref, weight_ref, frame_picks(ends, column, f + 2))
        resid = base_ref[f + 2].astype(F32).reshape(AREA, CH) + total
        resid = resid.astype(BF16).astype(F32)
        zero = jnp.zeros((8, CH), F32)

        def put(l, tiles):
            flat = [tiles[q][h] for q in range(4) for h in range(2)]
            flat = flat + [shift_k(tiles[0][h], -1) for h in range(2)]
            resid_ref[l] = jnp.concatenate(flat, axis=0).astype(BF16).reshape(5, 16, CH)

        for l in range(8):
            v = resid[l * 64 : (l + 1) * 64]
            tiles = [[v[q * 16 + h * 8 : q * 16 + h * 8 + 8] for h in range(2)] for q in range(4)]
            put(l, tiles)
            if l == 0:
                put(8, [[tiles[q][1], zero] for q in range(4)])
        taps = []
        for row in range(3):
            for col in range(3):
                parts = [resid_ref[2 * j + col, 2 * par + row] for j in range(4) for par in range(2)]
                taps.append(jnp.concatenate(parts, axis=0))
        latent = mm(jnp.concatenate(taps, axis=1), down)
        for j in range(4):
            for w in range(4):
                latent_ref[w, pl.ds(f * 8, 8), j * CH : (j + 1) * CH] = latent[j * 32 + w * 8 : j * 32 + w * 8 + 8]
        return carry

    lax.fori_loop(0, 4, conv_step, 0)
    table = counts_ref[0].astype(F32).astype(BF16)
    loader, other = iota((256, NDP), 0) // 8, iota((256, NDP), 1)
    count_i = pick_lane(mm(onehot(loader == other), table), station)
    start_i = pick_lane(mm(onehot(other < loader), table), station)
    i, m = iota((256, 128), 0), iota((256, 128), 1)
    slot = ((i // 4) % 2).astype(F32)
    place = onehot(((m % 32).astype(F32) == start_i + slot) & (m // 32 == i % 4) & (slot < count_i))
    out_ref[...] = mm(place, latent_ref[...].reshape(128, 512).astype(BF16)).astype(BF16)


def return_kernel(counts_ref, back_ref, out_ref):
    station = lax.axis_index("dp")
    table = counts_ref[0].astype(F32)
    sub, lane = iota((NDP, NDP), 0), iota((NDP, NDP), 1)
    row = jnp.sum(jnp.where(sub == station, table, 0.0), axis=0, keepdims=True)
    row8 = jnp.broadcast_to(row, (8, NDP)).astype(BF16)
    encoder, other = iota((NDP, 256), 1) // 8, iota((NDP, 256), 0)
    count_i = mm(row8, onehot(encoder == other))[0:1]
    start_i = mm(row8, onehot(other < encoder))[0:1]
    r, i = iota((128, 256), 0), iota((128, 256), 1)
    slot = ((i // 4) % 2).astype(F32)
    select = onehot(((r % 32).astype(F32) == start_i + slot) & (r // 32 == i % 4) & (slot < count_i))
    units = mm(select, back_ref[...]).astype(BF16)
    for w in range(4):
        out_ref[0, 0, :, w * 512 : (w + 1) * 512] = units[w * 32 : (w + 1) * 32]


VMEM = pl.BlockSpec(memory_space=pltpu.VMEM)
SMEM = pl.BlockSpec(memory_space=pltpu.SMEM)


def kernel_call(body, name, in_specs, outs, scratch=(), flops=0, bytes_accessed=1 << 20):
    outs = [jax.ShapeDtypeStruct(shape, dtype) for shape, dtype in outs]
    return pl.pallas_call(
        body,
        name=name,
        in_specs=in_specs,
        out_specs=[VMEM] * len(outs) if len(outs) > 1 else VMEM,
        out_shape=outs if len(outs) > 1 else outs[0],
        scratch_shapes=list(scratch),
        compiler_params=pltpu.CompilerParams(vmem_limit_bytes=VMEM_LIMIT),
        cost_estimate=pl.CostEstimate(flops=flops, bytes_accessed=bytes_accessed, transcendentals=0),
    )


def per_device(
    pixels,
    counts,
    clip_lengths,
    in_weight,
    in_bias,
    norm1_gain,
    norm1_bias,
    conv1_weight,
    norm2_gain,
    norm2_bias,
    conv2_weight,
    down_weight,
):
    row = lambda v: v.reshape(1, CH)
    packed = kernel_call(pack_kernel, "pack", [VMEM] * 2, [((256, 128), BF16)])(counts, pixels)
    arrived = lax.all_to_all(packed, "dp", split_axis=0, concat_axis=0, tiled=True)
    matrix = kernel_call(
        spread_kernel, "spread", [VMEM], [((384, 8 * CH), BF16)], [pltpu.VMEM((27, 8, CH), F32)], flops=1 << 28
    )(in_weight)
    onward = [(source, source + 1) for source in range(NTM - 1)]
    before = lax.ppermute(arrived, "tm", onward)
    base, stats = kernel_call(
        base_kernel,
        "base",
        [SMEM] + [VMEM] * 4,
        [((6, 8, 4, 16, CH), BF16), ((NTM, 8, CH), F32)],
        [pltpu.VMEM((8, 64, 128), BF16), pltpu.VMEM((384, 384), BF16)],
    )(clip_lengths, arrived, before, matrix, row(in_bias))
    stats = lax.all_to_all(stats, "tm", split_axis=0, concat_axis=0, tiled=True)
    act = pltpu.VMEM((6, 10, 6, 16, CH), BF16)
    norm = pltpu.VMEM((CLIPS, 8, CH), F32)
    middle, tail, stats = kernel_call(
        conv1_kernel,
        "conv1",
        [SMEM] + [VMEM] * 5,
        [((4, 8, 4, 16, CH), BF16), ((2, 8, 4, 16, CH), BF16), ((NTM, 8, CH), F32)],
        [act, norm, pltpu.VMEM((8, 8, CH), F32)],
        flops=1 << 31,
    )(clip_lengths, base, stats, row(norm1_gain), row(norm1_bias), conv1_weight)
    lead = lax.ppermute(tail, "tm", onward)
    stats = lax.all_to_all(stats, "tm", split_axis=0, concat_axis=0, tiled=True)
    packed = kernel_call(
        conv2_kernel,
        "conv2",
        [SMEM] + [VMEM] * 9,
        [((256, 512), BF16)],
        [act, norm, pltpu.VMEM((9, 5, 16, CH), BF16), pltpu.VMEM((4, 32, 512), F32)],
        flops=1 << 31,
    )(clip_lengths, counts, base, middle, lead, stats, row(norm2_gain), row(norm2_bias), conv2_weight, down_weight)
    returned = lax.all_to_all(packed, "dp", split_axis=0, concat_axis=0, tiled=True)
    return kernel_call(return_kernel, "place", [VMEM] * 2, [((1, 1, 32, 2048), BF16)])(counts, returned)


def solution(mesh):
    in_specs = (
        P("dp", "tm", None, None),
        P("tm", None, None),
        P("dp", None),
        P(),
        P(),
        P(),
        P(),
        P(),
        P(),
        P(),
        P(),
        P(),
    )
    out_specs = P("dp", "tm", None, None)
    return jax.shard_map(
        per_device, mesh=mesh, in_specs=in_specs, out_specs=out_specs, check_vma=False
    )
```

```python
import jax
import jax.numpy as jnp
from jax import lax
from jax.experimental import pallas as pl
from jax.experimental.pallas import tpu as pltpu
from jax.sharding import PartitionSpec as P


F32 = jnp.float32
BF16 = jnp.bfloat16
EPS = 1e-06
NDP = 32
NTM = 16
FT = 4
CLIPS = 4
CH = 128
AREA = 512
FRAME_N = AREA * 4
VMEM_LIMIT = 24 * 1024 * 1024


def iota(shape, dim):
    return lax.broadcasted_iota(jnp.int32, shape, dim)


def onehot(cond):
    return jnp.where(cond, 1.0, 0.0).astype(BF16)


def mm(a, b):
    return jnp.dot(a, b, preferred_element_type=F32)


def pick_lane(values, lane):
    return jnp.sum(jnp.where(iota(values.shape, 1) == lane, values, 0.0), axis=1, keepdims=True)


def pack_kernel(joined_ref, out_ref):
    station = lax.axis_index("dp")
    joined = joined_ref[...]
    table = joined[:, :NDP].astype(F32)
    sub, lane = iota((NDP, NDP), 0), iota((NDP, NDP), 1)
    row = jnp.sum(jnp.where(sub == station, table, 0.0), axis=0, keepdims=True)
    recv = jnp.sum(jnp.where(sub < station, table, 0.0), axis=0, keepdims=True)
    row8 = jnp.broadcast_to(row, (8, NDP))
    start = mm(row8.astype(BF16), onehot(sub < lane))[0:1]
    spread = (iota((256, NDP), 0) // 8 == iota((256, NDP), 1)).astype(F32)
    count_i = jnp.sum(spread * row, axis=1, keepdims=True)
    start_i = jnp.sum(spread * start, axis=1, keepdims=True)
    recv_i = jnp.sum(spread * recv, axis=1, keepdims=True)
    i, m = iota((256, 128), 0), iota((256, 128), 1)
    slot = ((i // 4) % 2).astype(F32)
    valid = slot < count_i
    unit = (m % 32).astype(F32)
    place = onehot((unit == start_i + slot) & (m // 32 == i % 4) & valid)
    src, dst = iota((NDP + 192, 128), 0) - NDP, iota((NDP + 192, 128), 1)
    t = dst % 32
    wanted = 24 * (dst // 32) - 3 + t
    inside = (t < 30) & (dst < 64) & (wanted >= 0) & (wanted < 48)
    rows = [mm(joined, onehot((src == 48 * q + wanted) & inside)).astype(BF16) for q in range(4)]
    packed = mm(place, jnp.concatenate(rows, axis=0))
    packed = jnp.where(m == 64, jnp.where(valid, recv_i + slot, 255.0), packed)
    out_ref[...] = packed.astype(BF16)


def spread_kernel(weight_ref, lengths_ref, *refs):
    vector_refs, (out_ref, vectors_ref, along_ref, taps_ref) = refs[:5], refs[5:]
    along_ref[...] = lengths_ref[...]
    for n, ref in enumerate(vector_refs):
        vectors_ref[n : n + 1, :] = ref[...]
    taps_ref[...] = jnp.zeros_like(taps_ref)
    for a in range(3):
        for b in range(3):
            for c in range(3):
                taps_ref[(a * 3 + b) * 3 + c, 0:3, :] = weight_ref[a, b, c].astype(F32)
    taps = taps_ref[...].reshape(27 * 8, CH).astype(BF16)
    r, j = iota((384, 216), 0), iota((384, 216), 1)
    dyi = (r // 32) % 4
    row_key = jnp.where(dyi < 3, ((2 - r // 128) * 3 + dyi) * 64 + r % 32, -1000)
    tap, color = j // 8, j % 8
    col_key = jnp.where(color < 3, (tap // 3) * 64 + (tap % 3) * 3 + color, -5000)
    diff = row_key - col_key
    for l in range(8):
        out_ref[:, l * CH : (l + 1) * CH] = mm(onehot(diff == 3 * l), taps).astype(BF16)


def clip_ends(lengths_ref):
    ends, total = [], 0
    for c in range(CLIPS):
        total = total + lengths_ref[0, c]
        ends.append(total)
    return ends


def clip_of(ends, frame):
    ident = jnp.int32(0)
    begin = jnp.int32(0)
    for c in range(CLIPS - 1):
        past = frame >= ends[c]
        ident = jnp.where(past, jnp.int32(c + 1), ident)
        begin = jnp.where(past, ends[c], begin)
    return ident, begin


def group_sum(x):
    lane = iota(x.shape, 1)
    x = x + pltpu.roll(x, 127, 1)
    x = x + pltpu.roll(x, 126, 1)
    x = jnp.where(lane % 4 == 0, x, 0.0)
    x = x + pltpu.roll(x, 1, 1)
    return x + pltpu.roll(x, 2, 1)


def shift_k(tile, step):
    moved = pltpu.roll(tile, step % 8, 0)
    return jnp.where(iota(tile.shape, 0) == (0 if step == 1 else 7), 0.0, moved)


class Moments:
    def __init__(self):
        self.pivot = None

    def add(self, rows):
        if self.pivot is None:
            self.pivot = rows[0:1]
            self.first = self.second = jnp.zeros((8, CH), F32)
        off = rows - self.pivot
        square = off * off
        self.first = self.first + fold(off)
        self.second = self.second + fold(square)

    def done(self):
        first = jnp.sum(self.first, axis=0, keepdims=True)
        second = jnp.sum(self.second, axis=0, keepdims=True)
        return first + AREA * self.pivot, second - first * first * (1.0 / AREA)


def fold(rows):
    return tree([rows[n : n + 8] for n in range(0, rows.shape[0], 8)])


def exact_mm(rows, matrix):
    high = rows.astype(BF16).astype(F32)
    middle = (rows - high).astype(BF16).astype(F32)
    low = rows - high - middle
    parts = mm(jnp.concatenate([high, middle, low, low], axis=0).astype(BF16), matrix)
    return parts[0:8] + parts[8:16] + parts[16:24]


def put_stats(pairs, stat_ref):
    sums = jnp.concatenate([p[0] for p in pairs], axis=0)
    devs = jnp.concatenate([p[1] for p in pairs], axis=0)
    off = sums * (1.0 / AREA) - group_sum(sums) * (1.0 / FRAME_N)
    rows = jnp.concatenate([sums, devs + AREA * (off * off)], axis=0)
    narrow = exact_mm(rows, onehot(iota((CH, 128), 0) // 4 == iota((CH, 128), 1) % 32))
    own = jnp.where(iota((8, 128), 0) % FT == iota((8, 128), 1) // 32, narrow, 0.0)
    stats = jnp.concatenate([jnp.sum(own[n : n + 4], axis=0, keepdims=True) for n in (0, 4)], axis=0)
    for j in range(NTM):
        stat_ref[j] = stats


def unpack_rows(arrived):
    wide = arrived.astype(F32)
    pos = wide[:, 64:65].astype(jnp.int32)
    i, m = iota((256, 128), 0), iota((256, 128), 1)
    target = (pos // 8) * 32 + (i % 4) * 8 + pos % 8
    select = jnp.where((m == target) & (pos < 32), 1.0, 0.0)
    rows = mm(select.T.astype(BF16), arrived)
    return jnp.where(iota((128, 128), 1) < 64, rows, 0.0)


def frame_rows(arrived, x_ref, first):
    low = iota((8, 128), 1) < 32
    rows = unpack_rows(arrived)
    for f in range(FT):
        tiles = [rows[f * 32 + q * 8 : f * 32 + q * 8 + 8] for q in range(4)]
        out = []
        for q in range(4):
            above = tiles[q - 1] if q > 0 else shift_k(tiles[3], 1)
            below = tiles[q + 1] if q < 3 else shift_k(tiles[0], -1)
            for h in range(2):
                a, b, c = above, tiles[q], below
                if h:
                    a, b, c = (pltpu.roll(v, 96, 1) for v in (a, b, c))
                a, b, c = (jnp.where(low, v, 0.0) for v in (a, b, c))
                out.append(a + pltpu.roll(b, 32, 1) + pltpu.roll(c, 64, 1))
        x_ref[first + f] = jnp.concatenate(out, axis=0).astype(BF16)


def base_frames(lengths_ref, x_ref, x_first, lhs_ref, matrix_ref, vectors_ref, base_ref, first):
    column = lax.axis_index("tm")
    ends = clip_ends(lengths_ref)
    count = base_ref.shape[0]
    for n in range(count):
        frame = column * FT - 2 + first + n
        unused, begin = clip_of(ends, frame)
        for lag in range(3):
            p = jnp.clip(jnp.maximum(frame - lag, begin) - (column * FT + x_first), 0, x_ref.shape[0] - 1)
            lhs_ref[n * 64 : (n + 1) * 64, lag * 128 : (lag + 1) * 128] = x_ref[p]
    bias = vectors_ref[0:1, :]
    moments = [Moments() for unused in range(count)]
    for pair in range(4):
        both = mm(lhs_ref[...], matrix_ref[:, pair * 256 : (pair + 1) * 256])
        for half in range(2):
            value = (both[:, half * CH : (half + 1) * CH] + bias).astype(BF16)
            for n in range(count):
                part = value[n * 64 : (n + 1) * 64]
                base_ref[n, pair * 2 + half] = part.reshape(4, 16, CH)
                if first + n >= 2:
                    moments[n].add(part.astype(F32))
    return [m.done() for m in moments if m.pivot is not None]


def late_kernel(lengths_ref, own_ref, matrix_ref, vectors_ref, base_ref, x_ref, part_ref, lhs_ref):
    frame_rows(own_ref[...], x_ref, 0)
    pairs = base_frames(lengths_ref, x_ref, 0, lhs_ref, matrix_ref, vectors_ref, base_ref, 4)
    part_ref[...] = jnp.concatenate([p[0] for p in pairs] * 2 + [p[1] for p in pairs] * 2, axis=0)


def early_kernel(
    lengths_ref, prev_ref, own_ref, part_ref, matrix_ref, vectors_ref, base_ref, stat_ref, x_ref, lhs_ref
):
    frame_rows(prev_ref[...], x_ref, 0)
    x_ref[FT:] = own_ref[...]
    pairs = base_frames(lengths_ref, x_ref, -FT, lhs_ref, matrix_ref, vectors_ref, base_ref, 0)
    pairs = pairs + [(part_ref[n : n + 1, :], part_ref[n + 4 : n + 5, :]) for n in range(2)]
    put_stats(pairs, stat_ref)


def clip_scales(stats_ref, lengths_ref, ends, gain, norm_ref):
    sums, devs = stats_ref[:, 0, :], stats_ref[:, 1, :]
    frame = iota((NTM, 128), 0) * FT + iota((NTM, 128), 1) // 32
    inside = [frame < ends[0]] + [(frame >= ends[c - 1]) & (frame < ends[c]) for c in range(1, CLIPS)]
    size = [(lengths_ref[0, c] * FRAME_N).astype(F32) for c in range(CLIPS)]

    def clip_mean(values):
        rows = [
            jnp.sum(jnp.where(inside[c], values[c], 0.0), axis=0, keepdims=True) / size[c] for c in range(CLIPS)
        ]
        rows = jnp.concatenate(rows, axis=0)
        rows = rows + pltpu.roll(rows, 32, 1)
        return rows + pltpu.roll(rows, 64, 1)

    means = clip_mean([sums] * CLIPS)
    offs = [sums * (1.0 / FRAME_N) - means[c : c + 1] for c in range(CLIPS)]
    scales = lax.rsqrt(clip_mean([devs + FRAME_N * (off * off) for off in offs]) + EPS)
    wide = exact_mm(jnp.concatenate([means, scales], axis=0), onehot(iota((128, CH), 0) == iota((128, CH), 1) // 4))
    norm_ref[...] = jnp.where(iota((8, CH), 0) < CLIPS, wide, wide * (0.5 * gain))


def clip_norm(norm_ref, ident):
    return norm_ref[pl.ds(ident, 1), :], norm_ref[pl.ds(ident + CLIPS, 1), :]


def tree(parts):
    while len(parts) > 1:
        parts = [a + b for a, b in zip(parts[0::2], parts[1::2])]
    return parts[0]


def store_padded(places, l, tiles):
    column = []
    for h in range(2):
        own = [tiles[q][h] for q in range(4)]
        column.append([shift_k(own[3], 1)] + own + [shift_k(own[0], -1)])
    flat = [column[h][q] for q in range(6) for h in range(2)]
    padded = jnp.concatenate(flat, axis=0).astype(BF16).reshape(6, 16, CH)
    for act_ref, o in places:
        act_ref[o, l] = padded


def norm_frame(value_of, places, mean, scale, bias):
    zero = jnp.zeros((8, CH), F32)
    for l in range(8):
        v = (value_of(l).astype(F32).reshape(64, CH) - mean) * scale + bias
        v = v + v * jnp.tanh(v)
        tiles = [[v[q * 16 + h * 8 : q * 16 + h * 8 + 8] for h in range(2)] for q in range(4)]
        store_padded(places, l + 1, tiles)
        if l == 0:
            store_padded(places, 9, [[tiles[q][1], zero] for q in range(4)])
        if l == 7:
            store_padded(places, 0, [[zero, tiles[q][0]] for q in range(4)])


class Norm:
    def __init__(self, norm_ref, ends, column, bias):
        self.norm_ref, self.ends, self.column, self.bias = norm_ref, ends, column, 0.5 * bias

    def frame(self, ref, n, o, places):
        ident, unused = clip_of(self.ends, self.column * FT - 2 + o)
        mean, scale = clip_norm(self.norm_ref, ident)
        norm_frame(lambda l: ref[n, l], places, mean, scale, self.bias)

    def loop(self, ref, n, o, count, places):
        def step(i, carry):
            self.frame(ref, n + i, o + i, [(act_ref, first + i) for act_ref, first in places])
            return carry

        lax.fori_loop(0, count, step, 0)


def conv_frames(act_ref, weight_ref, picks):
    taps = [(z, r) for z in range(3) for r in range(3)]

    def rows(first):
        blocks = []
        for pick in picks:
            parts = [
                act_ref[pick[2 - z], first : first + 9 - first // 2, r : r + 4].reshape(-1, CH) for z, r in taps
            ]
            blocks.append(jnp.concatenate(parts, axis=1))
        return jnp.concatenate(blocks, axis=0)

    left, here, right = (jnp.concatenate([weight_ref[z, r, c] for z, r in taps], axis=0) for c in range(3))
    both = mm(rows(0), jnp.concatenate([left, here], axis=1))
    last = mm(rows(2), right)
    totals = []
    for n in range(len(picks)):
        at = n * 576
        totals.append(
            both[at : at + AREA, :CH] + both[at + 64 : at + 576, CH:] + last[n * AREA : (n + 1) * AREA]
        )
    return totals


def frame_picks(ends, column, o, first):
    frame = column * FT - 2 + o
    unused, begin = clip_of(ends, frame)
    return [
        jnp.clip(jnp.maximum(frame - lag, begin) - (column * FT - 2 + first), 0, o - first) for lag in range(3)
    ]


def conv_halves(norm, sources, low_ref, high_ref, weight_ref):
    (a, an), (b, bn), (c, cn) = sources
    norm.loop(a, an, 0, 2, [(low_ref, 0)])
    norm.loop(b, bn, 2, 2, [(low_ref, 2), (high_ref, 0)])
    picks = lambda o, first: frame_picks(norm.ends, norm.column, o, first)
    totals = conv_frames(low_ref, weight_ref, [picks(2, 0), picks(3, 0)])
    norm.frame(c, cn, 4, [(high_ref, 2)])
    norm.frame(c, cn + 1, 5, [(high_ref, 3)])
    yield 0, totals
    yield 2, conv_frames(high_ref, weight_ref, [picks(4, 2), picks(5, 2)])


def conv1_kernel(
    lengths_ref, early_ref, late_ref, stats_ref, vectors_ref, weight_ref,
    middle_ref, tail_ref, stat_ref, low_ref, high_ref, norm_ref,
):
    column = lax.axis_index("tm")
    ends = clip_ends(lengths_ref)
    clip_scales(stats_ref, lengths_ref, ends, vectors_ref[1:2, :], norm_ref)
    norm = Norm(norm_ref, ends, column, vectors_ref[2:3, :])
    pairs = []
    for first, totals in conv_halves(
        norm, [(early_ref, 0), (early_ref, 2), (late_ref, 0)], low_ref, high_ref, weight_ref
    ):
        for f, total in enumerate(totals, first):
            value = total.astype(BF16)
            middle_ref[f] = value.reshape(8, 4, 16, CH)
            if f >= 2:
                tail_ref[f - 2] = value.reshape(8, 4, 16, CH)
            moments = Moments()
            moments.add(value.astype(F32))
            pairs.append(moments.done())
    put_stats(pairs, stat_ref)


def conv2_kernel(
    lengths_ref, counts_ref, early_ref, late_ref, middle_ref, lead_ref, stats_ref, vectors_ref, weight_ref, down_ref,
    out_ref, low_ref, high_ref, norm_ref, resid_ref, later_ref, latent_ref,
):
    column = lax.axis_index("tm")
    station = lax.axis_index("dp")
    ends = clip_ends(lengths_ref)
    clip_scales(stats_ref, lengths_ref, ends, vectors_ref[3:4, :], norm_ref)
    norm = Norm(norm_ref, ends, column, vectors_ref[4:5, :])
    down = down_ref[...].reshape(9 * CH, CH)
    zero = jnp.zeros((8, CH), F32)

    def put(ref, f, l, tiles):
        flat = [tiles[q][h] for q in range(4) for h in range(2)]
        flat = flat + [shift_k(tiles[0][h], -1) for h in range(2)]
        ref[f, l] = jnp.concatenate(flat, axis=0).astype(BF16).reshape(5, 16, CH)

    for first, totals in conv_halves(
        norm, [(lead_ref, 0), (middle_ref, 0), (middle_ref, 2)], low_ref, high_ref, weight_ref
    ):
        half_ref, base_ref = (later_ref, late_ref) if first else (resid_ref, early_ref)
        for f, total in enumerate(totals):
            base = base_ref[f if first else f + 2]
            resid = base.astype(F32).reshape(AREA, CH) + total
            resid = resid.astype(BF16).astype(F32)
            for l in range(8):
                v = resid[l * 64 : (l + 1) * 64]
                tiles = [[v[q * 16 + h * 8 : q * 16 + h * 8 + 8] for h in range(2)] for q in range(4)]
                put(half_ref, f, l, tiles)
                if l == 0:
                    put(half_ref, f, 8, [[tiles[q][1], zero] for q in range(4)])
        taps = []
        for row in range(3):
            for col in range(3):
                parts = [
                    half_ref[f, 2 * j + col, 2 * par + row] for f in range(2) for j in range(4) for par in range(2)
                ]
                taps.append(jnp.concatenate(parts, axis=0))
        latent = mm(jnp.concatenate(taps, axis=1), down)
        for f in range(2):
            for j in range(4):
                for w in range(4):
                    at, to = f * 128 + j * 32 + w * 8, (first + f) * 8
                    latent_ref[w, to : to + 8, j * CH : (j + 1) * CH] = latent[at : at + 8]
    table = counts_ref[0].astype(F32).astype(BF16)
    loader, other = iota((256, NDP), 0) // 8, iota((256, NDP), 1)
    count_i = pick_lane(mm(onehot(loader == other), table), station)
    start_i = pick_lane(mm(onehot(other < loader), table), station)
    i, m = iota((256, 128), 0), iota((256, 128), 1)
    slot = ((i // 4) % 2).astype(F32)
    place = onehot(((m % 32).astype(F32) == start_i + slot) & (m // 32 == i % 4) & (slot < count_i))
    out_ref[...] = mm(place, latent_ref[...].reshape(128, 512).astype(BF16)).astype(BF16)


def return_kernel(counts_ref, back_ref, out_ref):
    station = lax.axis_index("dp")
    table = counts_ref[0].astype(F32)
    sub, lane = iota((NDP, NDP), 0), iota((NDP, NDP), 1)
    row = jnp.sum(jnp.where(sub == station, table, 0.0), axis=0, keepdims=True)
    row8 = jnp.broadcast_to(row, (8, NDP)).astype(BF16)
    encoder, other = iota((NDP, 256), 1) // 8, iota((NDP, 256), 0)
    count_i = mm(row8, onehot(encoder == other))[0:1]
    start_i = mm(row8, onehot(other < encoder))[0:1]
    r, i = iota((128, 256), 0), iota((128, 256), 1)
    slot = ((i // 4) % 2).astype(F32)
    select = onehot(((r % 32).astype(F32) == start_i + slot) & (r // 32 == i % 4) & (slot < count_i))
    units = mm(select, back_ref[...]).astype(BF16)
    for w in range(4):
        out_ref[0, 0, :, w * 512 : (w + 1) * 512] = units[w * 32 : (w + 1) * 32]


VMEM = pl.BlockSpec(memory_space=pltpu.VMEM)
SMEM = pl.BlockSpec(memory_space=pltpu.SMEM)


def kernel_call(body, name, in_specs, outs, scratch=(), flops=0, bytes_accessed=1 << 20, limit=VMEM_LIMIT):
    outs = [jax.ShapeDtypeStruct(shape, dtype) for shape, dtype in outs]
    return pl.pallas_call(
        body,
        name=name,
        in_specs=in_specs,
        out_specs=[VMEM] * len(outs) if len(outs) > 1 else VMEM,
        out_shape=outs if len(outs) > 1 else outs[0],
        scratch_shapes=list(scratch),
        compiler_params=pltpu.CompilerParams(vmem_limit_bytes=limit),
        cost_estimate=pl.CostEstimate(flops=flops, bytes_accessed=bytes_accessed, transcendentals=0),
    )


def per_device(
    pixels,
    counts,
    clip_lengths,
    in_weight,
    in_bias,
    norm1_gain,
    norm1_bias,
    conv1_weight,
    norm2_gain,
    norm2_bias,
    conv2_weight,
    down_weight,
):
    row = lambda v: v.reshape(1, CH)
    joined = jnp.concatenate([counts[0].astype(BF16), pixels[0, 0]], axis=1)
    packed = kernel_call(pack_kernel, "pack", [VMEM], [((256, 128), BF16)])(joined)
    arrived = lax.all_to_all(packed, "dp", split_axis=0, concat_axis=0, tiled=True)
    matrix, vectors, lengths = kernel_call(
        spread_kernel,
        "spread",
        [VMEM] * 7,
        [((384, 8 * CH), BF16), ((8, CH), F32), ((1, CLIPS), jnp.int32)],
        [pltpu.VMEM((27, 8, CH), F32)],
        flops=1 << 28,
    )(in_weight, clip_lengths, row(in_bias), row(norm1_gain), row(norm1_bias), row(norm2_gain), row(norm2_bias))
    onward = [(source, source + 1) for source in range(NTM - 1)]
    before = lax.ppermute(arrived, "tm", onward)
    frames = lambda n: ((n, 8, 4, 16, CH), BF16)
    late, own, part = kernel_call(
        late_kernel,
        "late",
        [SMEM] + [VMEM] * 3,
        [frames(2), ((4, 64, 128), BF16), ((8, CH), F32)],
        [pltpu.VMEM((128, 384), BF16)],
    )(lengths, arrived, matrix, vectors)
    early, stats = kernel_call(
        early_kernel,
        "early",
        [SMEM] + [VMEM] * 5,
        [frames(4), ((NTM, 2, 128), F32)],
        [pltpu.VMEM((8, 64, 128), BF16), pltpu.VMEM((256, 384), BF16)],
    )(lengths, before, own, part, matrix, vectors)
    stats = lax.all_to_all(stats, "tm", split_axis=0, concat_axis=0, tiled=True)
    act = [pltpu.VMEM((4, 10, 6, 16, CH), BF16)] * 2
    norm = pltpu.VMEM((8, CH), F32)
    middle, tail, stats = kernel_call(
        conv1_kernel,
        "conv1",
        [SMEM] + [VMEM] * 5,
        [frames(4), frames(2), ((NTM, 2, 128), F32)],
        act + [norm],
        flops=1 << 31,
    )(lengths, early, late, stats, vectors, conv1_weight)
    lead = lax.ppermute(tail, "tm", onward)
    stats = lax.all_to_all(stats, "tm", split_axis=0, concat_axis=0, tiled=True)
    packed = kernel_call(
        conv2_kernel,
        "conv2",
        [SMEM] + [VMEM] * 9,
        [((256, 512), BF16)],
        act + [norm] + [pltpu.VMEM((2, 9, 5, 16, CH), BF16)] * 2 + [pltpu.VMEM((4, 32, 512), F32)],
        flops=1 << 31,
    )(lengths, counts, early, late, middle, lead, stats, vectors, conv2_weight, down_weight)
    returned = lax.all_to_all(packed, "dp", split_axis=0, concat_axis=0, tiled=True)
    return kernel_call(return_kernel, "place", [VMEM] * 2, [((1, 1, 32, 2048), BF16)])(counts, returned)


def solution(mesh):
    in_specs = (
        P("dp", "tm", None, None),
        P("tm", None, None),
        P("dp", None),
        P(),
        P(),
        P(),
        P(),
        P(),
        P(),
        P(),
        P(),
        P(),
    )
    out_specs = P("dp", "tm", None, None)
    return jax.shard_map(
        per_device, mesh=mesh, in_specs=in_specs, out_specs=out_specs, check_vma=False
    )
```

```python
import jax
import jax.numpy as jnp
from jax import lax
from jax.experimental import pallas as pl
from jax.experimental.pallas import tpu as pltpu
from jax.sharding import PartitionSpec as P


F32 = jnp.float32
BF16 = jnp.bfloat16
EPS = 1e-06
NDP = 32
NTM = 16
FT = 4
CLIPS = 4
CH = 128
AREA = 512
FRAME_N = AREA * 4
VMEM_LIMIT = 24 * 1024 * 1024


def iota(shape, dim):
    return lax.broadcasted_iota(jnp.int32, shape, dim)


def onehot(cond):
    return jnp.where(cond, 1.0, 0.0).astype(BF16)


def mm(a, b):
    return jnp.dot(a, b, preferred_element_type=F32)


def pick_lane(values, lane):
    return jnp.sum(jnp.where(iota(values.shape, 1) == lane, values, 0.0), axis=1, keepdims=True)


def pack_kernel(joined_ref, out_ref):
    station = lax.axis_index("dp")
    joined = joined_ref[...]
    table = joined[:, :NDP].astype(F32)
    sub, lane = iota((NDP, NDP), 0), iota((NDP, NDP), 1)
    row = jnp.sum(jnp.where(sub == station, table, 0.0), axis=0, keepdims=True)
    recv = jnp.sum(jnp.where(sub < station, table, 0.0), axis=0, keepdims=True)
    row8 = jnp.broadcast_to(row, (8, NDP))
    start = mm(row8.astype(BF16), onehot(sub < lane))[0:1]
    spread = (iota((256, NDP), 0) >> 3 == iota((256, NDP), 1)).astype(F32)
    count_i = jnp.sum(spread * row, axis=1, keepdims=True)
    start_i = jnp.sum(spread * start, axis=1, keepdims=True)
    recv_i = jnp.sum(spread * recv, axis=1, keepdims=True)
    i, m = iota((256, 128), 0), iota((256, 128), 1)
    slot = ((i >> 2) & 1).astype(F32)
    valid = slot < count_i
    unit = (m & 31).astype(F32)
    place = onehot((unit == start_i + slot) & (m >> 5 == (i & 3)) & valid)
    src, dst = iota((NDP + 192, 128), 0) - NDP, iota((NDP + 192, 128), 1)
    t = dst & 31
    wanted = 24 * (dst >> 5) - 3 + t
    inside = (t < 30) & (dst < 64) & (wanted >= 0) & (wanted < 48)
    rows = [mm(joined, onehot((src == 48 * q + wanted) & inside)).astype(BF16) for q in range(4)]
    packed = mm(place, jnp.concatenate(rows, axis=0))
    packed = jnp.where(m == 64, jnp.where(valid, recv_i + slot, 255.0), packed)
    out_ref[...] = packed.astype(BF16)


def spread_kernel(weight_ref, lengths_ref, *refs):
    vector_refs, (out_ref, vectors_ref, along_ref, taps_ref) = refs[:5], refs[5:]
    along_ref[...] = lengths_ref[...]
    for n, ref in enumerate(vector_refs):
        vectors_ref[n : n + 1, :] = ref[...]
    taps_ref[...] = jnp.zeros_like(taps_ref)
    for a in range(3):
        for b in range(3):
            for c in range(3):
                taps_ref[(a * 3 + b) * 3 + c, 0:3, :] = weight_ref[a, b, c].astype(F32)
    taps = taps_ref[...].reshape(27 * 8, CH).astype(BF16)
    r, j = iota((384, 1), 0), iota((1, 216), 1)
    dyi = (r >> 5) & 3
    row_key = jnp.where(dyi < 3, ((2 - (r >> 7)) * 3 + dyi) * 64 + (r & 31), -1000)
    tap, color = j >> 3, j & 7
    third = (tap * 43) >> 7
    col_key = jnp.where(color < 3, third * 64 + (tap - 3 * third) * 3 + color, -5000)
    diff = row_key - col_key
    for l in range(8):
        out_ref[:, l * CH : (l + 1) * CH] = mm(onehot(diff == 3 * l), taps).astype(BF16)


def clip_ends(lengths_ref):
    return [jnp.sum(lengths_ref[0:1, 0 : c + 1]) for c in range(CLIPS)]


def clip_of(ends, frame):
    ident = jnp.int32(0)
    begin = jnp.int32(0)
    for c in range(CLIPS - 1):
        past = frame >= ends[c]
        ident = jnp.where(past, jnp.int32(c + 1), ident)
        begin = jnp.where(past, ends[c], begin)
    return ident, begin


def group_sum(x):
    lane = iota(x.shape, 1)
    x = x + pltpu.roll(x, 127, 1)
    x = x + pltpu.roll(x, 126, 1)
    x = jnp.where(lane & 3 == 0, x, 0.0)
    x = x + pltpu.roll(x, 1, 1)
    return x + pltpu.roll(x, 2, 1)


def shift_k(tile, step):
    moved = pltpu.roll(tile, step % 8, 0)
    return jnp.where(iota(tile.shape, 0) == (0 if step == 1 else 7), 0.0, moved)


class Moments:
    def __init__(self):
        self.pivot = None

    def add(self, rows):
        if self.pivot is None:
            self.pivot = rows[0:1]
            self.first = self.second = jnp.zeros((8, CH), F32)
        off = rows - self.pivot
        square = off * off
        self.first = self.first + fold(off)
        self.second = self.second + fold(square)

    def done(self):
        first = jnp.sum(self.first, axis=0, keepdims=True)
        second = jnp.sum(self.second, axis=0, keepdims=True)
        return first + AREA * self.pivot, second - first * first * (1.0 / AREA)


def fold(rows):
    return tree([rows[n : n + 8] for n in range(0, rows.shape[0], 8)])


def exact_mm(rows, matrix):
    high = rows.astype(BF16).astype(F32)
    middle = (rows - high).astype(BF16).astype(F32)
    low = rows - high - middle
    parts = mm(jnp.concatenate([high, middle, low, low], axis=0).astype(BF16), matrix)
    return parts[0:8] + parts[8:16] + parts[16:24]


def put_stats(pairs, stat_ref):
    sums = jnp.concatenate([p[0] for p in pairs], axis=0)
    devs = jnp.concatenate([p[1] for p in pairs], axis=0)
    off = sums * (1.0 / AREA) - group_sum(sums) * (1.0 / FRAME_N)
    rows = jnp.concatenate([sums, devs + AREA * (off * off)], axis=0)
    narrow = exact_mm(rows, onehot(iota((CH, 128), 0) >> 2 == (iota((CH, 128), 1) & 31)))
    own = jnp.where(iota((8, 128), 0) & 3 == iota((8, 128), 1) >> 5, narrow, 0.0)
    stats = jnp.concatenate([jnp.sum(own[n : n + 4], axis=0, keepdims=True) for n in (0, 4)], axis=0)
    for j in range(NTM):
        stat_ref[j] = stats


def unpack_rows(arrived):
    lane64 = onehot(iota((8, 128), 1) == 64)
    pos = lax.dot_general(lane64, arrived, (((1,), (1,)), ((), ())), preferred_element_type=F32)[0:1]
    pos = pos.astype(jnp.int32)
    q = iota((1, 256), 1) & 3
    target = jnp.where(pos < 32, (pos >> 3) * 32 + q * 8 + (pos & 7), -1)
    return mm(onehot(iota((128, 256), 0) == target), arrived)


def frame_rows(arrived, x_ref, first):
    rows = unpack_rows(arrived)
    lane = iota((8, 128), 1)
    for f in range(FT):
        tiles = [rows[f * 32 + q * 8 : f * 32 + q * 8 + 8] for q in range(4)]
        above = [shift_k(tiles[3], 1)] + tiles[:3]
        below = tiles[1:] + [shift_k(tiles[0], -1)]
        out = []
        for q in range(4):
            for a, b, c in ((0, 32, 64), (96, 0, 32)):
                a, b, c = (
                    pltpu.roll(v, n, 1) if n else v for v, n in ((above[q], a), (tiles[q], b), (below[q], c))
                )
                out.append(jnp.where(lane < 32, a, jnp.where(lane < 64, b, c)))
        x_ref[first + f] = jnp.concatenate(out, axis=0).astype(BF16)


def base_frames(lengths_ref, x_ref, x_first, lhs_ref, matrix_ref, vectors_ref, base_ref, first):
    column = lax.axis_index("tm")
    ends = clip_ends(lengths_ref)
    count = base_ref.shape[0]
    for n in range(count):
        frame = column * FT - 2 + first + n
        unused, begin = clip_of(ends, frame)
        for lag in range(3):
            p = jnp.clip(jnp.maximum(frame - lag, begin) - (column * FT + x_first), 0, x_ref.shape[0] - 1)
            lhs_ref[n * 64 : (n + 1) * 64, lag * 128 : (lag + 1) * 128] = x_ref[p]
    bias = vectors_ref[0:1, :]
    moments = [Moments() for unused in range(count)]
    for pair in range(4):
        both = mm(lhs_ref[...], matrix_ref[:, pair * 256 : (pair + 1) * 256])
        for half in range(2):
            value = (both[:, half * CH : (half + 1) * CH] + bias).astype(BF16)
            for n in range(count):
                part = value[n * 64 : (n + 1) * 64]
                base_ref[n, pair * 2 + half] = part.reshape(4, 16, CH)
                if first + n >= 2:
                    moments[n].add(part.astype(F32))
    return [m.done() for m in moments if m.pivot is not None]


def late_kernel(lengths_ref, own_ref, matrix_ref, vectors_ref, base_ref, x_ref, part_ref, lhs_ref):
    frame_rows(own_ref[...], x_ref, 0)
    pairs = base_frames(lengths_ref, x_ref, 0, lhs_ref, matrix_ref, vectors_ref, base_ref, 4)
    part_ref[...] = jnp.concatenate([p[0] for p in pairs] * 2 + [p[1] for p in pairs] * 2, axis=0)


def early_kernel(
    lengths_ref, prev_ref, own_ref, part_ref, matrix_ref, vectors_ref, base_ref, stat_ref, x_ref, lhs_ref
):
    frame_rows(prev_ref[...], x_ref, 0)
    x_ref[FT:] = own_ref[...]
    pairs = base_frames(lengths_ref, x_ref, -FT, lhs_ref, matrix_ref, vectors_ref, base_ref, 0)
    pairs = pairs + [(part_ref[n : n + 1, :], part_ref[n + 4 : n + 5, :]) for n in range(2)]
    put_stats(pairs, stat_ref)


def clip_scales(stats_ref, lengths_ref, ends, gain, norm_ref):
    sums, devs = stats_ref[:, 0, :], stats_ref[:, 1, :]
    frame = iota((NTM, 128), 0) * FT + (iota((NTM, 128), 1) >> 5)
    inside = [frame < ends[0]] + [(frame >= ends[c - 1]) & (frame < ends[c]) for c in range(1, CLIPS)]
    size = [(lengths_ref[0:1, c : c + 1] * FRAME_N).astype(F32) for c in range(CLIPS)]

    def clip_mean(values):
        rows = [
            jnp.sum(jnp.where(inside[c], values[c], 0.0), axis=0, keepdims=True) / size[c] for c in range(CLIPS)
        ]
        rows = jnp.concatenate(rows, axis=0)
        rows = rows + pltpu.roll(rows, 32, 1)
        return rows + pltpu.roll(rows, 64, 1)

    means = clip_mean([sums] * CLIPS)
    offs = [sums * (1.0 / FRAME_N) - means[c : c + 1] for c in range(CLIPS)]
    scales = lax.rsqrt(clip_mean([devs + FRAME_N * (off * off) for off in offs]) + EPS)
    wide = exact_mm(jnp.concatenate([means, scales], axis=0), onehot(iota((128, CH), 0) == iota((128, CH), 1) >> 2))
    norm_ref[...] = jnp.where(iota((8, CH), 0) < CLIPS, wide, wide * (0.5 * gain))


def clip_norm(norm_ref, ident):
    return norm_ref[pl.ds(ident, 1), :], norm_ref[pl.ds(ident + CLIPS, 1), :]


def tree(parts):
    while len(parts) > 1:
        parts = [a + b for a, b in zip(parts[0::2], parts[1::2])]
    return parts[0]


def store_padded(places, l, tiles):
    column = []
    for h in range(2):
        own = [tiles[q][h] for q in range(4)]
        column.append([shift_k(own[3], 1)] + own + [shift_k(own[0], -1)])
    flat = [column[h][q] for q in range(6) for h in range(2)]
    padded = jnp.concatenate(flat, axis=0).astype(BF16).reshape(6, 16, CH)
    for act_ref, o in places:
        act_ref[o, l] = padded


def norm_frame(value_of, places, mean, scale, bias):
    zero = jnp.zeros((8, CH), F32)
    for l in range(8):
        v = (value_of(l).astype(F32).reshape(64, CH) - mean) * scale + bias
        v = v + v * jnp.tanh(v)
        tiles = [[v[q * 16 + h * 8 : q * 16 + h * 8 + 8] for h in range(2)] for q in range(4)]
        store_padded(places, l + 1, tiles)
        if l == 0:
            store_padded(places, 9, [[tiles[q][1], zero] for q in range(4)])
        if l == 7:
            store_padded(places, 0, [[zero, tiles[q][0]] for q in range(4)])


class Norm:
    def __init__(self, norm_ref, ends, column, bias):
        self.norm_ref, self.ends, self.column, self.bias = norm_ref, ends, column, 0.5 * bias

    def frame(self, ref, n, o, places):
        ident, unused = clip_of(self.ends, self.column * FT - 2 + o)
        mean, scale = clip_norm(self.norm_ref, ident)
        norm_frame(lambda l: ref[n, l], places, mean, scale, self.bias)

    def loop(self, ref, n, o, count, places):
        def step(i, carry):
            self.frame(ref, n + i, o + i, [(act_ref, first + i) for act_ref, first in places])
            return carry

        lax.fori_loop(0, count, step, 0)


def conv_frames(act_ref, weight_ref, picks):
    taps = [(z, r) for z in range(3) for r in range(3)]

    def rows(first):
        blocks = []
        for pick in picks:
            parts = [
                act_ref[pick[2 - z], first : first + 9 - first // 2, r : r + 4].reshape(-1, CH) for z, r in taps
            ]
            blocks.append(jnp.concatenate(parts, axis=1))
        return jnp.concatenate(blocks, axis=0)

    left, here, right = (jnp.concatenate([weight_ref[z, r, c] for z, r in taps], axis=0) for c in range(3))
    both = mm(rows(0), jnp.concatenate([left, here], axis=1))
    last = mm(rows(2), right)
    totals = []
    for n in range(len(picks)):
        at = n * 576
        totals.append(
            both[at : at + AREA, :CH] + both[at + 64 : at + 576, CH:] + last[n * AREA : (n + 1) * AREA]
        )
    return totals


def frame_picks(ends, column, o, first):
    frame = column * FT - 2 + o
    unused, begin = clip_of(ends, frame)
    return [
        jnp.clip(jnp.maximum(frame - lag, begin) - (column * FT - 2 + first), 0, o - first) for lag in range(3)
    ]


def conv_halves(norm, sources, low_ref, high_ref, weight_ref):
    (a, an), (b, bn), (c, cn) = sources
    norm.loop(a, an, 0, 2, [(low_ref, 0)])
    norm.loop(b, bn, 2, 2, [(low_ref, 2), (high_ref, 0)])
    picks = lambda o, first: frame_picks(norm.ends, norm.column, o, first)
    totals = conv_frames(low_ref, weight_ref, [picks(2, 0), picks(3, 0)])
    norm.frame(c, cn, 4, [(high_ref, 2)])
    norm.frame(c, cn + 1, 5, [(high_ref, 3)])
    yield 0, totals
    yield 2, conv_frames(high_ref, weight_ref, [picks(4, 2), picks(5, 2)])


def conv1_kernel(
    lengths_ref, early_ref, late_ref, stats_ref, vectors_ref, weight_ref,
    middle_ref, tail_ref, stat_ref, low_ref, high_ref, norm_ref,
):
    column = lax.axis_index("tm")
    ends = clip_ends(lengths_ref)
    clip_scales(stats_ref, lengths_ref, ends, vectors_ref[1:2, :], norm_ref)
    norm = Norm(norm_ref, ends, column, vectors_ref[2:3, :])
    pairs = []
    for first, totals in conv_halves(
        norm, [(early_ref, 0), (early_ref, 2), (late_ref, 0)], low_ref, high_ref, weight_ref
    ):
        for f, total in enumerate(totals, first):
            value = total.astype(BF16)
            middle_ref[f] = value.reshape(8, 4, 16, CH)
            if f >= 2:
                tail_ref[f - 2] = value.reshape(8, 4, 16, CH)
            moments = Moments()
            moments.add(value.astype(F32))
            pairs.append(moments.done())
    put_stats(pairs, stat_ref)


def conv2_kernel(
    lengths_ref, counts_ref, early_ref, late_ref, middle_ref, lead_ref, stats_ref, vectors_ref, weight_ref, down_ref,
    out_ref, low_ref, high_ref, norm_ref, resid_ref, later_ref, latent_ref,
):
    column = lax.axis_index("tm")
    station = lax.axis_index("dp")
    ends = clip_ends(lengths_ref)
    clip_scales(stats_ref, lengths_ref, ends, vectors_ref[3:4, :], norm_ref)
    norm = Norm(norm_ref, ends, column, vectors_ref[4:5, :])
    down = down_ref[...].reshape(9 * CH, CH)
    zero = jnp.zeros((8, CH), F32)

    def put(ref, f, l, tiles):
        flat = [tiles[q][h] for q in range(4) for h in range(2)]
        flat = flat + [shift_k(tiles[0][h], -1) for h in range(2)]
        ref[f, l] = jnp.concatenate(flat, axis=0).astype(BF16).reshape(5, 16, CH)

    for first, totals in conv_halves(
        norm, [(lead_ref, 0), (middle_ref, 0), (middle_ref, 2)], low_ref, high_ref, weight_ref
    ):
        half_ref, base_ref = (later_ref, late_ref) if first else (resid_ref, early_ref)
        for f, total in enumerate(totals):
            base = base_ref[f if first else f + 2]
            resid = base.astype(F32).reshape(AREA, CH) + total
            resid = resid.astype(BF16).astype(F32)
            for l in range(8):
                v = resid[l * 64 : (l + 1) * 64]
                tiles = [[v[q * 16 + h * 8 : q * 16 + h * 8 + 8] for h in range(2)] for q in range(4)]
                put(half_ref, f, l, tiles)
                if l == 0:
                    put(half_ref, f, 8, [[tiles[q][1], zero] for q in range(4)])
        taps = []
        for row in range(3):
            for col in range(3):
                parts = [
                    half_ref[f, 2 * j + col, 2 * par + row] for f in range(2) for j in range(4) for par in range(2)
                ]
                taps.append(jnp.concatenate(parts, axis=0))
        latent = mm(jnp.concatenate(taps, axis=1), down)
        for f in range(2):
            for j in range(4):
                for w in range(4):
                    at, to = f * 128 + j * 32 + w * 8, (first + f) * 8
                    latent_ref[w, to : to + 8, j * CH : (j + 1) * CH] = latent[at : at + 8]
    table = counts_ref[0].astype(F32).astype(BF16)
    loader, other = iota((256, NDP), 0) >> 3, iota((256, NDP), 1)
    count_i = pick_lane(mm(onehot(loader == other), table), station)
    start_i = pick_lane(mm(onehot(other < loader), table), station)
    i, m = iota((256, 128), 0), iota((256, 128), 1)
    slot = ((i >> 2) & 1).astype(F32)
    place = onehot(((m & 31).astype(F32) == start_i + slot) & (m >> 5 == (i & 3)) & (slot < count_i))
    out_ref[...] = mm(place, latent_ref[...].reshape(128, 512).astype(BF16)).astype(BF16)


def return_kernel(counts_ref, back_ref, out_ref):
    station = lax.axis_index("dp")
    table = counts_ref[0].astype(F32)
    sub, lane = iota((NDP, NDP), 0), iota((NDP, NDP), 1)
    row = jnp.sum(jnp.where(sub == station, table, 0.0), axis=0, keepdims=True)
    row8 = jnp.broadcast_to(row, (8, NDP)).astype(BF16)
    encoder, other = iota((NDP, 256), 1) >> 3, iota((NDP, 256), 0)
    count_i = mm(row8, onehot(encoder == other))[0:1]
    start_i = mm(row8, onehot(other < encoder))[0:1]
    r, i = iota((128, 256), 0), iota((128, 256), 1)
    slot = ((i >> 2) & 1).astype(F32)
    select = onehot(((r & 31).astype(F32) == start_i + slot) & (r >> 5 == (i & 3)) & (slot < count_i))
    units = mm(select, back_ref[...]).astype(BF16)
    for w in range(4):
        out_ref[0, 0, :, w * 512 : (w + 1) * 512] = units[w * 32 : (w + 1) * 32]


VMEM = pl.BlockSpec(memory_space=pltpu.VMEM)


def kernel_call(body, name, in_specs, outs, scratch=(), flops=0, bytes_accessed=1 << 20, limit=VMEM_LIMIT):
    outs = [jax.ShapeDtypeStruct(shape, dtype) for shape, dtype in outs]
    return pl.pallas_call(
        body,
        name=name,
        in_specs=in_specs,
        out_specs=[VMEM] * len(outs) if len(outs) > 1 else VMEM,
        out_shape=outs if len(outs) > 1 else outs[0],
        scratch_shapes=list(scratch),
        compiler_params=pltpu.CompilerParams(vmem_limit_bytes=limit),
        cost_estimate=pl.CostEstimate(flops=flops, bytes_accessed=bytes_accessed, transcendentals=0),
    )


def per_device(
    pixels,
    counts,
    clip_lengths,
    in_weight,
    in_bias,
    norm1_gain,
    norm1_bias,
    conv1_weight,
    norm2_gain,
    norm2_bias,
    conv2_weight,
    down_weight,
):
    row = lambda v: v.reshape(1, CH)
    joined = jnp.concatenate([counts[0].astype(BF16), pixels[0, 0]], axis=1)
    packed = kernel_call(pack_kernel, "pack", [VMEM], [((256, 128), BF16)])(joined)
    arrived = lax.all_to_all(packed, "dp", split_axis=0, concat_axis=0, tiled=True)
    matrix, vectors, lengths = kernel_call(
        spread_kernel,
        "spread",
        [VMEM] * 7,
        [((384, 8 * CH), BF16), ((8, CH), F32), ((1, CLIPS), jnp.int32)],
        [pltpu.VMEM((27, 8, CH), F32)],
        flops=1 << 28,
    )(in_weight, clip_lengths, row(in_bias), row(norm1_gain), row(norm1_bias), row(norm2_gain), row(norm2_bias))
    onward = [(source, source + 1) for source in range(NTM - 1)]
    before = lax.ppermute(arrived, "tm", onward)
    frames = lambda n: ((n, 8, 4, 16, CH), BF16)
    late, own, part = kernel_call(
        late_kernel,
        "late",
        [VMEM] * 4,
        [frames(2), ((4, 64, 128), BF16), ((8, CH), F32)],
        [pltpu.VMEM((128, 384), BF16)],
    )(lengths, arrived, matrix, vectors)
    early, stats = kernel_call(
        early_kernel,
        "early",
        [VMEM] * 6,
        [frames(4), ((NTM, 2, 128), F32)],
        [pltpu.VMEM((8, 64, 128), BF16), pltpu.VMEM((256, 384), BF16)],
    )(lengths, before, own, part, matrix, vectors)
    stats = lax.all_to_all(stats, "tm", split_axis=0, concat_axis=0, tiled=True)
    act = [pltpu.VMEM((4, 10, 6, 16, CH), BF16)] * 2
    norm = pltpu.VMEM((8, CH), F32)
    middle, tail, stats = kernel_call(
        conv1_kernel,
        "conv1",
        [VMEM] * 6,
        [frames(4), frames(2), ((NTM, 2, 128), F32)],
        act + [norm],
        flops=1 << 31,
    )(lengths, early, late, stats, vectors, conv1_weight)
    lead = lax.ppermute(tail, "tm", onward)
    stats = lax.all_to_all(stats, "tm", split_axis=0, concat_axis=0, tiled=True)
    packed = kernel_call(
        conv2_kernel,
        "conv2",
        [VMEM] * 10,
        [((256, 512), BF16)],
        act + [norm] + [pltpu.VMEM((2, 9, 5, 16, CH), BF16)] * 2 + [pltpu.VMEM((4, 32, 512), F32)],
        flops=1 << 31,
    )(lengths, counts, early, late, middle, lead, stats, vectors, conv2_weight, down_weight)
    returned = lax.all_to_all(packed, "dp", split_axis=0, concat_axis=0, tiled=True)
    return kernel_call(return_kernel, "place", [VMEM] * 2, [((1, 1, 32, 2048), BF16)])(counts, returned)


def solution(mesh):
    in_specs = (
        P("dp", "tm", None, None),
        P("tm", None, None),
        P("dp", None),
        P(),
        P(),
        P(),
        P(),
        P(),
        P(),
        P(),
        P(),
        P(),
    )
    out_specs = P("dp", "tm", None, None)
    return jax.shard_map(
        per_device, mesh=mesh, in_specs=in_specs, out_specs=out_specs, check_vma=False
    )
```

```python
import jax
import jax.numpy as jnp
from jax import lax
from jax.experimental import pallas as pl
from jax.experimental.pallas import tpu as pltpu
from jax.sharding import PartitionSpec as P


F32 = jnp.float32
BF16 = jnp.bfloat16
EPS = 1e-06
NDP = 32
NTM = 16
FT = 4
CLIPS = 4
CH = 128
AREA = 512
FRAME_N = AREA * 4
VMEM_LIMIT = 24 * 1024 * 1024


def iota(shape, dim):
    return lax.broadcasted_iota(jnp.int32, shape, dim)


def onehot(cond):
    return jnp.where(cond, 1.0, 0.0).astype(BF16)


def mm(a, b):
    return jnp.dot(a, b, preferred_element_type=F32)


def pick_lane(values, lane):
    return jnp.sum(jnp.where(iota(values.shape, 1) == lane, values, 0.0), axis=1, keepdims=True)


def pack_kernel(joined_ref, out_ref):
    station = lax.axis_index("dp")
    joined = joined_ref[...]
    table = joined[:, :NDP].astype(F32)
    sub, lane = iota((NDP, NDP), 0), iota((NDP, NDP), 1)
    row = jnp.sum(jnp.where(sub == station, table, 0.0), axis=0, keepdims=True)
    recv = jnp.sum(jnp.where(sub < station, table, 0.0), axis=0, keepdims=True)
    row8 = jnp.broadcast_to(row, (8, NDP))
    start = mm(row8.astype(BF16), onehot(sub < lane))[0:1]
    spread = (iota((128, NDP), 0) >> 2 == iota((128, NDP), 1)).astype(F32)
    count_i = jnp.sum(spread * row, axis=1, keepdims=True)
    start_i = jnp.sum(spread * start, axis=1, keepdims=True)
    recv_i = jnp.sum(spread * recv, axis=1, keepdims=True)
    i, m = iota((128, 64), 0), iota((128, 64), 1)
    slot = ((i >> 1) & 1).astype(F32)
    place = onehot(((m & 31).astype(F32) == start_i + slot) & (m >> 5 == (i & 1)) & (slot < count_i))
    src, dst = iota((NDP + 192, 128), 0) - NDP, iota((NDP + 192, 128), 1)
    t = dst & 31
    wanted = 24 * ((dst >> 5) & 1) - 3 + t
    inside = (t < 30) & (wanted >= 0) & (wanted < 48)
    wanted = wanted + 48 * (dst >> 6)
    rows = [mm(joined, onehot((src == 96 * qp + wanted) & inside)).astype(BF16) for qp in range(2)]
    packed = mm(place, jnp.concatenate(rows, axis=0))
    slot = ((iota((128, 128), 0) >> 1) & 1).astype(F32)
    packed = jnp.where(iota((128, 128), 1) == 30, jnp.where(slot < count_i, recv_i + slot, 255.0), packed)
    out_ref[...] = packed.reshape(NDP, 4, 128).astype(BF16)


def spread_kernel(weight_ref, lengths_ref, *refs):
    vector_refs, (out_ref, vectors_ref, along_ref, taps_ref) = refs[:5], refs[5:]
    along_ref[...] = lengths_ref[...]
    for n, ref in enumerate(vector_refs):
        vectors_ref[n : n + 1, :] = ref[...]
    taps_ref[...] = jnp.zeros_like(taps_ref)
    for a in range(3):
        for b in range(3):
            for c in range(3):
                taps_ref[(a * 3 + b) * 3 + c, 0:3, :] = weight_ref[a, b, c].astype(F32)
    taps = taps_ref[...].reshape(27 * 8, CH).astype(BF16)
    r, j = iota((384, 1), 0), iota((1, 216), 1)
    dyi = (r >> 5) & 3
    row_key = jnp.where(dyi < 3, ((2 - (r >> 7)) * 3 + dyi) * 64 + (r & 31), -1000)
    tap, color = j >> 3, j & 7
    third = (tap * 43) >> 7
    col_key = jnp.where(color < 3, third * 64 + (tap - 3 * third) * 3 + color, -5000)
    diff = row_key - col_key
    for l in range(8):
        out_ref[:, l * CH : (l + 1) * CH] = mm(onehot(diff == 3 * l), taps).astype(BF16)


def clip_ends(lengths_ref):
    return [jnp.sum(lengths_ref[0:1, 0 : c + 1]) for c in range(CLIPS)]


def clip_of(ends, frame):
    ident = jnp.int32(0)
    begin = jnp.int32(0)
    for c in range(CLIPS - 1):
        past = frame >= ends[c]
        ident = jnp.where(past, jnp.int32(c + 1), ident)
        begin = jnp.where(past, ends[c], begin)
    return ident, begin


def group_sum(x):
    lane = iota(x.shape, 1)
    x = x + pltpu.roll(x, 127, 1)
    x = x + pltpu.roll(x, 126, 1)
    x = jnp.where(lane & 3 == 0, x, 0.0)
    x = x + pltpu.roll(x, 1, 1)
    return x + pltpu.roll(x, 2, 1)


def shift_k(tile, step):
    moved = pltpu.roll(tile, step % 8, 0)
    return jnp.where(iota(tile.shape, 0) == (0 if step == 1 else 7), 0.0, moved)


class Moments:
    def __init__(self):
        self.pivot = None

    def add(self, rows):
        if self.pivot is None:
            self.pivot = rows[0:1]
            self.first = self.second = jnp.zeros((8, CH), F32)
        off = rows - self.pivot
        square = off * off
        self.first = self.first + fold(off)
        self.second = self.second + fold(square)

    def done(self):
        first = jnp.sum(self.first, axis=0, keepdims=True)
        second = jnp.sum(self.second, axis=0, keepdims=True)
        return first + AREA * self.pivot, second - first * first * (1.0 / AREA)


def fold(rows):
    return tree([rows[n : n + 8] for n in range(0, rows.shape[0], 8)])


def exact_mm(rows, matrix):
    high = rows.astype(BF16).astype(F32)
    middle = (rows - high).astype(BF16).astype(F32)
    low = rows - high - middle
    parts = mm(jnp.concatenate([high, middle, low, low], axis=0).astype(BF16), matrix)
    return parts[0:8] + parts[8:16] + parts[16:24]


def put_stats(pairs, stat_ref):
    sums = jnp.concatenate([p[0] for p in pairs], axis=0)
    devs = jnp.concatenate([p[1] for p in pairs], axis=0)
    off = sums * (1.0 / AREA) - group_sum(sums) * (1.0 / FRAME_N)
    rows = jnp.concatenate([sums, devs + AREA * (off * off)], axis=0)
    narrow = exact_mm(rows, onehot(iota((CH, 128), 0) >> 2 == (iota((CH, 128), 1) & 31)))
    own = jnp.where(iota((8, 128), 0) & 3 == iota((8, 128), 1) >> 5, narrow, 0.0)
    stats = jnp.concatenate([jnp.sum(own[n : n + 4], axis=0, keepdims=True) for n in (0, 4)], axis=0)
    for j in range(NTM):
        stat_ref[j] = stats


def unpack_rows(arrived):
    lane30 = onehot(iota((8, 128), 1) == 30)
    pos = lax.dot_general(lane30, arrived, (((1,), (1,)), ((), ())), preferred_element_type=F32)[0:1]
    pos = pos.astype(jnp.int32)
    qp = iota((1, 128), 1) & 1
    target = jnp.where(pos < 32, (pos >> 3) * 16 + qp * 8 + (pos & 7), -1)
    return mm(onehot(iota((64, 128), 0) == target), arrived)


def frame_rows(arrived, x_ref, first):
    rows = unpack_rows(arrived.reshape(128, 128))
    lane = iota((8, 128), 1)
    move = lambda tile, n: pltpu.roll(tile, n % 128, 1) if n % 128 else tile
    for f in range(FT):
        tiles = [(rows[f * 16 + (q >> 1) * 8 :][:8], 64 * (q & 1)) for q in range(4)]
        above = [(shift_k(tiles[3][0], 1), tiles[3][1])] + tiles[:3]
        below = tiles[1:] + [(shift_k(tiles[0][0], -1), tiles[0][1])]
        out = []
        for q in range(4):
            for h in range(2):
                a, b, c = (
                    move(tile, to - at - 32 * h)
                    for (tile, at), to in ((above[q], 0), (tiles[q], 32), (below[q], 64))
                )
                out.append(jnp.where(lane < 32, a, jnp.where(lane < 64, b, c)))
        x_ref[first + f] = jnp.concatenate(out, axis=0).astype(BF16)


def base_frames(lengths_ref, x_ref, x_first, lhs_ref, matrix_ref, vectors_ref, base_ref, first):
    column = lax.axis_index("tm")
    ends = clip_ends(lengths_ref)
    count = base_ref.shape[0]
    for n in range(count):
        frame = column * FT - 2 + first + n
        unused, begin = clip_of(ends, frame)
        for lag in range(3):
            p = jnp.clip(jnp.maximum(frame - lag, begin) - (column * FT + x_first), 0, x_ref.shape[0] - 1)
            lhs_ref[n * 64 : (n + 1) * 64, lag * 128 : (lag + 1) * 128] = x_ref[p]
    bias = vectors_ref[0:1, :]
    moments = [Moments() for unused in range(count)]
    for pair in range(4):
        both = mm(lhs_ref[...], matrix_ref[:, pair * 256 : (pair + 1) * 256])
        for half in range(2):
            value = (both[:, half * CH : (half + 1) * CH] + bias).astype(BF16)
            for n in range(count):
                part = value[n * 64 : (n + 1) * 64]
                base_ref[n, pair * 2 + half] = part.reshape(4, 16, CH)
                if first + n >= 2:
                    moments[n].add(part.astype(F32))
    return [m.done() for m in moments if m.pivot is not None]


def return_routes(counts_ref, place_ref, select_ref):
    station = lax.axis_index("dp")
    table = counts_ref[0].astype(F32)
    narrow = table.astype(BF16)
    loader, other = iota((256, NDP), 0) >> 3, iota((256, NDP), 1)
    count_i = pick_lane(mm(onehot(loader == other), narrow), station)
    start_i = pick_lane(mm(onehot(other < loader), narrow), station)
    i, m = iota((256, 128), 0), iota((256, 128), 1)
    slot = ((i >> 2) & 1).astype(F32)
    place_ref[...] = onehot(
        ((m & 31).astype(F32) == start_i + slot) & (m >> 5 == (i & 3)) & (slot < count_i)
    )
    row = jnp.sum(jnp.where(iota((NDP, NDP), 0) == station, table, 0.0), axis=0, keepdims=True)
    row8 = jnp.broadcast_to(row, (8, NDP)).astype(BF16)
    encoder, other = iota((NDP, 256), 1) >> 3, iota((NDP, 256), 0)
    count_i = mm(row8, onehot(encoder == other))[0:1]
    start_i = mm(row8, onehot(other < encoder))[0:1]
    r, i = iota((128, 256), 0), iota((128, 256), 1)
    slot = ((i >> 2) & 1).astype(F32)
    select_ref[...] = onehot(
        ((r & 31).astype(F32) == start_i + slot) & (r >> 5 == (i & 3)) & (slot < count_i)
    )


def late_kernel(
    lengths_ref, own_ref, matrix_ref, vectors_ref, counts_ref, base_ref, x_ref, part_ref, place_ref, select_ref, lhs_ref
):
    return_routes(counts_ref, place_ref, select_ref)
    frame_rows(own_ref[...], x_ref, 0)
    pairs = base_frames(lengths_ref, x_ref, 0, lhs_ref, matrix_ref, vectors_ref, base_ref, 4)
    part_ref[...] = jnp.concatenate([p[0] for p in pairs] * 2 + [p[1] for p in pairs] * 2, axis=0)


def early_kernel(
    lengths_ref, prev_ref, own_ref, part_ref, matrix_ref, vectors_ref, base_ref, stat_ref, x_ref, lhs_ref
):
    frame_rows(prev_ref[...], x_ref, 0)
    x_ref[FT:] = own_ref[...]
    pairs = base_frames(lengths_ref, x_ref, -FT, lhs_ref, matrix_ref, vectors_ref, base_ref, 0)
    pairs = pairs + [(part_ref[n : n + 1, :], part_ref[n + 4 : n + 5, :]) for n in range(2)]
    put_stats(pairs, stat_ref)


def clip_scales(stats_ref, lengths_ref, ends, gain, norm_ref):
    sums, devs = stats_ref[:, 0, :], stats_ref[:, 1, :]
    frame = iota((NTM, 128), 0) * FT + (iota((NTM, 128), 1) >> 5)
    inside = [frame < ends[0]] + [(frame >= ends[c - 1]) & (frame < ends[c]) for c in range(1, CLIPS)]
    size = [(lengths_ref[0:1, c : c + 1] * FRAME_N).astype(F32) for c in range(CLIPS)]

    def clip_mean(values):
        rows = [
            jnp.sum(jnp.where(inside[c], values[c], 0.0), axis=0, keepdims=True) / size[c] for c in range(CLIPS)
        ]
        rows = jnp.concatenate(rows, axis=0)
        rows = rows + pltpu.roll(rows, 32, 1)
        return rows + pltpu.roll(rows, 64, 1)

    means = clip_mean([sums] * CLIPS)
    offs = [sums * (1.0 / FRAME_N) - means[c : c + 1] for c in range(CLIPS)]
    scales = lax.rsqrt(clip_mean([devs + FRAME_N * (off * off) for off in offs]) + EPS)
    wide = exact_mm(jnp.concatenate([means, scales], axis=0), onehot(iota((128, CH), 0) == iota((128, CH), 1) >> 2))
    norm_ref[...] = jnp.where(iota((8, CH), 0) < CLIPS, wide, wide * (0.5 * gain))


def clip_norm(norm_ref, ident):
    return norm_ref[pl.ds(ident, 1), :], norm_ref[pl.ds(ident + CLIPS, 1), :]


def tree(parts):
    while len(parts) > 1:
        parts = [a + b for a, b in zip(parts[0::2], parts[1::2])]
    return parts[0]


def store_padded(places, l, tiles):
    column = []
    for h in range(2):
        own = [tiles[q][h] for q in range(4)]
        column.append([shift_k(own[3], 1)] + own + [shift_k(own[0], -1)])
    flat = [column[h][q] for q in range(6) for h in range(2)]
    padded = jnp.concatenate(flat, axis=0).astype(BF16).reshape(6, 16, CH)
    for act_ref, o in places:
        act_ref[o, l] = padded


def norm_frame(value_of, places, mean, scale, bias):
    zero = jnp.zeros((8, CH), F32)
    for l in range(8):
        v = (value_of(l).astype(F32).reshape(64, CH) - mean) * scale + bias
        v = v + v * jnp.tanh(v)
        tiles = [[v[q * 16 + h * 8 : q * 16 + h * 8 + 8] for h in range(2)] for q in range(4)]
        store_padded(places, l + 1, tiles)
        if l == 0:
            store_padded(places, 9, [[tiles[q][1], zero] for q in range(4)])
        if l == 7:
            store_padded(places, 0, [[zero, tiles[q][0]] for q in range(4)])


class Norm:
    def __init__(self, norm_ref, ends, column, bias):
        self.norm_ref, self.ends, self.column, self.bias = norm_ref, ends, column, 0.5 * bias

    def frame(self, ref, n, o, places):
        ident, unused = clip_of(self.ends, self.column * FT - 2 + o)
        mean, scale = clip_norm(self.norm_ref, ident)
        norm_frame(lambda l: ref[n, l], places, mean, scale, self.bias)

    def loop(self, ref, n, o, count, places):
        def step(i, carry):
            self.frame(ref, n + i, o + i, [(act_ref, first + i) for act_ref, first in places])
            return carry

        lax.fori_loop(0, count, step, 0, unroll=True)


def conv_frames(act_ref, weight_ref, picks):
    taps = [(z, r) for z in range(3) for r in range(3)]

    def rows(first):
        blocks = []
        for pick in picks:
            parts = [
                act_ref[pick[2 - z], first : first + 9 - first // 2, r : r + 4].reshape(-1, CH) for z, r in taps
            ]
            blocks.append(jnp.concatenate(parts, axis=1))
        return jnp.concatenate(blocks, axis=0)

    left, here, right = (jnp.concatenate([weight_ref[z, r, c] for z, r in taps], axis=0) for c in range(3))
    both = mm(rows(0), jnp.concatenate([left, here], axis=1))
    last = mm(rows(2), right)
    totals = []
    for n in range(len(picks)):
        at = n * 576
        totals.append(
            both[at : at + AREA, :CH] + both[at + 64 : at + 576, CH:] + last[n * AREA : (n + 1) * AREA]
        )
    return totals


def frame_picks(ends, column, o, first):
    frame = column * FT - 2 + o
    unused, begin = clip_of(ends, frame)
    return [
        jnp.clip(jnp.maximum(frame - lag, begin) - (column * FT - 2 + first), 0, o - first) for lag in range(3)
    ]


def conv_halves(norm, sources, low_ref, high_ref, weight_ref):
    (a, an), (b, bn), (c, cn) = sources
    norm.loop(a, an, 0, 2, [(low_ref, 0)])
    norm.loop(b, bn, 2, 2, [(low_ref, 2), (high_ref, 0)])
    picks = lambda o, first: frame_picks(norm.ends, norm.column, o, first)
    totals = conv_frames(low_ref, weight_ref, [picks(2, 0), picks(3, 0)])
    norm.frame(c, cn, 4, [(high_ref, 2)])
    norm.frame(c, cn + 1, 5, [(high_ref, 3)])
    yield 0, totals
    yield 2, conv_frames(high_ref, weight_ref, [picks(4, 2), picks(5, 2)])


def conv1_kernel(
    lengths_ref, early_ref, late_ref, stats_ref, vectors_ref, weight_ref,
    middle_ref, tail_ref, stat_ref, low_ref, high_ref, norm_ref,
):
    column = lax.axis_index("tm")
    ends = clip_ends(lengths_ref)
    clip_scales(stats_ref, lengths_ref, ends, vectors_ref[1:2, :], norm_ref)
    norm = Norm(norm_ref, ends, column, vectors_ref[2:3, :])
    pairs = []
    for first, totals in conv_halves(
        norm, [(early_ref, 0), (early_ref, 2), (late_ref, 0)], low_ref, high_ref, weight_ref
    ):
        for f, total in enumerate(totals, first):
            value = total.astype(BF16)
            middle_ref[f] = value.reshape(8, 4, 16, CH)
            if f >= 2:
                tail_ref[f - 2] = value.reshape(8, 4, 16, CH)
            moments = Moments()
            moments.add(value.astype(F32))
            pairs.append(moments.done())
    put_stats(pairs, stat_ref)


def conv2_kernel(
    lengths_ref, place_ref, early_ref, late_ref, middle_ref, lead_ref, stats_ref, vectors_ref, weight_ref, down_ref,
    out_ref, low_ref, high_ref, norm_ref, resid_ref, later_ref, latent_ref,
):
    column = lax.axis_index("tm")
    ends = clip_ends(lengths_ref)
    clip_scales(stats_ref, lengths_ref, ends, vectors_ref[3:4, :], norm_ref)
    norm = Norm(norm_ref, ends, column, vectors_ref[4:5, :])
    down = down_ref[...].reshape(9 * CH, CH)
    zero = jnp.zeros((8, CH), F32)

    def put(ref, f, l, tiles):
        flat = [tiles[q][h] for q in range(4) for h in range(2)]
        flat = flat + [shift_k(tiles[0][h], -1) for h in range(2)]
        ref[f, l] = jnp.concatenate(flat, axis=0).astype(BF16).reshape(5, 16, CH)

    for first, totals in conv_halves(
        norm, [(lead_ref, 0), (middle_ref, 0), (middle_ref, 2)], low_ref, high_ref, weight_ref
    ):
        half_ref, base_ref = (later_ref, late_ref) if first else (resid_ref, early_ref)
        for f, total in enumerate(totals):
            base = base_ref[f if first else f + 2]
            resid = base.astype(F32).reshape(AREA, CH) + total
            resid = resid.astype(BF16).astype(F32)
            for l in range(8):
                v = resid[l * 64 : (l + 1) * 64]
                tiles = [[v[q * 16 + h * 8 : q * 16 + h * 8 + 8] for h in range(2)] for q in range(4)]
                put(half_ref, f, l, tiles)
                if l == 0:
                    put(half_ref, f, 8, [[tiles[q][1], zero] for q in range(4)])
    taps = []
    for row in range(3):
        for col in range(3):
            parts = [
                half_ref[f, 2 * j + col, 2 * par + row]
                for half_ref in (resid_ref, later_ref)
                for f in range(2)
                for j in range(4)
                for par in range(2)
            ]
            taps.append(jnp.concatenate(parts, axis=0))
    latent = mm(jnp.concatenate(taps, axis=1), down)
    for f in range(FT):
        for j in range(4):
            for w in range(4):
                at = f * 128 + j * 32 + w * 8
                latent_ref[w, f * 8 : f * 8 + 8, j * CH : (j + 1) * CH] = latent[at : at + 8]
    out_ref[...] = mm(place_ref[...], latent_ref[...].reshape(128, 512).astype(BF16)).astype(BF16)


def return_kernel(select_ref, back_ref, out_ref):
    units = mm(select_ref[...], back_ref[...]).astype(BF16)
    for w in range(4):
        out_ref[0, 0, :, w * 512 : (w + 1) * 512] = units[w * 32 : (w + 1) * 32]


VMEM = pl.BlockSpec(memory_space=pltpu.VMEM)


def kernel_call(body, name, in_specs, outs, scratch=(), flops=0, bytes_accessed=1 << 20, limit=VMEM_LIMIT):
    outs = [jax.ShapeDtypeStruct(shape, dtype) for shape, dtype in outs]
    return pl.pallas_call(
        body,
        name=name,
        in_specs=in_specs,
        out_specs=[VMEM] * len(outs) if len(outs) > 1 else VMEM,
        out_shape=outs if len(outs) > 1 else outs[0],
        scratch_shapes=list(scratch),
        compiler_params=pltpu.CompilerParams(vmem_limit_bytes=limit),
        cost_estimate=pl.CostEstimate(flops=flops, bytes_accessed=bytes_accessed, transcendentals=0),
    )


def per_device(
    pixels,
    counts,
    clip_lengths,
    in_weight,
    in_bias,
    norm1_gain,
    norm1_bias,
    conv1_weight,
    norm2_gain,
    norm2_bias,
    conv2_weight,
    down_weight,
):
    row = lambda v: v.reshape(1, CH)
    joined = jnp.concatenate([counts[0].astype(BF16), pixels[0, 0]], axis=1)
    packed = kernel_call(pack_kernel, "pack", [VMEM], [((NDP, 4, 128), BF16)])(joined)
    arrived = lax.all_to_all(packed, "dp", split_axis=0, concat_axis=0, tiled=True)
    matrix, vectors, lengths = kernel_call(
        spread_kernel,
        "spread",
        [VMEM] * 7,
        [((384, 8 * CH), BF16), ((8, CH), F32), ((1, CLIPS), jnp.int32)],
        [pltpu.VMEM((27, 8, CH), F32)],
        flops=1 << 28,
    )(in_weight, clip_lengths, row(in_bias), row(norm1_gain), row(norm1_bias), row(norm2_gain), row(norm2_bias))
    onward = [(source, source + 1) for source in range(NTM - 1)]
    before = lax.ppermute(arrived, "tm", onward)
    frames = lambda n: ((n, 8, 4, 16, CH), BF16)
    late, own, part, place, select = kernel_call(
        late_kernel,
        "late",
        [VMEM] * 5,
        [frames(2), ((4, 64, 128), BF16), ((8, CH), F32), ((256, 128), BF16), ((128, 256), BF16)],
        [pltpu.VMEM((128, 384), BF16)],
    )(lengths, arrived, matrix, vectors, counts)
    early, stats = kernel_call(
        early_kernel,
        "early",
        [VMEM] * 6,
        [frames(4), ((NTM, 2, 128), F32)],
        [pltpu.VMEM((8, 64, 128), BF16), pltpu.VMEM((256, 384), BF16)],
    )(lengths, before, own, part, matrix, vectors)
    stats = lax.all_to_all(stats, "tm", split_axis=0, concat_axis=0, tiled=True)
    act = [pltpu.VMEM((4, 10, 6, 16, CH), BF16)] * 2
    norm = pltpu.VMEM((8, CH), F32)
    middle, tail, stats = kernel_call(
        conv1_kernel,
        "conv1",
        [VMEM] * 6,
        [frames(4), frames(2), ((NTM, 2, 128), F32)],
        act + [norm],
        flops=1 << 31,
    )(lengths, early, late, stats, vectors, conv1_weight)
    stats = lax.all_to_all(stats, "tm", split_axis=0, concat_axis=0, tiled=True)
    lead = lax.ppermute(tail, "tm", onward)
    packed = kernel_call(
        conv2_kernel,
        "conv2",
        [VMEM] * 10,
        [((256, 512), BF16)],
        act + [norm] + [pltpu.VMEM((2, 9, 5, 16, CH), BF16)] * 2 + [pltpu.VMEM((4, 32, 512), F32)],
        flops=1 << 31,
    )(lengths, place, early, late, middle, lead, stats, vectors, conv2_weight, down_weight)
    returned = lax.all_to_all(packed, "dp", split_axis=0, concat_axis=0, tiled=True)
    return kernel_call(return_kernel, "place", [VMEM] * 2, [((1, 1, 32, 2048), BF16)])(select, returned)


def solution(mesh):
    in_specs = (
        P("dp", "tm", None, None),
        P("tm", None, None),
        P("dp", None),
        P(),
        P(),
        P(),
        P(),
        P(),
        P(),
        P(),
        P(),
        P(),
    )
    out_specs = P("dp", "tm", None, None)
    return jax.shard_map(
        per_device, mesh=mesh, in_specs=in_specs, out_specs=out_specs, check_vma=False
    )
```

```python
import jax
import jax.numpy as jnp
from jax import lax
from jax.experimental import pallas as pl
from jax.experimental.pallas import tpu as pltpu
from jax.sharding import PartitionSpec as P


F32 = jnp.float32
BF16 = jnp.bfloat16
EPS = 1e-06
NDP = 32
NTM = 16
FT = 4
CLIPS = 4
CH = 128
AREA = 512
FRAME_N = AREA * 4
VMEM_LIMIT = 24 * 1024 * 1024


def iota(shape, dim):
    return lax.broadcasted_iota(jnp.int32, shape, dim)


def onehot(cond):
    return jnp.where(cond, 1.0, 0.0).astype(BF16)


def mm(a, b):
    return jnp.dot(a, b, preferred_element_type=F32)


def pick_lane(values, lane):
    return jnp.sum(jnp.where(iota(values.shape, 1) == lane, values, 0.0), axis=1, keepdims=True)


def pack_kernel(joined_ref, out_ref):
    station = lax.axis_index("dp")
    joined = joined_ref[...]
    table = joined[:, :NDP].astype(F32)
    sub, lane = iota((NDP, NDP), 0), iota((NDP, NDP), 1)
    row = jnp.sum(jnp.where(sub == station, table, 0.0), axis=0, keepdims=True)
    recv = jnp.sum(jnp.where(sub < station, table, 0.0), axis=0, keepdims=True)
    row8 = jnp.broadcast_to(row, (8, NDP))
    start = mm(row8.astype(BF16), onehot(sub < lane))[0:1]
    spread = (iota((128, NDP), 0) >> 2 == iota((128, NDP), 1)).astype(F32)
    count_i = jnp.sum(spread * row, axis=1, keepdims=True)
    start_i = jnp.sum(spread * start, axis=1, keepdims=True)
    recv_i = jnp.sum(spread * recv, axis=1, keepdims=True)
    i, m = iota((128, 64), 0), iota((128, 64), 1)
    slot = ((i >> 1) & 1).astype(F32)
    place = onehot(((m & 31).astype(F32) == start_i + slot) & (m >> 5 == (i & 1)) & (slot < count_i))
    src, dst = iota((NDP + 192, 128), 0) - NDP, iota((NDP + 192, 128), 1)
    t = dst & 31
    wanted = 24 * ((dst >> 5) & 1) - 3 + t
    inside = (t < 30) & (wanted >= 0) & (wanted < 48)
    wanted = wanted + 48 * (dst >> 6)
    rows = [mm(joined, onehot((src == 96 * qp + wanted) & inside)).astype(BF16) for qp in range(2)]
    packed = mm(place, jnp.concatenate(rows, axis=0))
    slot = ((iota((128, 128), 0) >> 1) & 1).astype(F32)
    packed = jnp.where(iota((128, 128), 1) == 30, jnp.where(slot < count_i, recv_i + slot, 255.0), packed)
    out_ref[...] = packed.reshape(NDP, 4, 128).astype(BF16)


def spread_kernel(weight_ref, lengths_ref, *refs):
    vector_refs, (out_ref, vectors_ref, along_ref, taps_ref) = refs[:5], refs[5:]
    along_ref[...] = lengths_ref[...]
    for n, ref in enumerate(vector_refs):
        vectors_ref[n : n + 1, :] = ref[...]
    taps_ref[...] = jnp.zeros_like(taps_ref)
    for a in range(3):
        for b in range(3):
            for c in range(3):
                taps_ref[(a * 3 + b) * 3 + c, 0:3, :] = weight_ref[a, b, c].astype(F32)
    taps = taps_ref[...].reshape(27 * 8, CH).astype(BF16)
    r, j = iota((384, 1), 0), iota((1, 216), 1)
    dyi = (r >> 5) & 3
    row_key = jnp.where(dyi < 3, ((2 - (r >> 7)) * 3 + dyi) * 64 + (r & 31), -1000)
    tap, color = j >> 3, j & 7
    third = (tap * 43) >> 7
    col_key = jnp.where(color < 3, third * 64 + (tap - 3 * third) * 3 + color, -5000)
    diff = row_key - col_key
    for l in range(8):
        out_ref[:, l * CH : (l + 1) * CH] = mm(onehot(diff == 3 * l), taps).astype(BF16)


def clip_ends(lengths_ref):
    return [jnp.sum(lengths_ref[0:1, 0 : c + 1]) for c in range(CLIPS)]


def clip_of(ends, frame):
    ident = jnp.int32(0)
    begin = jnp.int32(0)
    for c in range(CLIPS - 1):
        past = frame >= ends[c]
        ident = jnp.where(past, jnp.int32(c + 1), ident)
        begin = jnp.where(past, ends[c], begin)
    return ident, begin


def group_sum(x):
    lane = iota(x.shape, 1)
    x = x + pltpu.roll(x, 127, 1)
    x = x + pltpu.roll(x, 126, 1)
    x = jnp.where(lane & 3 == 0, x, 0.0)
    x = x + pltpu.roll(x, 1, 1)
    return x + pltpu.roll(x, 2, 1)


def shift_k(tile, step):
    moved = pltpu.roll(tile, step % 8, 0)
    return jnp.where(iota(tile.shape, 0) == (0 if step == 1 else 7), 0.0, moved)


class Moments:
    def __init__(self):
        self.pivot = None

    def add(self, rows):
        if self.pivot is None:
            self.pivot = rows[0:1]
            self.first = self.second = jnp.zeros((8, CH), F32)
        off = rows - self.pivot
        square = off * off
        self.first = self.first + fold(off)
        self.second = self.second + fold(square)

    def done(self):
        first = jnp.sum(self.first, axis=0, keepdims=True)
        second = jnp.sum(self.second, axis=0, keepdims=True)
        return first + AREA * self.pivot, second - first * first * (1.0 / AREA)


def fold(rows):
    return tree([rows[n : n + 8] for n in range(0, rows.shape[0], 8)])


def exact_mm(rows, matrix):
    high = rows.astype(BF16).astype(F32)
    middle = (rows - high).astype(BF16).astype(F32)
    low = rows - high - middle
    parts = mm(jnp.concatenate([high, middle, low, low], axis=0).astype(BF16), matrix)
    return parts[0:8] + parts[8:16] + parts[16:24]


def put_stats(pairs, stat_ref):
    sums = jnp.concatenate([p[0] for p in pairs], axis=0)
    devs = jnp.concatenate([p[1] for p in pairs], axis=0)
    off = sums * (1.0 / AREA) - group_sum(sums) * (1.0 / FRAME_N)
    rows = jnp.concatenate([sums, devs + AREA * (off * off)], axis=0)
    narrow = exact_mm(rows, onehot(iota((CH, 128), 0) >> 2 == (iota((CH, 128), 1) & 31)))
    own = jnp.where(iota((8, 128), 0) & 3 == iota((8, 128), 1) >> 5, narrow, 0.0)
    stats = jnp.concatenate([jnp.sum(own[n : n + 4], axis=0, keepdims=True) for n in (0, 4)], axis=0)
    for j in range(NTM):
        stat_ref[j] = stats


def unpack_rows(arrived):
    lane30 = onehot(iota((8, 128), 1) == 30)
    pos = lax.dot_general(lane30, arrived, (((1,), (1,)), ((), ())), preferred_element_type=F32)[0:1]
    pos = pos.astype(jnp.int32)
    qp = iota((1, 128), 1) & 1
    target = jnp.where(pos < 32, (pos >> 3) * 16 + qp * 8 + (pos & 7), -1)
    return mm(onehot(iota((64, 128), 0) == target), arrived)


def frame_rows(arrived, x_ref, first):
    rows = unpack_rows(arrived.reshape(128, 128))
    lane = iota((8, 128), 1)
    move = lambda tile, n: pltpu.roll(tile, n % 128, 1) if n % 128 else tile
    for f in range(FT):
        tiles = [(rows[f * 16 + (q >> 1) * 8 :][:8], 64 * (q & 1)) for q in range(4)]
        above = [(shift_k(tiles[3][0], 1), tiles[3][1])] + tiles[:3]
        below = tiles[1:] + [(shift_k(tiles[0][0], -1), tiles[0][1])]
        out = []
        for q in range(4):
            for h in range(2):
                a, b, c = (
                    move(tile, to - at - 32 * h)
                    for (tile, at), to in ((above[q], 0), (tiles[q], 32), (below[q], 64))
                )
                out.append(jnp.where(lane < 32, a, jnp.where(lane < 64, b, c)))
        x_ref[first + f] = jnp.concatenate(out, axis=0).astype(BF16)


def base_frames(lengths_ref, x_ref, x_first, lhs_ref, matrix_ref, vectors_ref, base_ref, first):
    column = lax.axis_index("tm")
    ends = clip_ends(lengths_ref)
    count = base_ref.shape[0]
    for n in range(count):
        frame = column * FT - 2 + first + n
        unused, begin = clip_of(ends, frame)
        for lag in range(3):
            p = jnp.clip(jnp.maximum(frame - lag, begin) - (column * FT + x_first), 0, x_ref.shape[0] - 1)
            lhs_ref[n * 64 : (n + 1) * 64, lag * 128 : (lag + 1) * 128] = x_ref[p]
    bias = vectors_ref[0:1, :]
    moments = [Moments() for unused in range(count)]
    for pair in range(4):
        both = mm(lhs_ref[...], matrix_ref[:, pair * 256 : (pair + 1) * 256])
        for half in range(2):
            value = (both[:, half * CH : (half + 1) * CH] + bias).astype(BF16)
            for n in range(count):
                part = value[n * 64 : (n + 1) * 64]
                base_ref[n, pair * 2 + half] = part.reshape(4, 16, CH)
                if first + n >= 2:
                    moments[n].add(part.astype(F32))
    return [m.done() for m in moments if m.pivot is not None]


def return_routes(counts_ref, place_ref, select_ref):
    station = lax.axis_index("dp")
    table = counts_ref[0].astype(F32)
    narrow = table.astype(BF16)
    loader, other = iota((256, NDP), 0) >> 3, iota((256, NDP), 1)
    count_i = pick_lane(mm(onehot(loader == other), narrow), station)
    start_i = pick_lane(mm(onehot(other < loader), narrow), station)
    i, m = iota((256, 128), 0), iota((256, 128), 1)
    slot = ((i >> 2) & 1).astype(F32)
    place_ref[...] = onehot(
        ((m & 31).astype(F32) == start_i + slot) & (m >> 5 == (i & 3)) & (slot < count_i)
    )
    row = jnp.sum(jnp.where(iota((NDP, NDP), 0) == station, table, 0.0), axis=0, keepdims=True)
    row8 = jnp.broadcast_to(row, (8, NDP)).astype(BF16)
    encoder, other = iota((NDP, 256), 1) >> 3, iota((NDP, 256), 0)
    count_i = mm(row8, onehot(encoder == other))[0:1]
    start_i = mm(row8, onehot(other < encoder))[0:1]
    r, i = iota((128, 256), 0), iota((128, 256), 1)
    slot = ((i >> 2) & 1).astype(F32)
    select_ref[...] = onehot(
        ((r & 31).astype(F32) == start_i + slot) & (r >> 5 == (i & 3)) & (slot < count_i)
    )


def late_kernel(
    lengths_ref, own_ref, matrix_ref, vectors_ref, counts_ref, base_ref, x_ref, part_ref, place_ref, select_ref, lhs_ref
):
    return_routes(counts_ref, place_ref, select_ref)
    frame_rows(own_ref[...], x_ref, 0)
    pairs = base_frames(lengths_ref, x_ref, 0, lhs_ref, matrix_ref, vectors_ref, base_ref, 4)
    part_ref[...] = jnp.concatenate([p[0] for p in pairs] * 2 + [p[1] for p in pairs] * 2, axis=0)


def early_kernel(
    lengths_ref, prev_ref, own_ref, part_ref, matrix_ref, vectors_ref, base_ref, stat_ref, x_ref, lhs_ref
):
    frame_rows(prev_ref[...], x_ref, 0)
    x_ref[FT:] = own_ref[...]
    pairs = base_frames(lengths_ref, x_ref, -FT, lhs_ref, matrix_ref, vectors_ref, base_ref, 0)
    pairs = pairs + [(part_ref[n : n + 1, :], part_ref[n + 4 : n + 5, :]) for n in range(2)]
    put_stats(pairs, stat_ref)


def clip_scales(stats_ref, lengths_ref, ends, gain, norm_ref):
    sums, devs = stats_ref[:, 0, :], stats_ref[:, 1, :]
    frame = iota((NTM, 128), 0) * FT + (iota((NTM, 128), 1) >> 5)
    inside = [frame < ends[0]] + [(frame >= ends[c - 1]) & (frame < ends[c]) for c in range(1, CLIPS)]
    size = [(lengths_ref[0:1, c : c + 1] * FRAME_N).astype(F32) for c in range(CLIPS)]

    def clip_mean(values):
        rows = [
            jnp.sum(jnp.where(inside[c], values[c], 0.0), axis=0, keepdims=True) / size[c] for c in range(CLIPS)
        ]
        rows = jnp.concatenate(rows, axis=0)
        rows = rows + pltpu.roll(rows, 32, 1)
        return rows + pltpu.roll(rows, 64, 1)

    means = clip_mean([sums] * CLIPS)
    offs = [sums * (1.0 / FRAME_N) - means[c : c + 1] for c in range(CLIPS)]
    scales = lax.rsqrt(clip_mean([devs + FRAME_N * (off * off) for off in offs]) + EPS)
    wide = exact_mm(jnp.concatenate([means, scales], axis=0), onehot(iota((128, CH), 0) == iota((128, CH), 1) >> 2))
    norm_ref[...] = jnp.where(iota((8, CH), 0) < CLIPS, wide, wide * (0.5 * gain))


def clip_norm(norm_ref, ident):
    return norm_ref[pl.ds(ident, 1), :], norm_ref[pl.ds(ident + CLIPS, 1), :]


def tree(parts):
    while len(parts) > 1:
        parts = [a + b for a, b in zip(parts[0::2], parts[1::2])]
    return parts[0]


def store_padded(places, l, tiles):
    column = []
    for h in range(2):
        own = [tiles[q][h] for q in range(4)]
        column.append([shift_k(own[3], 1)] + own + [shift_k(own[0], -1)])
    flat = [column[h][q] for q in range(6) for h in range(2)]
    padded = jnp.concatenate(flat, axis=0).astype(BF16).reshape(6, 16, CH)
    for act_ref, o in places:
        act_ref[o, l] = padded


def norm_frame(value_of, places, mean, scale, bias):
    zero = jnp.zeros((8, CH), F32)
    for l in range(8):
        v = (value_of(l).astype(F32).reshape(64, CH) - mean) * scale + bias
        v = v + v * jnp.tanh(v)
        tiles = [[v[q * 16 + h * 8 : q * 16 + h * 8 + 8] for h in range(2)] for q in range(4)]
        store_padded(places, l + 1, tiles)
        if l == 0:
            store_padded(places, 9, [[tiles[q][1], zero] for q in range(4)])
        if l == 7:
            store_padded(places, 0, [[zero, tiles[q][0]] for q in range(4)])


class Norm:
    def __init__(self, norm_ref, ends, column, bias):
        self.norm_ref, self.ends, self.column, self.bias = norm_ref, ends, column, 0.5 * bias

    def frame(self, ref, n, o, places):
        ident, unused = clip_of(self.ends, self.column * FT - 2 + o)
        mean, scale = clip_norm(self.norm_ref, ident)
        norm_frame(lambda l: ref[n, l], places, mean, scale, self.bias)

    def loop(self, ref, n, o, count, places):
        def step(i, carry):
            self.frame(ref, n + i, o + i, [(act_ref, first + i) for act_ref, first in places])
            return carry

        lax.fori_loop(0, count, step, 0, unroll=True)


def conv_frames(act_ref, weight_ref, picks):
    taps = [(z, r) for z in range(3) for r in range(3)]

    def rows(first):
        blocks = []
        for pick in picks:
            parts = [
                act_ref[pick[2 - z], first : first + 9 - first // 2, r : r + 4].reshape(-1, CH) for z, r in taps
            ]
            blocks.append(jnp.concatenate(parts, axis=1))
        return jnp.concatenate(blocks, axis=0)

    left, here, right = (jnp.concatenate([weight_ref[z, r, c] for z, r in taps], axis=0) for c in range(3))
    both = mm(rows(0), jnp.concatenate([left, here], axis=1))
    last = mm(rows(2), right)
    totals = []
    for n in range(len(picks)):
        at = n * 576
        totals.append(
            both[at : at + AREA, :CH] + both[at + 64 : at + 576, CH:] + last[n * AREA : (n + 1) * AREA]
        )
    return totals


def frame_picks(ends, column, o, first):
    frame = column * FT - 2 + o
    unused, begin = clip_of(ends, frame)
    return [
        jnp.clip(jnp.maximum(frame - lag, begin) - (column * FT - 2 + first), 0, o - first) for lag in range(3)
    ]


def conv_halves(norm, sources, low_ref, high_ref, weight_ref):
    (a, an), (b, bn), (c, cn) = sources
    norm.loop(a, an, 0, 2, [(low_ref, 0)])
    norm.loop(b, bn, 2, 2, [(low_ref, 2), (high_ref, 0)])
    picks = lambda o, first: frame_picks(norm.ends, norm.column, o, first)
    totals = conv_frames(low_ref, weight_ref, [picks(2, 0), picks(3, 0)])
    norm.frame(c, cn, 4, [(high_ref, 2)])
    norm.frame(c, cn + 1, 5, [(high_ref, 3)])
    yield 0, totals
    yield 2, conv_frames(high_ref, weight_ref, [picks(4, 2), picks(5, 2)])


def conv1_kernel(
    lengths_ref, early_ref, late_ref, stats_ref, vectors_ref, weight_ref,
    middle_ref, tail_ref, stat_ref, low_ref, high_ref, norm_ref,
):
    column = lax.axis_index("tm")
    ends = clip_ends(lengths_ref)
    clip_scales(stats_ref, lengths_ref, ends, vectors_ref[1:2, :], norm_ref)
    norm = Norm(norm_ref, ends, column, vectors_ref[2:3, :])
    pairs = []
    for first, totals in conv_halves(
        norm, [(early_ref, 0), (early_ref, 2), (late_ref, 0)], low_ref, high_ref, weight_ref
    ):
        for f, total in enumerate(totals, first):
            value = total.astype(BF16)
            middle_ref[f] = value.reshape(8, 4, 16, CH)
            if f >= 2:
                tail_ref[f - 2] = value.reshape(8, 4, 16, CH)
            moments = Moments()
            moments.add(value.astype(F32))
            pairs.append(moments.done())
    put_stats(pairs, stat_ref)


def beside_kernel(place_ref, tail_ref, out_ref):
    out_ref[...] = place_ref[...]


def conv2_kernel(
    lengths_ref, place_ref, early_ref, late_ref, middle_ref, lead_ref, stats_ref, vectors_ref, weight_ref, down_ref,
    out_ref, low_ref, high_ref, norm_ref, resid_ref, later_ref, latent_ref,
):
    column = lax.axis_index("tm")
    ends = clip_ends(lengths_ref)
    clip_scales(stats_ref, lengths_ref, ends, vectors_ref[3:4, :], norm_ref)
    norm = Norm(norm_ref, ends, column, vectors_ref[4:5, :])
    down = down_ref[...].reshape(9 * CH, CH)
    zero = jnp.zeros((8, CH), F32)

    def put(ref, f, l, tiles):
        flat = [tiles[q][h] for q in range(4) for h in range(2)]
        flat = flat + [shift_k(tiles[0][h], -1) for h in range(2)]
        ref[f, l] = jnp.concatenate(flat, axis=0).astype(BF16).reshape(5, 16, CH)

    for first, totals in conv_halves(
        norm, [(lead_ref, 0), (middle_ref, 0), (middle_ref, 2)], low_ref, high_ref, weight_ref
    ):
        half_ref, base_ref = (later_ref, late_ref) if first else (resid_ref, early_ref)
        for f, total in enumerate(totals):
            base = base_ref[f if first else f + 2]
            resid = base.astype(F32).reshape(AREA, CH) + total
            resid = resid.astype(BF16).astype(F32)
            for l in range(8):
                v = resid[l * 64 : (l + 1) * 64]
                tiles = [[v[q * 16 + h * 8 : q * 16 + h * 8 + 8] for h in range(2)] for q in range(4)]
                put(half_ref, f, l, tiles)
                if l == 0:
                    put(half_ref, f, 8, [[tiles[q][1], zero] for q in range(4)])
    taps = []
    for row in range(3):
        for col in range(3):
            parts = [
                half_ref[f, 2 * j + col, 2 * par + row]
                for half_ref in (resid_ref, later_ref)
                for f in range(2)
                for j in range(4)
                for par in range(2)
            ]
            taps.append(jnp.concatenate(parts, axis=0))
    latent = mm(jnp.concatenate(taps, axis=1), down)
    for f in range(FT):
        for j in range(4):
            for w in range(4):
                at = f * 128 + j * 32 + w * 8
                latent_ref[w, f * 8 : f * 8 + 8, j * CH : (j + 1) * CH] = latent[at : at + 8]
    out_ref[...] = mm(place_ref[...], latent_ref[...].reshape(128, 512).astype(BF16)).astype(BF16)


def return_kernel(select_ref, back_ref, out_ref):
    units = mm(select_ref[...], back_ref[...]).astype(BF16)
    for w in range(4):
        out_ref[0, 0, :, w * 512 : (w + 1) * 512] = units[w * 32 : (w + 1) * 32]


VMEM = pl.BlockSpec(memory_space=pltpu.VMEM)


def kernel_call(body, name, in_specs, outs, scratch=(), flops=0, bytes_accessed=1 << 20, limit=VMEM_LIMIT):
    outs = [jax.ShapeDtypeStruct(shape, dtype) for shape, dtype in outs]
    return pl.pallas_call(
        body,
        name=name,
        in_specs=in_specs,
        out_specs=[VMEM] * len(outs) if len(outs) > 1 else VMEM,
        out_shape=outs if len(outs) > 1 else outs[0],
        scratch_shapes=list(scratch),
        compiler_params=pltpu.CompilerParams(vmem_limit_bytes=limit),
        cost_estimate=pl.CostEstimate(flops=flops, bytes_accessed=bytes_accessed, transcendentals=0),
    )


def per_device(
    pixels,
    counts,
    clip_lengths,
    in_weight,
    in_bias,
    norm1_gain,
    norm1_bias,
    conv1_weight,
    norm2_gain,
    norm2_bias,
    conv2_weight,
    down_weight,
):
    row = lambda v: v.reshape(1, CH)
    joined = jnp.concatenate([counts[0].astype(BF16), pixels[0, 0]], axis=1)
    packed = kernel_call(pack_kernel, "pack", [VMEM], [((NDP, 4, 128), BF16)])(joined)
    arrived = lax.all_to_all(packed, "dp", split_axis=0, concat_axis=0, tiled=True)
    matrix, vectors, lengths = kernel_call(
        spread_kernel,
        "spread",
        [VMEM] * 7,
        [((384, 8 * CH), BF16), ((8, CH), F32), ((1, CLIPS), jnp.int32)],
        [pltpu.VMEM((27, 8, CH), F32)],
        flops=1 << 28,
    )(in_weight, clip_lengths, row(in_bias), row(norm1_gain), row(norm1_bias), row(norm2_gain), row(norm2_bias))
    onward = [(source, source + 1) for source in range(NTM - 1)]
    before = lax.ppermute(arrived, "tm", onward)
    frames = lambda n: ((n, 8, 4, 16, CH), BF16)
    late, own, part, place, select = kernel_call(
        late_kernel,
        "late",
        [VMEM] * 5,
        [frames(2), ((4, 64, 128), BF16), ((8, CH), F32), ((256, 128), BF16), ((128, 256), BF16)],
        [pltpu.VMEM((128, 384), BF16)],
    )(lengths, arrived, matrix, vectors, counts)
    early, stats = kernel_call(
        early_kernel,
        "early",
        [VMEM] * 6,
        [frames(4), ((NTM, 2, 128), F32)],
        [pltpu.VMEM((8, 64, 128), BF16), pltpu.VMEM((256, 384), BF16)],
    )(lengths, before, own, part, matrix, vectors)
    stats = lax.all_to_all(stats, "tm", split_axis=0, concat_axis=0, tiled=True)
    act = [pltpu.VMEM((4, 10, 6, 16, CH), BF16)] * 2
    norm = pltpu.VMEM((8, CH), F32)
    middle, tail, stats = kernel_call(
        conv1_kernel,
        "conv1",
        [VMEM] * 6,
        [frames(4), frames(2), ((NTM, 2, 128), F32)],
        act + [norm],
        flops=1 << 31,
    )(lengths, early, late, stats, vectors, conv1_weight)
    stats = lax.all_to_all(stats, "tm", split_axis=0, concat_axis=0, tiled=True)
    place = kernel_call(beside_kernel, "beside", [VMEM] * 2, [((256, 128), BF16)], flops=1 << 36)(place, tail)
    lead = lax.ppermute(tail, "tm", onward)
    packed = kernel_call(
        conv2_kernel,
        "conv2",
        [VMEM] * 10,
        [((256, 512), BF16)],
        act + [norm] + [pltpu.VMEM((2, 9, 5, 16, CH), BF16)] * 2 + [pltpu.VMEM((4, 32, 512), F32)],
        flops=1 << 31,
    )(lengths, place, early, late, middle, lead, stats, vectors, conv2_weight, down_weight)
    returned = lax.all_to_all(packed, "dp", split_axis=0, concat_axis=0, tiled=True)
    return kernel_call(return_kernel, "place", [VMEM] * 2, [((1, 1, 32, 2048), BF16)])(select, returned)


def solution(mesh):
    in_specs = (
        P("dp", "tm", None, None),
        P("tm", None, None),
        P("dp", None),
        P(),
        P(),
        P(),
        P(),
        P(),
        P(),
        P(),
        P(),
        P(),
    )
    out_specs = P("dp", "tm", None, None)
    return jax.shard_map(
        per_device, mesh=mesh, in_specs=in_specs, out_specs=out_specs, check_vma=False
    )
```

```python
import jax
import jax.numpy as jnp
from jax import lax
from jax.experimental import pallas as pl
from jax.experimental.pallas import tpu as pltpu
from jax.sharding import PartitionSpec as P


F32 = jnp.float32
BF16 = jnp.bfloat16
EPS = 1e-06
NDP = 32
NTM = 16
FT = 4
CLIPS = 4
CH = 128
AREA = 512
FRAME_N = AREA * 4
VMEM_LIMIT = 24 * 1024 * 1024


def iota(shape, dim):
    return lax.broadcasted_iota(jnp.int32, shape, dim)


def onehot(cond):
    return jnp.where(cond, 1.0, 0.0).astype(BF16)


def mm(a, b):
    return jnp.dot(a, b, preferred_element_type=F32)


def pick_lane(values, lane):
    return jnp.sum(jnp.where(iota(values.shape, 1) == lane, values, 0.0), axis=1, keepdims=True)


def pack_kernel(counts_ref, pixels_ref, out_ref):
    station = lax.axis_index("dp")
    table = counts_ref[...].astype(F32)
    pixels = pixels_ref[0, 0]
    sub, lane = iota((NDP, NDP), 0), iota((NDP, NDP), 1)
    row = jnp.sum(jnp.where(sub == station, table, 0.0), axis=0, keepdims=True)
    recv = jnp.sum(jnp.where(sub < station, table, 0.0), axis=0, keepdims=True)
    row8 = jnp.broadcast_to(row, (8, NDP))
    start = mm(row8.astype(BF16), onehot(sub < lane))[0:1]
    spread = (iota((128, NDP), 0) >> 2 == iota((128, NDP), 1)).astype(F32)
    count_i = jnp.sum(spread * row, axis=1, keepdims=True)
    start_i = jnp.sum(spread * start, axis=1, keepdims=True)
    recv_i = jnp.sum(spread * recv, axis=1, keepdims=True)
    i, m = iota((128, 64), 0), iota((128, 64), 1)
    slot = ((i >> 1) & 1).astype(F32)
    place = onehot(((m & 31).astype(F32) == start_i + slot) & (m >> 5 == (i & 1)) & (slot < count_i))
    src, dst = iota((192, 128), 0), iota((192, 128), 1)
    t = dst & 31
    wanted = 24 * ((dst >> 5) & 1) - 3 + t
    inside = (t < 30) & (wanted >= 0) & (wanted < 48)
    wanted = wanted + 48 * (dst >> 6)
    rows = [mm(pixels, onehot((src == 96 * qp + wanted) & inside)).astype(BF16) for qp in range(2)]
    packed = mm(place, jnp.concatenate(rows, axis=0))
    slot = ((iota((128, 128), 0) >> 1) & 1).astype(F32)
    packed = jnp.where(iota((128, 128), 1) == 30, jnp.where(slot < count_i, recv_i + slot, 255.0), packed)
    out_ref[...] = packed.reshape(NDP, 4, 128).astype(BF16)


def spread_kernel(weight_ref, lengths_ref, *refs):
    vector_refs, (out_ref, vectors_ref, along_ref, taps_ref) = refs[:5], refs[5:]
    along_ref[...] = lengths_ref[...]
    for n, ref in enumerate(vector_refs):
        vectors_ref[n : n + 1, :] = ref[...]
    taps_ref[...] = jnp.zeros_like(taps_ref)
    for a in range(3):
        for b in range(3):
            for c in range(3):
                taps_ref[(a * 3 + b) * 3 + c, 0:3, :] = weight_ref[a, b, c].astype(F32)
    taps = taps_ref[...].reshape(27 * 8, CH).astype(BF16)
    r, j = iota((384, 1), 0), iota((1, 216), 1)
    dyi = (r >> 5) & 3
    row_key = jnp.where(dyi < 3, ((2 - (r >> 7)) * 3 + dyi) * 64 + (r & 31), -1000)
    tap, color = j >> 3, j & 7
    third = (tap * 43) >> 7
    col_key = jnp.where(color < 3, third * 64 + (tap - 3 * third) * 3 + color, -5000)
    diff = row_key - col_key
    for l in range(8):
        out_ref[:, l * CH : (l + 1) * CH] = mm(onehot(diff == 3 * l), taps).astype(BF16)


def clip_ends(lengths_ref):
    return [jnp.sum(lengths_ref[0:1, 0 : c + 1]) for c in range(CLIPS)]


def clip_of(ends, frame):
    ident = jnp.int32(0)
    begin = jnp.int32(0)
    for c in range(CLIPS - 1):
        past = frame >= ends[c]
        ident = jnp.where(past, jnp.int32(c + 1), ident)
        begin = jnp.where(past, ends[c], begin)
    return ident, begin


def group_sum(x):
    lane = iota(x.shape, 1)
    for n in (1, 2):
        x = x + jnp.where(lane & n == 0, pltpu.roll(x, 128 - n, 1), pltpu.roll(x, n, 1))
    return x


def shift_k(tile, step):
    moved = pltpu.roll(tile, step % 8, 0)
    return jnp.where(iota(tile.shape, 0) == (0 if step == 1 else 7), 0.0, moved)


class Moments:
    def __init__(self):
        self.pivot = None

    def add(self, rows):
        if self.pivot is None:
            self.pivot = rows[0:1]
            self.first = self.second = jnp.zeros((8, CH), F32)
        off = rows - self.pivot
        square = off * off
        self.first = self.first + fold(off)
        self.second = self.second + fold(square)

    def done(self):
        first = jnp.sum(self.first, axis=0, keepdims=True)
        second = jnp.sum(self.second, axis=0, keepdims=True)
        return first + AREA * self.pivot, second - first * first * (1.0 / AREA)


def fold(rows):
    return tree([rows[n : n + 8] for n in range(0, rows.shape[0], 8)])


def exact_mm(rows, matrix):
    high = rows.astype(BF16).astype(F32)
    middle = (rows - high).astype(BF16).astype(F32)
    low = rows - high - middle
    parts = mm(jnp.concatenate([high, middle, low, low], axis=0).astype(BF16), matrix)
    return parts[0:8] + parts[8:16] + parts[16:24]


def put_stats(pairs, stat_ref):
    sums = jnp.concatenate([p[0] for p in pairs], axis=0)
    devs = jnp.concatenate([p[1] for p in pairs], axis=0)
    off = sums * (1.0 / AREA) - group_sum(sums) * (1.0 / FRAME_N)
    rows = jnp.concatenate([sums, devs + AREA * (off * off)], axis=0)
    narrow = exact_mm(rows, onehot(iota((CH, 128), 0) >> 2 == (iota((CH, 128), 1) & 31)))
    own = jnp.where(iota((8, 128), 0) & 3 == iota((8, 128), 1) >> 5, narrow, 0.0)
    stats = jnp.concatenate([jnp.sum(own[n : n + 4], axis=0, keepdims=True) for n in (0, 4)], axis=0)
    for j in range(NTM):
        stat_ref[j] = stats


def unpack_rows(arrived):
    lane30 = onehot(iota((8, 128), 1) == 30)
    pos = lax.dot_general(lane30, arrived, (((1,), (1,)), ((), ())), preferred_element_type=F32)[0:1]
    pos = pos.astype(jnp.int32)
    qp = iota((1, 128), 1) & 1
    target = jnp.where(pos < 32, (pos >> 3) * 16 + qp * 8 + (pos & 7), -1)
    return mm(onehot(iota((64, 128), 0) == target), arrived)


def frame_rows(arrived, x_ref, first):
    rows = unpack_rows(arrived.reshape(128, 128))
    lane = iota((8, 128), 1)
    move = lambda tile, n: pltpu.roll(tile, n % 128, 1) if n % 128 else tile
    for f in range(FT):
        tiles = [(rows[f * 16 + (q >> 1) * 8 :][:8], 64 * (q & 1)) for q in range(4)]
        above = [(shift_k(tiles[3][0], 1), tiles[3][1])] + tiles[:3]
        below = tiles[1:] + [(shift_k(tiles[0][0], -1), tiles[0][1])]
        out = []
        for q in range(4):
            for h in range(2):
                a, b, c = (
                    move(tile, to - at - 32 * h)
                    for (tile, at), to in ((above[q], 0), (tiles[q], 32), (below[q], 64))
                )
                out.append(jnp.where(lane < 32, a, jnp.where(lane < 64, b, c)))
        x_ref[first + f] = jnp.concatenate(out, axis=0).astype(BF16)


def base_frames(lengths_ref, x_ref, x_first, lhs_ref, matrix_ref, vectors_ref, base_ref, first):
    column = lax.axis_index("tm")
    ends = clip_ends(lengths_ref)
    count = base_ref.shape[0]
    for n in range(count):
        frame = column * FT - 2 + first + n
        unused, begin = clip_of(ends, frame)
        for lag in range(3):
            p = jnp.clip(jnp.maximum(frame - lag, begin) - (column * FT + x_first), 0, x_ref.shape[0] - 1)
            lhs_ref[n * 64 : (n + 1) * 64, lag * 128 : (lag + 1) * 128] = x_ref[p]
    bias = vectors_ref[0:1, :]
    moments = [Moments() for unused in range(count)]
    for pair in range(4):
        both = mm(lhs_ref[...], matrix_ref[:, pair * 256 : (pair + 1) * 256])
        for half in range(2):
            value = (both[:, half * CH : (half + 1) * CH] + bias).astype(BF16)
            for n in range(count):
                part = value[n * 64 : (n + 1) * 64]
                base_ref[n, pair * 2 + half] = part.reshape(4, 16, CH)
                if first + n >= 2:
                    moments[n].add(part.astype(F32))
    return [m.done() for m in moments if m.pivot is not None]


def return_routes(counts_ref, place_ref, select_ref):
    station = lax.axis_index("dp")
    table = counts_ref[0].astype(F32)
    narrow = table.astype(BF16)
    loader, other = iota((64, NDP), 0) >> 1, iota((64, NDP), 1)
    count_i = pick_lane(mm(onehot(loader == other), narrow), station)
    start_i = pick_lane(mm(onehot(other < loader), narrow), station)
    slot = (iota((64, NDP), 0) & 1).astype(F32)
    place_ref[...] = onehot((other.astype(F32) == start_i + slot) & (slot < count_i))
    row = jnp.sum(jnp.where(iota((NDP, NDP), 0) == station, table, 0.0), axis=0, keepdims=True)
    row8 = jnp.broadcast_to(row, (8, NDP)).astype(BF16)
    encoder, other = iota((NDP, 64), 1) >> 1, iota((NDP, 64), 0)
    count_i = mm(row8, onehot(encoder == other))[0:1]
    start_i = mm(row8, onehot(other < encoder))[0:1]
    slot = (iota((NDP, 64), 1) & 1).astype(F32)
    select_ref[...] = onehot((other.astype(F32) == start_i + slot) & (slot < count_i))


def late_kernel(
    lengths_ref, own_ref, matrix_ref, vectors_ref, counts_ref, base_ref, x_ref, part_ref, place_ref, select_ref, lhs_ref
):
    return_routes(counts_ref, place_ref, select_ref)
    frame_rows(own_ref[...], x_ref, 0)
    pairs = base_frames(lengths_ref, x_ref, 0, lhs_ref, matrix_ref, vectors_ref, base_ref, 4)
    part_ref[...] = jnp.concatenate([p[0] for p in pairs] * 2 + [p[1] for p in pairs] * 2, axis=0)


def early_kernel(
    lengths_ref, prev_ref, own_ref, part_ref, matrix_ref, vectors_ref, base_ref, stat_ref, x_ref, lhs_ref
):
    frame_rows(prev_ref[...], x_ref, 0)
    x_ref[FT:] = own_ref[...]
    pairs = base_frames(lengths_ref, x_ref, -FT, lhs_ref, matrix_ref, vectors_ref, base_ref, 0)
    pairs = pairs + [(part_ref[n : n + 1, :], part_ref[n + 4 : n + 5, :]) for n in range(2)]
    put_stats(pairs, stat_ref)


def clip_scales(stats_ref, lengths_ref, ends, gain, norm_ref):
    sums, devs = stats_ref[:, 0, :], stats_ref[:, 1, :]
    frame = iota((NTM, 128), 0) * FT + (iota((NTM, 128), 1) >> 5)
    inside = [frame < ends[0]] + [(frame >= ends[c - 1]) & (frame < ends[c]) for c in range(1, CLIPS)]
    size = [(lengths_ref[0:1, c : c + 1] * FRAME_N).astype(F32) for c in range(CLIPS)]

    def clip_rows(values):
        rows = [
            jnp.sum(jnp.where(inside[c], values[c], 0.0), axis=0, keepdims=True) / size[c] for c in range(CLIPS)
        ]
        return jnp.concatenate(rows, axis=0)

    parts = clip_rows([sums] * CLIPS)
    means = parts + pltpu.roll(parts, 32, 1)
    means = means + pltpu.roll(means, 64, 1)
    offs = [sums * (1.0 / FRAME_N) - means[c : c + 1] for c in range(CLIPS)]
    rows = jnp.concatenate([parts, clip_rows([devs + FRAME_N * (off * off) for off in offs])], axis=0)
    wide = exact_mm(rows, onehot(iota((128, CH), 0) & 31 == iota((128, CH), 1) >> 2))
    norm_ref[...] = jnp.where(iota((8, CH), 0) < CLIPS, wide, lax.rsqrt(wide + EPS) * (0.5 * gain))


def clip_norm(norm_ref, ident):
    return norm_ref[pl.ds(ident, 1), :], norm_ref[pl.ds(ident + CLIPS, 1), :]


def tree(parts):
    while len(parts) > 1:
        parts = [a + b for a, b in zip(parts[0::2], parts[1::2])]
    return parts[0]


def store_padded(places, l, tiles):
    column = []
    for h in range(2):
        own = [tiles[q][h] for q in range(4)]
        column.append([shift_k(own[3], 1)] + own + [shift_k(own[0], -1)])
    flat = [column[h][q] for q in range(6) for h in range(2)]
    padded = jnp.concatenate(flat, axis=0).astype(BF16).reshape(6, 16, CH)
    for act_ref, o in places:
        act_ref[o, l] = padded


def norm_frame(value_of, places, mean, scale, bias):
    zero = jnp.zeros((8, CH), F32)
    for l in range(8):
        v = (value_of(l).astype(F32).reshape(64, CH) - mean) * scale + bias
        v = v + v * jnp.tanh(v)
        tiles = [[v[q * 16 + h * 8 : q * 16 + h * 8 + 8] for h in range(2)] for q in range(4)]
        store_padded(places, l + 1, tiles)
        if l == 0:
            store_padded(places, 9, [[tiles[q][1], zero] for q in range(4)])
        if l == 7:
            store_padded(places, 0, [[zero, tiles[q][0]] for q in range(4)])


class Norm:
    def __init__(self, norm_ref, ends, column, bias):
        self.norm_ref, self.ends, self.column, self.bias = norm_ref, ends, column, 0.5 * bias

    def frame(self, ref, n, o, places):
        ident, unused = clip_of(self.ends, self.column * FT - 2 + o)
        mean, scale = clip_norm(self.norm_ref, ident)
        norm_frame(lambda l: ref[n, l], places, mean, scale, self.bias)

    def loop(self, ref, n, o, count, places):
        def step(i, carry):
            self.frame(ref, n + i, o + i, [(act_ref, first + i) for act_ref, first in places])
            return carry

        lax.fori_loop(0, count, step, 0, unroll=True)


def conv_frames(act_ref, weight_ref, picks):
    taps = [(z, r) for z in range(3) for r in range(3)]

    def rows(first):
        blocks = []
        for pick in picks:
            parts = [
                act_ref[pick[2 - z], first : first + 9 - first // 2, r : r + 4].reshape(-1, CH) for z, r in taps
            ]
            blocks.append(jnp.concatenate(parts, axis=1))
        return jnp.concatenate(blocks, axis=0)

    left, here, right = (jnp.concatenate([weight_ref[z, r, c] for z, r in taps], axis=0) for c in range(3))
    both = mm(rows(0), jnp.concatenate([left, here], axis=1))
    last = mm(rows(2), right)
    totals = []
    for n in range(len(picks)):
        at = n * 576
        totals.append(
            both[at : at + AREA, :CH] + both[at + 64 : at + 576, CH:] + last[n * AREA : (n + 1) * AREA]
        )
    return totals


def frame_picks(ends, column, o, first):
    frame = column * FT - 2 + o
    unused, begin = clip_of(ends, frame)
    return [
        jnp.clip(jnp.maximum(frame - lag, begin) - (column * FT - 2 + first), 0, o - first) for lag in range(3)
    ]


def conv_halves(norm, sources, low_ref, high_ref, weight_ref):
    (a, an), (b, bn), (c, cn) = sources
    norm.loop(a, an, 0, 2, [(low_ref, 0)])
    norm.loop(b, bn, 2, 2, [(low_ref, 2), (high_ref, 0)])
    picks = lambda o, first: frame_picks(norm.ends, norm.column, o, first)
    totals = conv_frames(low_ref, weight_ref, [picks(2, 0), picks(3, 0)])
    norm.frame(c, cn, 4, [(high_ref, 2)])
    norm.frame(c, cn + 1, 5, [(high_ref, 3)])
    yield 0, totals
    yield 2, conv_frames(high_ref, weight_ref, [picks(4, 2), picks(5, 2)])


def conv1_kernel(
    lengths_ref, early_ref, late_ref, stats_ref, vectors_ref, weight_ref,
    middle_ref, tail_ref, stat_ref, low_ref, high_ref, norm_ref,
):
    column = lax.axis_index("tm")
    ends = clip_ends(lengths_ref)
    clip_scales(stats_ref, lengths_ref, ends, vectors_ref[1:2, :], norm_ref)
    norm = Norm(norm_ref, ends, column, vectors_ref[2:3, :])
    pairs = []
    for first, totals in conv_halves(
        norm, [(early_ref, 0), (early_ref, 2), (late_ref, 0)], low_ref, high_ref, weight_ref
    ):
        for f, total in enumerate(totals, first):
            value = total.astype(BF16)
            middle_ref[f] = value.reshape(8, 4, 16, CH)
            if f >= 2:
                tail_ref[f - 2] = value.reshape(8, 4, 16, CH)
            moments = Moments()
            moments.add(value.astype(F32))
            pairs.append(moments.done())
    put_stats(pairs, stat_ref)


def beside_kernel(place_ref, tail_ref, out_ref):
    out_ref[...] = place_ref[...]


def conv2_kernel(
    lengths_ref, place_ref, early_ref, late_ref, middle_ref, lead_ref, stats_ref, vectors_ref, weight_ref, down_ref,
    out_ref, low_ref, high_ref, norm_ref, resid_ref, later_ref, latent_ref,
):
    column = lax.axis_index("tm")
    ends = clip_ends(lengths_ref)
    clip_scales(stats_ref, lengths_ref, ends, vectors_ref[3:4, :], norm_ref)
    norm = Norm(norm_ref, ends, column, vectors_ref[4:5, :])
    down = down_ref[...].reshape(9 * CH, CH)
    zero = jnp.zeros((8, CH), F32)

    def put(ref, f, l, tiles):
        flat = [tiles[q][h] for q in range(4) for h in range(2)]
        flat = flat + [shift_k(tiles[0][h], -1) for h in range(2)]
        ref[f, l] = jnp.concatenate(flat, axis=0).astype(BF16).reshape(5, 16, CH)

    for first, totals in conv_halves(
        norm, [(lead_ref, 0), (middle_ref, 0), (middle_ref, 2)], low_ref, high_ref, weight_ref
    ):
        half_ref, base_ref = (later_ref, late_ref) if first else (resid_ref, early_ref)
        for f, total in enumerate(totals):
            base = base_ref[f if first else f + 2]
            resid = base.astype(F32).reshape(AREA, CH) + total
            resid = resid.astype(BF16).astype(F32)
            for l in range(8):
                v = resid[l * 64 : (l + 1) * 64]
                tiles = [[v[q * 16 + h * 8 : q * 16 + h * 8 + 8] for h in range(2)] for q in range(4)]
                put(half_ref, f, l, tiles)
                if l == 0:
                    put(half_ref, f, 8, [[tiles[q][1], zero] for q in range(4)])
    taps = []
    for row in range(3):
        for col in range(3):
            parts = [
                half_ref[f, 2 * j + col, 2 * par + row]
                for half_ref in (resid_ref, later_ref)
                for f in range(2)
                for j in range(4)
                for par in range(2)
            ]
            taps.append(jnp.concatenate(parts, axis=0))
    latent = mm(jnp.concatenate(taps, axis=1), down)
    for f in range(FT):
        for j in range(4):
            for w in range(4):
                at = f * 128 + j * 32 + w * 8
                latent_ref[w, f * 8 : f * 8 + 8, j * CH : (j + 1) * CH] = latent[at : at + 8]
    for w in range(4):
        rows = mm(place_ref[...], latent_ref[w].astype(BF16))
        out_ref[:, :, w * 512 : (w + 1) * 512] = rows.reshape(NDP, 2, 512).astype(BF16)


def return_kernel(select_ref, back_ref, out_ref):
    out_ref[0, 0] = mm(select_ref[...], back_ref[...].reshape(2 * NDP, 2048)).astype(BF16)


VMEM = pl.BlockSpec(memory_space=pltpu.VMEM)


def kernel_call(body, name, in_specs, outs, scratch=(), flops=0, bytes_accessed=1 << 20, limit=VMEM_LIMIT):
    outs = [jax.ShapeDtypeStruct(shape, dtype) for shape, dtype in outs]
    return pl.pallas_call(
        body,
        name=name,
        in_specs=in_specs,
        out_specs=[VMEM] * len(outs) if len(outs) > 1 else VMEM,
        out_shape=outs if len(outs) > 1 else outs[0],
        scratch_shapes=list(scratch),
        compiler_params=pltpu.CompilerParams(vmem_limit_bytes=limit),
        cost_estimate=pl.CostEstimate(flops=flops, bytes_accessed=bytes_accessed, transcendentals=0),
    )


def per_device(
    pixels,
    counts,
    clip_lengths,
    in_weight,
    in_bias,
    norm1_gain,
    norm1_bias,
    conv1_weight,
    norm2_gain,
    norm2_bias,
    conv2_weight,
    down_weight,
):
    row = lambda v: v.reshape(1, CH)
    packed = kernel_call(pack_kernel, "pack", [VMEM] * 2, [((NDP, 4, 128), BF16)])(counts[0].astype(BF16), pixels)
    arrived = lax.all_to_all(packed, "dp", split_axis=0, concat_axis=0, tiled=True)
    matrix, vectors, lengths = kernel_call(
        spread_kernel,
        "spread",
        [VMEM] * 7,
        [((384, 8 * CH), BF16), ((8, CH), F32), ((1, CLIPS), jnp.int32)],
        [pltpu.VMEM((27, 8, CH), F32)],
        flops=1 << 28,
    )(in_weight, clip_lengths, row(in_bias), row(norm1_gain), row(norm1_bias), row(norm2_gain), row(norm2_bias))
    onward = [(source, source + 1) for source in range(NTM - 1)]
    before = lax.ppermute(arrived, "tm", onward)
    frames = lambda n: ((n, 8, 4, 16, CH), BF16)
    late, own, part, place, select = kernel_call(
        late_kernel,
        "late",
        [VMEM] * 5,
        [frames(2), ((4, 64, 128), BF16), ((8, CH), F32), ((64, NDP), BF16), ((NDP, 64), BF16)],
        [pltpu.VMEM((128, 384), BF16)],
    )(lengths, arrived, matrix, vectors, counts)
    early, stats = kernel_call(
        early_kernel,
        "early",
        [VMEM] * 6,
        [frames(4), ((NTM, 2, 128), F32)],
        [pltpu.VMEM((8, 64, 128), BF16), pltpu.VMEM((256, 384), BF16)],
    )(lengths, before, own, part, matrix, vectors)
    stats = lax.all_to_all(stats, "tm", split_axis=0, concat_axis=0, tiled=True)
    act = [pltpu.VMEM((4, 10, 6, 16, CH), BF16)] * 2
    norm = pltpu.VMEM((8, CH), F32)
    middle, tail, stats = kernel_call(
        conv1_kernel,
        "conv1",
        [VMEM] * 6,
        [frames(4), frames(2), ((NTM, 2, 128), F32)],
        act + [norm],
        flops=1 << 31,
    )(lengths, early, late, stats, vectors, conv1_weight)
    stats = lax.all_to_all(stats, "tm", split_axis=0, concat_axis=0, tiled=True)
    place = kernel_call(beside_kernel, "beside", [VMEM] * 2, [((64, NDP), BF16)], flops=1 << 36)(place, tail)
    lead = lax.ppermute(tail, "tm", onward)
    packed = kernel_call(
        conv2_kernel,
        "conv2",
        [VMEM] * 10,
        [((NDP, 2, 2048), BF16)],
        act + [norm] + [pltpu.VMEM((2, 9, 5, 16, CH), BF16)] * 2 + [pltpu.VMEM((4, 32, 512), F32)],
        flops=1 << 31,
    )(lengths, place, early, late, middle, lead, stats, vectors, conv2_weight, down_weight)
    returned = lax.all_to_all(packed, "dp", split_axis=0, concat_axis=0, tiled=True)
    return kernel_call(return_kernel, "place", [VMEM] * 2, [((1, 1, 32, 2048), BF16)])(select, returned)


def solution(mesh):
    in_specs = (
        P("dp", "tm", None, None),
        P("tm", None, None),
        P("dp", None),
        P(),
        P(),
        P(),
        P(),
        P(),
        P(),
        P(),
        P(),
        P(),
    )
    out_specs = P("dp", "tm", None, None)
    return jax.shard_map(
        per_device, mesh=mesh, in_specs=in_specs, out_specs=out_specs, check_vma=False
    )
```

```python
import jax
import jax.numpy as jnp
from jax import lax
from jax.experimental import pallas as pl
from jax.experimental.pallas import tpu as pltpu
from jax.sharding import PartitionSpec as P


F32 = jnp.float32
BF16 = jnp.bfloat16
EPS = 1e-06
NDP = 32
NTM = 16
FT = 4
CLIPS = 4
CH = 128
AREA = 512
FRAME_N = AREA * 4
VMEM_LIMIT = 24 * 1024 * 1024


def iota(shape, dim):
    return lax.broadcasted_iota(jnp.int32, shape, dim)


def onehot(cond):
    return jnp.where(cond, 1.0, 0.0).astype(BF16)


def mm(a, b):
    return jnp.dot(a, b, preferred_element_type=F32)


def pick_lane(values, lane):
    return jnp.sum(jnp.where(iota(values.shape, 1) == lane, values, 0.0), axis=1, keepdims=True)


def pack_kernel(counts_ref, pixels_ref, out_ref):
    station = lax.axis_index("dp")
    table = counts_ref[...].astype(F32)
    pixels = pixels_ref[0, 0]
    sub, lane = iota((NDP, NDP), 0), iota((NDP, NDP), 1)
    row = jnp.sum(jnp.where(sub == station, table, 0.0), axis=0, keepdims=True)
    recv = jnp.sum(jnp.where(sub < station, table, 0.0), axis=0, keepdims=True)
    row8 = jnp.broadcast_to(row, (8, NDP))
    start = mm(row8.astype(BF16), onehot(sub < lane))[0:1]
    spread = (iota((128, NDP), 0) >> 2 == iota((128, NDP), 1)).astype(F32)
    count_i = jnp.sum(spread * row, axis=1, keepdims=True)
    start_i = jnp.sum(spread * start, axis=1, keepdims=True)
    recv_i = jnp.sum(spread * recv, axis=1, keepdims=True)
    i, m = iota((128, 64), 0), iota((128, 64), 1)
    slot = ((i >> 1) & 1).astype(F32)
    place = onehot(((m & 31).astype(F32) == start_i + slot) & (m >> 5 == (i & 1)) & (slot < count_i))
    src, dst = iota((192, 128), 0), iota((192, 128), 1)
    t = dst & 31
    wanted = 24 * ((dst >> 5) & 1) - 3 + t
    inside = (t < 30) & (wanted >= 0) & (wanted < 48)
    wanted = wanted + 48 * (dst >> 6)
    rows = [mm(pixels, onehot((src == 96 * qp + wanted) & inside)).astype(BF16) for qp in range(2)]
    packed = mm(place, jnp.concatenate(rows, axis=0))
    slot = ((iota((128, 128), 0) >> 1) & 1).astype(F32)
    packed = jnp.where(iota((128, 128), 1) == 30, jnp.where(slot < count_i, recv_i + slot, 255.0), packed)
    out_ref[...] = packed.reshape(NDP, 4, 128).astype(BF16)


def spread_kernel(weight_ref, lengths_ref, *refs):
    vector_refs, (out_ref, vectors_ref, along_ref, bounds_ref, taps_ref) = refs[:5], refs[5:]
    along_ref[...] = lengths_ref[...]
    lengths = [jnp.sum(lengths_ref[0:1, c : c + 1]) for c in range(CLIPS)]
    for c in range(CLIPS):
        bounds_ref[c : c + 1, :] = jnp.broadcast_to(sum(lengths[: c + 1]), (1, 128)).astype(F32)
        size = (lengths[c] * FRAME_N).astype(F32)
        bounds_ref[c + CLIPS : c + CLIPS + 1, :] = 1.0 / jnp.broadcast_to(size, (1, 128))
    for n, ref in enumerate(vector_refs):
        vectors_ref[n : n + 1, :] = ref[...]
    taps_ref[...] = jnp.zeros_like(taps_ref)
    for a in range(3):
        for b in range(3):
            for c in range(3):
                taps_ref[(a * 3 + b) * 3 + c, 0:3, :] = weight_ref[a, b, c].astype(F32)
    taps = taps_ref[...].reshape(27 * 8, CH).astype(BF16)
    r, j = iota((384, 1), 0), iota((1, 216), 1)
    dyi = (r >> 5) & 3
    row_key = jnp.where(dyi < 3, ((2 - (r >> 7)) * 3 + dyi) * 64 + (r & 31), -1000)
    tap, color = j >> 3, j & 7
    third = (tap * 43) >> 7
    col_key = jnp.where(color < 3, third * 64 + (tap - 3 * third) * 3 + color, -5000)
    diff = row_key - col_key
    for l in range(8):
        out_ref[:, l * CH : (l + 1) * CH] = mm(onehot(diff == 3 * l), taps).astype(BF16)


def clip_ends(lengths_ref):
    return [jnp.sum(lengths_ref[0:1, 0 : c + 1]) for c in range(CLIPS)]


def clip_of(ends, frame):
    ident = jnp.int32(0)
    begin = jnp.int32(0)
    for c in range(CLIPS - 1):
        past = frame >= ends[c]
        ident = jnp.where(past, jnp.int32(c + 1), ident)
        begin = jnp.where(past, ends[c], begin)
    return ident, begin


def group_sum(x):
    lane = iota(x.shape, 1)
    for n in (1, 2):
        x = x + jnp.where(lane & n == 0, pltpu.roll(x, 128 - n, 1), pltpu.roll(x, n, 1))
    return x


def shift_k(tile, step):
    moved = pltpu.roll(tile, step % 8, 0)
    return jnp.where(iota(tile.shape, 0) == (0 if step == 1 else 7), 0.0, moved)


class Moments:
    def __init__(self):
        self.pivot = None

    def add(self, rows):
        if self.pivot is None:
            self.pivot = rows[0:1]
            self.first = self.second = jnp.zeros((8, CH), F32)
        off = rows - self.pivot
        square = off * off
        self.first = self.first + fold(off)
        self.second = self.second + fold(square)

    def done(self):
        first = jnp.sum(self.first, axis=0, keepdims=True)
        second = jnp.sum(self.second, axis=0, keepdims=True)
        return first + AREA * self.pivot, second - first * first * (1.0 / AREA)


def fold(rows):
    return tree([rows[n : n + 8] for n in range(0, rows.shape[0], 8)])


def exact_mm(rows, matrix):
    high = rows.astype(BF16).astype(F32)
    middle = (rows - high).astype(BF16).astype(F32)
    low = rows - high - middle
    parts = mm(jnp.concatenate([high, middle, low, low], axis=0).astype(BF16), matrix)
    return parts[0:8] + parts[8:16] + parts[16:24]


def put_stats(pairs, stat_ref):
    sums = jnp.concatenate([p[0] for p in pairs], axis=0)
    devs = jnp.concatenate([p[1] for p in pairs], axis=0)
    off = sums * (1.0 / AREA) - group_sum(sums) * (1.0 / FRAME_N)
    rows = jnp.concatenate([sums, devs + AREA * (off * off)], axis=0)
    narrow = exact_mm(rows, onehot(iota((CH, 128), 0) >> 2 == (iota((CH, 128), 1) & 31)))
    own = jnp.where(iota((8, 128), 0) & 3 == iota((8, 128), 1) >> 5, narrow, 0.0)
    stats = jnp.concatenate([jnp.sum(own[n : n + 4], axis=0, keepdims=True) for n in (0, 4)], axis=0)
    for j in range(NTM):
        stat_ref[j] = stats


def unpack_rows(arrived):
    lane30 = onehot(iota((8, 128), 1) == 30)
    pos = lax.dot_general(lane30, arrived, (((1,), (1,)), ((), ())), preferred_element_type=F32)[0:1]
    pos = pos.astype(jnp.int32)
    qp = iota((1, 128), 1) & 1
    target = jnp.where(pos < 32, (pos >> 3) * 16 + qp * 8 + (pos & 7), -1)
    return mm(onehot(iota((64, 128), 0) == target), arrived)


def frame_rows(arrived, x_ref, first):
    rows = unpack_rows(arrived.reshape(128, 128))
    lane = iota((8, 128), 1)
    move = lambda tile, n: pltpu.roll(tile, n % 128, 1) if n % 128 else tile
    for f in range(FT):
        tiles = [(rows[f * 16 + (q >> 1) * 8 :][:8], 64 * (q & 1)) for q in range(4)]
        above = [(shift_k(tiles[3][0], 1), tiles[3][1])] + tiles[:3]
        below = tiles[1:] + [(shift_k(tiles[0][0], -1), tiles[0][1])]
        out = []
        for q in range(4):
            for h in range(2):
                a, b, c = (
                    move(tile, to - at - 32 * h)
                    for (tile, at), to in ((above[q], 0), (tiles[q], 32), (below[q], 64))
                )
                out.append(jnp.where(lane < 32, a, jnp.where(lane < 64, b, c)))
        x_ref[first + f] = jnp.concatenate(out, axis=0).astype(BF16)


def base_frames(lengths_ref, x_ref, x_first, lhs_ref, matrix_ref, vectors_ref, base_ref, first):
    column = lax.axis_index("tm")
    ends = clip_ends(lengths_ref)
    count = base_ref.shape[0]
    for n in range(count):
        frame = column * FT - 2 + first + n
        unused, begin = clip_of(ends, frame)
        for lag in range(3):
            p = jnp.clip(jnp.maximum(frame - lag, begin) - (column * FT + x_first), 0, x_ref.shape[0] - 1)
            lhs_ref[n * 64 : (n + 1) * 64, lag * 128 : (lag + 1) * 128] = x_ref[p]
    bias = vectors_ref[0:1, :]
    moments = [Moments() for unused in range(count)]
    for pair in range(4):
        both = mm(lhs_ref[...], matrix_ref[:, pair * 256 : (pair + 1) * 256])
        for half in range(2):
            value = (both[:, half * CH : (half + 1) * CH] + bias).astype(BF16)
            for n in range(count):
                part = value[n * 64 : (n + 1) * 64]
                base_ref[n, pair * 2 + half] = part.reshape(4, 16, CH)
                if first + n >= 2:
                    moments[n].add(part.astype(F32))
    return [m.done() for m in moments if m.pivot is not None]


def return_routes(counts_ref, place_ref, select_ref):
    station = lax.axis_index("dp")
    table = counts_ref[0].astype(F32)
    narrow = table.astype(BF16)
    loader, other = iota((64, NDP), 0) >> 1, iota((64, NDP), 1)
    count_i = pick_lane(mm(onehot(loader == other), narrow), station)
    start_i = pick_lane(mm(onehot(other < loader), narrow), station)
    slot = (iota((64, NDP), 0) & 1).astype(F32)
    place_ref[...] = onehot((other.astype(F32) == start_i + slot) & (slot < count_i))
    row = jnp.sum(jnp.where(iota((NDP, NDP), 0) == station, table, 0.0), axis=0, keepdims=True)
    row8 = jnp.broadcast_to(row, (8, NDP)).astype(BF16)
    encoder, other = iota((NDP, 64), 1) >> 1, iota((NDP, 64), 0)
    count_i = mm(row8, onehot(encoder == other))[0:1]
    start_i = mm(row8, onehot(other < encoder))[0:1]
    slot = (iota((NDP, 64), 1) & 1).astype(F32)
    select_ref[...] = onehot((other.astype(F32) == start_i + slot) & (slot < count_i))


def late_kernel(
    lengths_ref, own_ref, matrix_ref, vectors_ref, counts_ref, base_ref, x_ref, part_ref, place_ref, select_ref, lhs_ref
):
    return_routes(counts_ref, place_ref, select_ref)
    frame_rows(own_ref[...], x_ref, 0)
    pairs = base_frames(lengths_ref, x_ref, 0, lhs_ref, matrix_ref, vectors_ref, base_ref, 4)
    part_ref[...] = jnp.concatenate([p[0] for p in pairs] * 2 + [p[1] for p in pairs] * 2, axis=0)


def early_kernel(
    lengths_ref, prev_ref, own_ref, part_ref, matrix_ref, vectors_ref, base_ref, stat_ref, x_ref, lhs_ref
):
    frame_rows(prev_ref[...], x_ref, 0)
    x_ref[FT:] = own_ref[...]
    pairs = base_frames(lengths_ref, x_ref, -FT, lhs_ref, matrix_ref, vectors_ref, base_ref, 0)
    pairs = pairs + [(part_ref[n : n + 1, :], part_ref[n + 4 : n + 5, :]) for n in range(2)]
    put_stats(pairs, stat_ref)


def clip_scales(stats_ref, bounds_ref, gain, norm_ref):
    sums, devs = stats_ref[:, 0, :], stats_ref[:, 1, :]
    frame = (iota((NTM, 128), 0) * FT + (iota((NTM, 128), 1) >> 5)).astype(F32)
    ends = [bounds_ref[c : c + 1, :] for c in range(CLIPS)]
    inside = [frame < ends[0]] + [(frame >= ends[c - 1]) & (frame < ends[c]) for c in range(1, CLIPS)]

    def clip_rows(values):
        rows = [
            jnp.sum(jnp.where(inside[c], values[c], 0.0), axis=0, keepdims=True) for c in range(CLIPS)
        ]
        return jnp.concatenate(rows, axis=0) * bounds_ref[CLIPS:, :]

    parts = clip_rows([sums] * CLIPS)
    means = parts + pltpu.roll(parts, 32, 1)
    means = means + pltpu.roll(means, 64, 1)
    offs = [sums * (1.0 / FRAME_N) - means[c : c + 1] for c in range(CLIPS)]
    rows = jnp.concatenate([parts, clip_rows([devs + FRAME_N * (off * off) for off in offs])], axis=0)
    wide = exact_mm(rows, onehot(iota((128, CH), 0) & 31 == iota((128, CH), 1) >> 2))
    norm_ref[...] = jnp.where(iota((8, CH), 0) < CLIPS, wide, lax.rsqrt(wide + EPS) * (0.5 * gain))


def clip_norm(norm_ref, ident):
    return norm_ref[pl.ds(ident, 1), :], norm_ref[pl.ds(ident + CLIPS, 1), :]


def tree(parts):
    while len(parts) > 1:
        parts = [a + b for a, b in zip(parts[0::2], parts[1::2])]
    return parts[0]


def store_padded(places, l, tiles):
    column = []
    for h in range(2):
        own = [tiles[q][h] for q in range(4)]
        column.append([shift_k(own[3], 1)] + own + [shift_k(own[0], -1)])
    flat = [column[h][q] for q in range(6) for h in range(2)]
    padded = jnp.concatenate(flat, axis=0).astype(BF16).reshape(6, 16, CH)
    for act_ref, o in places:
        act_ref[o, l] = padded


def norm_frame(value_of, places, mean, scale, bias):
    zero = jnp.zeros((8, CH), F32)
    for l in range(8):
        v = (value_of(l).astype(F32).reshape(64, CH) - mean) * scale + bias
        v = v + v * jnp.tanh(v)
        tiles = [[v[q * 16 + h * 8 : q * 16 + h * 8 + 8] for h in range(2)] for q in range(4)]
        store_padded(places, l + 1, tiles)
        if l == 0:
            store_padded(places, 9, [[tiles[q][1], zero] for q in range(4)])
        if l == 7:
            store_padded(places, 0, [[zero, tiles[q][0]] for q in range(4)])


class Norm:
    def __init__(self, norm_ref, ends, column, bias):
        self.norm_ref, self.ends, self.column, self.bias = norm_ref, ends, column, 0.5 * bias

    def frame(self, ref, n, o, places):
        ident, unused = clip_of(self.ends, self.column * FT - 2 + o)
        mean, scale = clip_norm(self.norm_ref, ident)
        norm_frame(lambda l: ref[n, l], places, mean, scale, self.bias)

    def loop(self, ref, n, o, count, places):
        def step(i, carry):
            self.frame(ref, n + i, o + i, [(act_ref, first + i) for act_ref, first in places])
            return carry

        lax.fori_loop(0, count, step, 0, unroll=True)


def conv_frames(act_ref, weight_ref, picks):
    taps = [(z, r) for z in range(3) for r in range(3)]

    def rows(first):
        blocks = []
        for pick in picks:
            parts = [
                act_ref[pick[2 - z], first : first + 9 - first // 2, r : r + 4].reshape(-1, CH) for z, r in taps
            ]
            blocks.append(jnp.concatenate(parts, axis=1))
        return jnp.concatenate(blocks, axis=0)

    left, here, right = (jnp.concatenate([weight_ref[z, r, c] for z, r in taps], axis=0) for c in range(3))
    both = mm(rows(0), jnp.concatenate([left, here], axis=1))
    last = mm(rows(2), right)
    totals = []
    for n in range(len(picks)):
        at = n * 576
        totals.append(
            both[at : at + AREA, :CH] + both[at + 64 : at + 576, CH:] + last[n * AREA : (n + 1) * AREA]
        )
    return totals


def frame_picks(ends, column, o, first):
    frame = column * FT - 2 + o
    unused, begin = clip_of(ends, frame)
    return [
        jnp.clip(jnp.maximum(frame - lag, begin) - (column * FT - 2 + first), 0, o - first) for lag in range(3)
    ]


def conv_halves(norm, sources, low_ref, high_ref, weight_ref):
    (a, an), (b, bn), (c, cn) = sources
    norm.loop(a, an, 0, 2, [(low_ref, 0)])
    norm.loop(b, bn, 2, 2, [(low_ref, 2), (high_ref, 0)])
    picks = lambda o, first: frame_picks(norm.ends, norm.column, o, first)
    totals = conv_frames(low_ref, weight_ref, [picks(2, 0), picks(3, 0)])
    norm.frame(c, cn, 4, [(high_ref, 2)])
    norm.frame(c, cn + 1, 5, [(high_ref, 3)])
    yield 0, totals
    yield 2, conv_frames(high_ref, weight_ref, [picks(4, 2), picks(5, 2)])


def conv1_kernel(
    lengths_ref, early_ref, late_ref, stats_ref, bounds_ref, vectors_ref, weight_ref,
    middle_ref, tail_ref, stat_ref, low_ref, high_ref, norm_ref,
):
    column = lax.axis_index("tm")
    ends = clip_ends(lengths_ref)
    clip_scales(stats_ref, bounds_ref, vectors_ref[1:2, :], norm_ref)
    norm = Norm(norm_ref, ends, column, vectors_ref[2:3, :])
    pairs = []
    for first, totals in conv_halves(
        norm, [(early_ref, 0), (early_ref, 2), (late_ref, 0)], low_ref, high_ref, weight_ref
    ):
        for f, total in enumerate(totals, first):
            value = total.astype(BF16)
            half_ref = tail_ref if first else middle_ref
            half_ref[f & 1] = value.reshape(8, 4, 16, CH)
            moments = Moments()
            moments.add(value.astype(F32))
            pairs.append(moments.done())
    put_stats(pairs, stat_ref)


def beside_kernel(place_ref, tail_ref, out_ref):
    out_ref[...] = place_ref[...]


def conv2_kernel(
    lengths_ref, place_ref, early_ref, late_ref, middle_ref, tail_ref, lead_ref, stats_ref, bounds_ref, vectors_ref, weight_ref, down_ref,
    out_ref, low_ref, high_ref, norm_ref, resid_ref, later_ref, latent_ref,
):
    column = lax.axis_index("tm")
    ends = clip_ends(lengths_ref)
    clip_scales(stats_ref, bounds_ref, vectors_ref[3:4, :], norm_ref)
    norm = Norm(norm_ref, ends, column, vectors_ref[4:5, :])
    down = down_ref[...].reshape(9 * CH, CH)
    zero = jnp.zeros((8, CH), F32)

    def put(ref, f, l, tiles):
        flat = [tiles[q][h] for q in range(4) for h in range(2)]
        flat = flat + [shift_k(tiles[0][h], -1) for h in range(2)]
        ref[f, l] = jnp.concatenate(flat, axis=0).astype(BF16).reshape(5, 16, CH)

    for first, totals in conv_halves(
        norm, [(lead_ref, 0), (middle_ref, 0), (tail_ref, 0)], low_ref, high_ref, weight_ref
    ):
        half_ref, base_ref = (later_ref, late_ref) if first else (resid_ref, early_ref)
        for f, total in enumerate(totals):
            base = base_ref[f if first else f + 2]
            resid = base.astype(F32).reshape(AREA, CH) + total
            resid = resid.astype(BF16).astype(F32)
            for l in range(8):
                v = resid[l * 64 : (l + 1) * 64]
                tiles = [[v[q * 16 + h * 8 : q * 16 + h * 8 + 8] for h in range(2)] for q in range(4)]
                put(half_ref, f, l, tiles)
                if l == 0:
                    put(half_ref, f, 8, [[tiles[q][1], zero] for q in range(4)])
    taps = []
    for row in range(3):
        for col in range(3):
            parts = [
                half_ref[f, 2 * j + col, 2 * par + row]
                for half_ref in (resid_ref, later_ref)
                for f in range(2)
                for j in range(4)
                for par in range(2)
            ]
            taps.append(jnp.concatenate(parts, axis=0))
    latent = mm(jnp.concatenate(taps, axis=1), down)
    for f in range(FT):
        for j in range(4):
            for w in range(4):
                at = f * 128 + j * 32 + w * 8
                latent_ref[w, f * 8 : f * 8 + 8, j * CH : (j + 1) * CH] = latent[at : at + 8]
    for w in range(4):
        rows = mm(place_ref[...], latent_ref[w].astype(BF16))
        out_ref[:, :, w * 512 : (w + 1) * 512] = rows.reshape(NDP, 2, 512).astype(BF16)


def return_kernel(select_ref, back_ref, out_ref):
    out_ref[0, 0] = mm(select_ref[...], back_ref[...].reshape(2 * NDP, 2048)).astype(BF16)


VMEM = pl.BlockSpec(memory_space=pltpu.VMEM)


def kernel_call(body, name, in_specs, outs, scratch=(), flops=0, bytes_accessed=1 << 20, limit=VMEM_LIMIT):
    outs = [jax.ShapeDtypeStruct(shape, dtype) for shape, dtype in outs]
    return pl.pallas_call(
        body,
        name=name,
        in_specs=in_specs,
        out_specs=[VMEM] * len(outs) if len(outs) > 1 else VMEM,
        out_shape=outs if len(outs) > 1 else outs[0],
        scratch_shapes=list(scratch),
        compiler_params=pltpu.CompilerParams(vmem_limit_bytes=limit),
        cost_estimate=pl.CostEstimate(flops=flops, bytes_accessed=bytes_accessed, transcendentals=0),
    )


def per_device(
    pixels,
    counts,
    clip_lengths,
    in_weight,
    in_bias,
    norm1_gain,
    norm1_bias,
    conv1_weight,
    norm2_gain,
    norm2_bias,
    conv2_weight,
    down_weight,
):
    row = lambda v: v.reshape(1, CH)
    packed = kernel_call(pack_kernel, "pack", [VMEM] * 2, [((NDP, 4, 128), BF16)])(counts[0].astype(BF16), pixels)
    arrived = lax.all_to_all(packed, "dp", split_axis=0, concat_axis=0, tiled=True)
    matrix, vectors, lengths, bounds = kernel_call(
        spread_kernel,
        "spread",
        [VMEM] * 7,
        [((384, 8 * CH), BF16), ((8, CH), F32), ((1, CLIPS), jnp.int32), ((8, 128), F32)],
        [pltpu.VMEM((27, 8, CH), F32)],
        flops=1 << 28,
    )(in_weight, clip_lengths, row(in_bias), row(norm1_gain), row(norm1_bias), row(norm2_gain), row(norm2_bias))
    onward = [(source, source + 1) for source in range(NTM - 1)]
    before = lax.ppermute(arrived, "tm", onward)
    frames = lambda n: ((n, 8, 4, 16, CH), BF16)
    late, own, part, place, select = kernel_call(
        late_kernel,
        "late",
        [VMEM] * 5,
        [frames(2), ((4, 64, 128), BF16), ((8, CH), F32), ((64, NDP), BF16), ((NDP, 64), BF16)],
        [pltpu.VMEM((128, 384), BF16)],
    )(lengths, arrived, matrix, vectors, counts)
    early, stats = kernel_call(
        early_kernel,
        "early",
        [VMEM] * 6,
        [frames(4), ((NTM, 2, 128), F32)],
        [pltpu.VMEM((8, 64, 128), BF16), pltpu.VMEM((256, 384), BF16)],
    )(lengths, before, own, part, matrix, vectors)
    stats = lax.all_to_all(stats, "tm", split_axis=0, concat_axis=0, tiled=True)
    act = [pltpu.VMEM((4, 10, 6, 16, CH), BF16)] * 2
    norm = pltpu.VMEM((8, CH), F32)
    middle, tail, stats = kernel_call(
        conv1_kernel,
        "conv1",
        [VMEM] * 7,
        [frames(2), frames(2), ((NTM, 2, 128), F32)],
        act + [norm],
        flops=1 << 31,
    )(lengths, early, late, stats, bounds, vectors, conv1_weight)
    stats = lax.all_to_all(stats, "tm", split_axis=0, concat_axis=0, tiled=True)
    place = kernel_call(beside_kernel, "beside", [VMEM] * 2, [((64, NDP), BF16)], flops=1 << 36)(place, tail)
    lead = lax.ppermute(tail, "tm", onward)
    packed = kernel_call(
        conv2_kernel,
        "conv2",
        [VMEM] * 12,
        [((NDP, 2, 2048), BF16)],
        act + [norm] + [pltpu.VMEM((2, 9, 5, 16, CH), BF16)] * 2 + [pltpu.VMEM((4, 32, 512), F32)],
        flops=1 << 31,
    )(lengths, place, early, late, middle, tail, lead, stats, bounds, vectors, conv2_weight, down_weight)
    returned = lax.all_to_all(packed, "dp", split_axis=0, concat_axis=0, tiled=True)
    return kernel_call(return_kernel, "place", [VMEM] * 2, [((1, 1, 32, 2048), BF16)])(select, returned)


def solution(mesh):
    in_specs = (
        P("dp", "tm", None, None),
        P("tm", None, None),
        P("dp", None),
        P(),
        P(),
        P(),
        P(),
        P(),
        P(),
        P(),
        P(),
        P(),
    )
    out_specs = P("dp", "tm", None, None)
    return jax.shard_map(
        per_device, mesh=mesh, in_specs=in_specs, out_specs=out_specs, check_vma=False
    )
```

```python
import jax
import jax.numpy as jnp
from jax import lax
from jax.experimental import pallas as pl
from jax.experimental.pallas import tpu as pltpu
from jax.sharding import PartitionSpec as P


F32 = jnp.float32
BF16 = jnp.bfloat16
EPS = 1e-06
NDP = 32
NTM = 16
FT = 4
CLIPS = 4
CH = 128
AREA = 512
FRAME_N = AREA * 4
VMEM_LIMIT = 24 * 1024 * 1024


def iota(shape, dim):
    return lax.broadcasted_iota(jnp.int32, shape, dim)


def onehot(cond):
    return jnp.where(cond, 1.0, 0.0).astype(BF16)


def mm(a, b):
    return jnp.dot(a, b, preferred_element_type=F32)


def pick_lane(values, lane):
    return jnp.sum(jnp.where(iota(values.shape, 1) == lane, values, 0.0), axis=1, keepdims=True)


def pack_kernel(counts_ref, pixels_ref, out_ref):
    station = lax.axis_index("dp")
    table = counts_ref[...].astype(F32)
    pixels = pixels_ref[0, 0]
    sub, lane = iota((NDP, NDP), 0), iota((NDP, NDP), 1)
    row = jnp.sum(jnp.where(sub == station, table, 0.0), axis=0, keepdims=True)
    recv = jnp.sum(jnp.where(sub < station, table, 0.0), axis=0, keepdims=True)
    row8 = jnp.broadcast_to(row, (8, NDP))
    start = mm(row8.astype(BF16), onehot(sub < lane))[0:1]
    spread = (iota((128, NDP), 0) >> 2 == iota((128, NDP), 1)).astype(F32)
    count_i = jnp.sum(spread * row, axis=1, keepdims=True)
    start_i = jnp.sum(spread * start, axis=1, keepdims=True)
    recv_i = jnp.sum(spread * recv, axis=1, keepdims=True)
    i, m = iota((128, 64), 0), iota((128, 64), 1)
    slot = ((i >> 1) & 1).astype(F32)
    place = onehot(((m & 31).astype(F32) == start_i + slot) & (m >> 5 == (i & 1)) & (slot < count_i))
    src, dst = iota((192, 128), 0), iota((192, 128), 1)
    t = dst & 31
    wanted = 24 * ((dst >> 5) & 1) - 3 + t
    inside = (t < 30) & (wanted >= 0) & (wanted < 48)
    wanted = wanted + 48 * (dst >> 6)
    rows = [mm(pixels, onehot((src == 96 * qp + wanted) & inside)).astype(BF16) for qp in range(2)]
    packed = mm(place, jnp.concatenate(rows, axis=0))
    slot = ((iota((128, 128), 0) >> 1) & 1).astype(F32)
    packed = jnp.where(iota((128, 128), 1) == 30, jnp.where(slot < count_i, recv_i + slot, 255.0), packed)
    out_ref[...] = packed.reshape(NDP, 4, 128).astype(BF16)


def spread_kernel(weight_ref, lengths_ref, *refs):
    vector_refs, (out_ref, vectors_ref, along_ref, bounds_ref, taps_ref) = refs[:5], refs[5:]
    along_ref[...] = lengths_ref[...]
    lengths = [jnp.sum(lengths_ref[0:1, c : c + 1]) for c in range(CLIPS)]
    for c in range(CLIPS):
        bounds_ref[c : c + 1, :] = jnp.broadcast_to(sum(lengths[: c + 1]), (1, 128)).astype(F32)
        size = (lengths[c] * FRAME_N).astype(F32)
        bounds_ref[c + CLIPS : c + CLIPS + 1, :] = 1.0 / jnp.broadcast_to(size, (1, 128))
    for n, ref in enumerate(vector_refs):
        vectors_ref[n : n + 1, :] = ref[...]
    taps_ref[...] = jnp.zeros_like(taps_ref)
    for a in range(3):
        for b in range(3):
            for c in range(3):
                taps_ref[(a * 3 + b) * 3 + c, 0:3, :] = weight_ref[a, b, c].astype(F32)
    taps = taps_ref[...].reshape(27 * 8, CH).astype(BF16)
    r, j = iota((384, 1), 0), iota((1, 216), 1)
    dyi = (r >> 5) & 3
    row_key = jnp.where(dyi < 3, ((2 - (r >> 7)) * 3 + dyi) * 64 + (r & 31), -1000)
    tap, color = j >> 3, j & 7
    third = (tap * 43) >> 7
    col_key = jnp.where(color < 3, third * 64 + (tap - 3 * third) * 3 + color, -5000)
    diff = row_key - col_key
    for l in range(8):
        out_ref[:, l * CH : (l + 1) * CH] = mm(onehot(diff == 3 * l), taps).astype(BF16)


def clip_ends(lengths_ref):
    return [jnp.sum(lengths_ref[0:1, 0 : c + 1]) for c in range(CLIPS)]


def clip_of(ends, frame):
    ident = jnp.int32(0)
    begin = jnp.int32(0)
    for c in range(CLIPS - 1):
        past = frame >= ends[c]
        ident = jnp.where(past, jnp.int32(c + 1), ident)
        begin = jnp.where(past, ends[c], begin)
    return ident, begin


def group_sum(x):
    lane = iota(x.shape, 1)
    for n in (1, 2):
        x = x + jnp.where(lane & n == 0, pltpu.roll(x, 128 - n, 1), pltpu.roll(x, n, 1))
    return x


def shift_k(tile, step):
    moved = pltpu.roll(tile, step % 8, 0)
    return jnp.where(iota(tile.shape, 0) == (0 if step == 1 else 7), 0.0, moved)


class Moments:
    def __init__(self):
        self.pivot = None

    def add(self, rows):
        if self.pivot is None:
            self.pivot = rows[0:1]
            self.first = self.second = jnp.zeros((8, CH), F32)
        off = rows - self.pivot
        square = off * off
        self.first = self.first + fold(off)
        self.second = self.second + fold(square)

    def done(self):
        first = jnp.sum(self.first, axis=0, keepdims=True)
        second = jnp.sum(self.second, axis=0, keepdims=True)
        return first + AREA * self.pivot, second - first * first * (1.0 / AREA)


def fold(rows):
    return tree([rows[n : n + 8] for n in range(0, rows.shape[0], 8)])


def exact_mm(rows, matrix):
    high = rows.astype(BF16).astype(F32)
    middle = (rows - high).astype(BF16).astype(F32)
    low = rows - high - middle
    parts = mm(jnp.concatenate([high, middle, low, low], axis=0).astype(BF16), matrix)
    return parts[0:8] + parts[8:16] + parts[16:24]


def put_stats(pairs, stat_ref):
    sums = jnp.concatenate([p[0] for p in pairs], axis=0)
    devs = jnp.concatenate([p[1] for p in pairs], axis=0)
    off = sums * (1.0 / AREA) - group_sum(sums) * (1.0 / FRAME_N)
    rows = jnp.concatenate([sums, devs + AREA * (off * off)], axis=0)
    narrow = exact_mm(rows, onehot(iota((CH, 128), 0) >> 2 == (iota((CH, 128), 1) & 31)))
    own = jnp.where(iota((8, 128), 0) & 3 == iota((8, 128), 1) >> 5, narrow, 0.0)
    stats = jnp.concatenate([jnp.sum(own[n : n + 4], axis=0, keepdims=True) for n in (0, 4)], axis=0)
    for j in range(NTM):
        stat_ref[j] = stats


def unpack_rows(arrived):
    lane30 = onehot(iota((8, 128), 1) == 30)
    pos = lax.dot_general(lane30, arrived, (((1,), (1,)), ((), ())), preferred_element_type=F32)[0:1]
    pos = pos.astype(jnp.int32)
    qp = iota((1, 128), 1) & 1
    target = jnp.where(pos < 32, (pos >> 3) * 16 + qp * 8 + (pos & 7), -1)
    return mm(onehot(iota((64, 128), 0) == target), arrived)


def frame_rows(arrived, x_ref, first):
    rows = unpack_rows(arrived.reshape(128, 128))
    lane = iota((8, 128), 1)
    move = lambda tile, n: pltpu.roll(tile, n % 128, 1) if n % 128 else tile
    for f in range(FT):
        tiles = [(rows[f * 16 + (q >> 1) * 8 :][:8], 64 * (q & 1)) for q in range(4)]
        above = [(shift_k(tiles[3][0], 1), tiles[3][1])] + tiles[:3]
        below = tiles[1:] + [(shift_k(tiles[0][0], -1), tiles[0][1])]
        out = []
        for q in range(4):
            for h in range(2):
                a, b, c = (
                    move(tile, to - at - 32 * h)
                    for (tile, at), to in ((above[q], 0), (tiles[q], 32), (below[q], 64))
                )
                out.append(jnp.where(lane < 32, a, jnp.where(lane < 64, b, c)))
        x_ref[first + f] = jnp.concatenate(out, axis=0).astype(BF16)


def base_frames(lengths_ref, x_ref, x_first, lhs_ref, matrix_ref, vectors_ref, base_ref, first):
    column = lax.axis_index("tm")
    ends = clip_ends(lengths_ref)
    count = base_ref.shape[0]
    for n in range(count):
        frame = column * FT - 2 + first + n
        unused, begin = clip_of(ends, frame)
        for lag in range(3):
            p = jnp.clip(jnp.maximum(frame - lag, begin) - (column * FT + x_first), 0, x_ref.shape[0] - 1)
            lhs_ref[n * 64 : (n + 1) * 64, lag * 128 : (lag + 1) * 128] = x_ref[p]
    bias = vectors_ref[0:1, :]
    moments = [Moments() for unused in range(count)]
    for pair in range(4):
        both = mm(lhs_ref[...], matrix_ref[:, pair * 256 : (pair + 1) * 256])
        for half in range(2):
            value = (both[:, half * CH : (half + 1) * CH] + bias).astype(BF16)
            for n in range(count):
                part = value[n * 64 : (n + 1) * 64]
                base_ref[n, pair * 2 + half] = part.reshape(4, 16, CH)
                if first + n >= 2:
                    moments[n].add(part.astype(F32))
    return [m.done() for m in moments if m.pivot is not None]


def return_routes(counts_ref, place_ref, select_ref):
    station = lax.axis_index("dp")
    table = counts_ref[0].astype(F32)
    narrow = table.astype(BF16)
    loader, other = iota((64, NDP), 0) >> 1, iota((64, NDP), 1)
    count_i = pick_lane(mm(onehot(loader == other), narrow), station)
    start_i = pick_lane(mm(onehot(other < loader), narrow), station)
    slot = (iota((64, NDP), 0) & 1).astype(F32)
    place_ref[...] = onehot((other.astype(F32) == start_i + slot) & (slot < count_i))
    row = jnp.sum(jnp.where(iota((NDP, NDP), 0) == station, table, 0.0), axis=0, keepdims=True)
    row8 = jnp.broadcast_to(row, (8, NDP)).astype(BF16)
    encoder, other = iota((NDP, 64), 1) >> 1, iota((NDP, 64), 0)
    count_i = mm(row8, onehot(encoder == other))[0:1]
    start_i = mm(row8, onehot(other < encoder))[0:1]
    slot = (iota((NDP, 64), 1) & 1).astype(F32)
    select_ref[...] = onehot((other.astype(F32) == start_i + slot) & (slot < count_i))


def late_kernel(
    lengths_ref, own_ref, matrix_ref, vectors_ref, counts_ref, base_ref, x_ref, part_ref, place_ref, select_ref, lhs_ref
):
    return_routes(counts_ref, place_ref, select_ref)
    frame_rows(own_ref[...], x_ref, 0)
    pairs = base_frames(lengths_ref, x_ref, 0, lhs_ref, matrix_ref, vectors_ref, base_ref, 4)
    part_ref[...] = jnp.concatenate([p[0] for p in pairs] * 2 + [p[1] for p in pairs] * 2, axis=0)


def early_kernel(
    lengths_ref, prev_ref, own_ref, part_ref, matrix_ref, vectors_ref, base_ref, stat_ref, x_ref, lhs_ref
):
    frame_rows(prev_ref[...], x_ref, 0)
    x_ref[FT:] = own_ref[...]
    pairs = base_frames(lengths_ref, x_ref, -FT, lhs_ref, matrix_ref, vectors_ref, base_ref, 0)
    pairs = pairs + [(part_ref[n : n + 1, :], part_ref[n + 4 : n + 5, :]) for n in range(2)]
    put_stats(pairs, stat_ref)


def clip_scales(stats_ref, bounds_ref, gain, norm_ref):
    sums, devs = stats_ref[:, 0, :], stats_ref[:, 1, :]
    frame = (iota((NTM, 128), 0) * FT + (iota((NTM, 128), 1) >> 5)).astype(F32)
    ends = [bounds_ref[c : c + 1, :] for c in range(CLIPS)]
    inside = [frame < ends[0]] + [(frame >= ends[c - 1]) & (frame < ends[c]) for c in range(1, CLIPS)]

    def clip_rows(values):
        rows = [
            jnp.sum(jnp.where(inside[c], values[c], 0.0), axis=0, keepdims=True) for c in range(CLIPS)
        ]
        return jnp.concatenate(rows, axis=0) * bounds_ref[CLIPS:, :]

    parts = clip_rows([sums] * CLIPS)
    means = parts + pltpu.roll(parts, 32, 1)
    means = means + pltpu.roll(means, 64, 1)
    offs = [sums * (1.0 / FRAME_N) - means[c : c + 1] for c in range(CLIPS)]
    rows = jnp.concatenate([parts, clip_rows([devs + FRAME_N * (off * off) for off in offs])], axis=0)
    wide = exact_mm(rows, onehot(iota((128, CH), 0) & 31 == iota((128, CH), 1) >> 2))
    norm_ref[...] = jnp.where(iota((8, CH), 0) < CLIPS, wide, lax.rsqrt(wide + EPS) * (0.5 * gain))


def clip_norm(norm_ref, ident):
    return norm_ref[pl.ds(ident, 1), :], norm_ref[pl.ds(ident + CLIPS, 1), :]


def tree(parts):
    while len(parts) > 1:
        parts = [a + b for a, b in zip(parts[0::2], parts[1::2])]
    return parts[0]


def store_padded(places, l, tiles):
    column = []
    for h in range(2):
        own = [tiles[q][h] for q in range(4)]
        column.append([shift_k(own[3], 1)] + own + [shift_k(own[0], -1)])
    flat = [column[h][q] for q in range(6) for h in range(2)]
    padded = jnp.concatenate(flat, axis=0).astype(BF16).reshape(6, 16, CH)
    for act_ref, o in places:
        act_ref[o, l] = padded


def norm_frame(value_of, places, mean, scale, bias):
    zero = jnp.zeros((8, CH), F32)
    for l in range(8):
        v = (value_of(l).astype(F32).reshape(64, CH) - mean) * scale + bias
        v = v + v * jnp.tanh(v)
        tiles = [[v[q * 16 + h * 8 : q * 16 + h * 8 + 8] for h in range(2)] for q in range(4)]
        store_padded(places, l + 1, tiles)
        if l == 0:
            store_padded(places, 9, [[tiles[q][1], zero] for q in range(4)])
        if l == 7:
            store_padded(places, 0, [[zero, tiles[q][0]] for q in range(4)])


class Norm:
    def __init__(self, norm_ref, ends, column, bias):
        self.norm_ref, self.ends, self.column, self.bias = norm_ref, ends, column, 0.5 * bias

    def frame(self, ref, n, o, places):
        ident, unused = clip_of(self.ends, self.column * FT - 2 + o)
        mean, scale = clip_norm(self.norm_ref, ident)
        norm_frame(lambda l: ref[n, l], places, mean, scale, self.bias)

    def loop(self, ref, n, o, count, places):
        def step(i, carry):
            self.frame(ref, n + i, o + i, [(act_ref, first + i) for act_ref, first in places])
            return carry

        lax.fori_loop(0, count, step, 0, unroll=True)


def conv_frames(act_ref, weight_ref, picks):
    taps = [(z, r) for z in range(3) for r in range(3)]

    def rows(first):
        blocks = []
        for pick in picks:
            parts = [
                act_ref[pick[2 - z], first : first + 9 - first // 2, r : r + 4].reshape(-1, CH) for z, r in taps
            ]
            blocks.append(jnp.concatenate(parts, axis=1))
        return jnp.concatenate(blocks, axis=0)

    left, here, right = (jnp.concatenate([weight_ref[z, r, c] for z, r in taps], axis=0) for c in range(3))
    both = mm(rows(0), jnp.concatenate([left, here], axis=1))
    last = mm(rows(2), right)
    totals = []
    for n in range(len(picks)):
        at = n * 576
        totals.append(
            both[at : at + AREA, :CH] + both[at + 64 : at + 576, CH:] + last[n * AREA : (n + 1) * AREA]
        )
    return totals


def frame_picks(ends, column, o, first):
    frame = column * FT - 2 + o
    unused, begin = clip_of(ends, frame)
    return [
        jnp.clip(jnp.maximum(frame - lag, begin) - (column * FT - 2 + first), 0, o - first) for lag in range(3)
    ]


def conv_halves(norm, sources, low_ref, high_ref, weight_ref):
    (a, an), (b, bn), (c, cn) = sources
    norm.loop(a, an, 0, 2, [(low_ref, 0)])
    norm.loop(b, bn, 2, 2, [(low_ref, 2), (high_ref, 0)])
    picks = lambda o, first: frame_picks(norm.ends, norm.column, o, first)
    totals = conv_frames(low_ref, weight_ref, [picks(2, 0), picks(3, 0)])
    norm.frame(c, cn, 4, [(high_ref, 2)])
    norm.frame(c, cn + 1, 5, [(high_ref, 3)])
    yield 0, totals
    yield 2, conv_frames(high_ref, weight_ref, [picks(4, 2), picks(5, 2)])


def conv1_kernel(
    lengths_ref, early_ref, late_ref, stats_ref, bounds_ref, vectors_ref, weight_ref,
    middle_ref, tail_ref, stat_ref, low_ref, high_ref, norm_ref,
):
    column = lax.axis_index("tm")
    ends = clip_ends(lengths_ref)
    clip_scales(stats_ref, bounds_ref, vectors_ref[1:2, :], norm_ref)
    norm = Norm(norm_ref, ends, column, vectors_ref[2:3, :])
    pairs = []
    for first, totals in conv_halves(
        norm, [(early_ref, 0), (early_ref, 2), (late_ref, 0)], low_ref, high_ref, weight_ref
    ):
        for f, total in enumerate(totals, first):
            value = total.astype(BF16)
            half_ref = tail_ref if first else middle_ref
            half_ref[f & 1] = value.reshape(8, 4, 16, CH)
            moments = Moments()
            moments.add(value.astype(F32))
            pairs.append(moments.done())
    put_stats(pairs, stat_ref)


def beside_kernel(place_ref, tail_ref, out_ref):
    out_ref[...] = place_ref[...]


def conv2_kernel(
    lengths_ref, place_ref, early_ref, late_ref, middle_ref, tail_ref, lead_ref, stats_ref, bounds_ref, vectors_ref, weight_ref, down_ref,
    out_ref, low_ref, high_ref, norm_ref, resid_ref, later_ref,
):
    column = lax.axis_index("tm")
    ends = clip_ends(lengths_ref)
    clip_scales(stats_ref, bounds_ref, vectors_ref[3:4, :], norm_ref)
    norm = Norm(norm_ref, ends, column, vectors_ref[4:5, :])
    down = down_ref[...].reshape(9 * CH, CH)
    zero = jnp.zeros((8, CH), F32)

    def put(ref, f, l, tiles):
        flat = [tiles[q][h] for q in range(4) for h in range(2)]
        flat = flat + [shift_k(tiles[0][h], -1) for h in range(2)]
        ref[f, l] = jnp.concatenate(flat, axis=0).astype(BF16).reshape(5, 16, CH)

    for first, totals in conv_halves(
        norm, [(lead_ref, 0), (middle_ref, 0), (tail_ref, 0)], low_ref, high_ref, weight_ref
    ):
        half_ref, base_ref = (later_ref, late_ref) if first else (resid_ref, early_ref)
        for f, total in enumerate(totals):
            base = base_ref[f if first else f + 2]
            resid = base.astype(F32).reshape(AREA, CH) + total
            resid = resid.astype(BF16).astype(F32)
            for l in range(8):
                v = resid[l * 64 : (l + 1) * 64]
                tiles = [[v[q * 16 + h * 8 : q * 16 + h * 8 + 8] for h in range(2)] for q in range(4)]
                put(half_ref, f, l, tiles)
                if l == 0:
                    put(half_ref, f, 8, [[tiles[q][1], zero] for q in range(4)])
    taps = []
    for row in range(3):
        for col in range(3):
            parts = [
                half_ref[f, 2 * j + col, 2 * par + row]
                for half_ref in (resid_ref, later_ref)
                for f in range(2)
                for j in range(4)
                for par in range(2)
            ]
            taps.append(jnp.concatenate(parts, axis=0))
    latent = mm(jnp.concatenate(taps, axis=1), down)
    piece = lambda f, j, w: latent[f * 128 + j * 32 + w * 8 :][:8]
    for w in range(4):
        units = [jnp.concatenate([piece(f, j, w) for f in range(FT)], axis=0) for j in range(4)]
        rows = mm(place_ref[...], jnp.concatenate(units, axis=1).astype(BF16))
        out_ref[:, :, w * 512 : (w + 1) * 512] = rows.reshape(NDP, 2, 512).astype(BF16)


def return_kernel(select_ref, back_ref, out_ref):
    out_ref[0, 0] = mm(select_ref[...], back_ref[...].reshape(2 * NDP, 2048)).astype(BF16)


VMEM = pl.BlockSpec(memory_space=pltpu.VMEM)


def kernel_call(body, name, in_specs, outs, scratch=(), flops=0, bytes_accessed=1 << 20, limit=VMEM_LIMIT):
    outs = [jax.ShapeDtypeStruct(shape, dtype) for shape, dtype in outs]
    return pl.pallas_call(
        body,
        name=name,
        in_specs=in_specs,
        out_specs=[VMEM] * len(outs) if len(outs) > 1 else VMEM,
        out_shape=outs if len(outs) > 1 else outs[0],
        scratch_shapes=list(scratch),
        compiler_params=pltpu.CompilerParams(vmem_limit_bytes=limit),
        cost_estimate=pl.CostEstimate(flops=flops, bytes_accessed=bytes_accessed, transcendentals=0),
    )


def per_device(
    pixels,
    counts,
    clip_lengths,
    in_weight,
    in_bias,
    norm1_gain,
    norm1_bias,
    conv1_weight,
    norm2_gain,
    norm2_bias,
    conv2_weight,
    down_weight,
):
    row = lambda v: v.reshape(1, CH)
    packed = kernel_call(pack_kernel, "pack", [VMEM] * 2, [((NDP, 4, 128), BF16)])(counts[0].astype(BF16), pixels)
    arrived = lax.all_to_all(packed, "dp", split_axis=0, concat_axis=0, tiled=True)
    matrix, vectors, lengths, bounds = kernel_call(
        spread_kernel,
        "spread",
        [VMEM] * 7,
        [((384, 8 * CH), BF16), ((8, CH), F32), ((1, CLIPS), jnp.int32), ((8, 128), F32)],
        [pltpu.VMEM((27, 8, CH), F32)],
        flops=1 << 28,
    )(in_weight, clip_lengths, row(in_bias), row(norm1_gain), row(norm1_bias), row(norm2_gain), row(norm2_bias))
    onward = [(source, source + 1) for source in range(NTM - 1)]
    before = lax.ppermute(arrived, "tm", onward)
    frames = lambda n: ((n, 8, 4, 16, CH), BF16)
    late, own, part, place, select = kernel_call(
        late_kernel,
        "late",
        [VMEM] * 5,
        [frames(2), ((4, 64, 128), BF16), ((8, CH), F32), ((64, NDP), BF16), ((NDP, 64), BF16)],
        [pltpu.VMEM((128, 384), BF16)],
    )(lengths, arrived, matrix, vectors, counts)
    early, stats = kernel_call(
        early_kernel,
        "early",
        [VMEM] * 6,
        [frames(4), ((NTM, 2, 128), F32)],
        [pltpu.VMEM((8, 64, 128), BF16), pltpu.VMEM((256, 384), BF16)],
    )(lengths, before, own, part, matrix, vectors)
    stats = lax.all_to_all(stats, "tm", split_axis=0, concat_axis=0, tiled=True)
    act = [pltpu.VMEM((4, 10, 6, 16, CH), BF16)] * 2
    norm = pltpu.VMEM((8, CH), F32)
    middle, tail, stats = kernel_call(
        conv1_kernel,
        "conv1",
        [VMEM] * 7,
        [frames(2), frames(2), ((NTM, 2, 128), F32)],
        act + [norm],
        flops=1 << 31,
    )(lengths, early, late, stats, bounds, vectors, conv1_weight)
    stats = lax.all_to_all(stats, "tm", split_axis=0, concat_axis=0, tiled=True)
    place = kernel_call(beside_kernel, "beside", [VMEM] * 2, [((64, NDP), BF16)], flops=1 << 36)(place, tail)
    lead = lax.ppermute(tail, "tm", onward)
    packed = kernel_call(
        conv2_kernel,
        "conv2",
        [VMEM] * 12,
        [((NDP, 2, 2048), BF16)],
        act + [norm] + [pltpu.VMEM((2, 9, 5, 16, CH), BF16)] * 2,
        flops=1 << 31,
    )(lengths, place, early, late, middle, tail, lead, stats, bounds, vectors, conv2_weight, down_weight)
    returned = lax.all_to_all(packed, "dp", split_axis=0, concat_axis=0, tiled=True)
    return kernel_call(return_kernel, "place", [VMEM] * 2, [((1, 1, 32, 2048), BF16)])(select, returned)


def solution(mesh):
    in_specs = (
        P("dp", "tm", None, None),
        P("tm", None, None),
        P("dp", None),
        P(),
        P(),
        P(),
        P(),
        P(),
        P(),
        P(),
        P(),
        P(),
    )
    out_specs = P("dp", "tm", None, None)
    return jax.shard_map(
        per_device, mesh=mesh, in_specs=in_specs, out_specs=out_specs, check_vma=False
    )
```
